32 devices in a mesh: lon: 8 (over y, x, core), rad: 4 (over z).
Axes of the slice: x: 2, y: 2, z: 4, core: 2. Of those that a mesh axis runs over, the one named last changes fastest.
Arguments:
- state: float32 [5, 32, 48, 1024], P(None, 'rad', None, 'lon'), may hold values from -6 to 6
- outer_rows: float32 [5, 32, 4, 1024], P(None, 'rad', None, 'lon'), may hold values from -6 to 6
- kappa: float32 [32], P('rad'), may hold values from 5e-05 to 0.0005
Outputs:
- increment: float32 [5, 32, 48, 1024], P(None, 'rad', None, 'lon')
The draws below stay inside these ranges and needn't reach their ends.
All inputs are finite; a program needn't handle non-finite values.
Results may differ from the reference program's by a relative error of at most 0.00002.
Values sent between devices are 32-bit elements; how exact they have to be, the bound alone decides.
No kernel may reach another device: no remote copies, remote signals or barrier semaphores. Data moves between devices by JAX's collectives and lax.ppermute only.
A program may use at most 128 MiB of HBM per device.

```python
import math
import jax
import jax.numpy as jnp
from jax import lax

LEV_DEV = 8
ROWS = 48
NLON = 1024
NLEV = 32
N_RAD = 4


def level_of(stream_key, shape, pieces, least, high):
    def one(axis_at, blocks):
        heights = jax.random.uniform(jax.random.fold_in(jax.random.fold_in(stream_key, 6), axis_at), (blocks,), jnp.float32, least / len(pieces), high / len(pieces))
        return jnp.repeat(jnp.exp(heights), shape[axis_at] // blocks).reshape((-1,) + (1,) * (len(shape) - axis_at - 1))

    gain = one(*pieces[0])
    for cut in pieces[1:]:
        gain = gain * one(*cut)
    return gain


def scatter_about(stream_key, extent, scale, bound, shards=(), kind=jnp.bfloat16):
    values = jax.random.normal(stream_key, extent, jnp.float32) * scale
    if len(shards) > 0:
        values = level_of(stream_key, extent, shards, -0.22, 0.18) * values
    return jnp.clip(values, min=-bound, max=bound).astype(kind)


def setup_inputs(seed: int = 0) -> dict:
    keys = jax.random.split(jax.random.key(seed), 4)
    return {
        "state": scatter_about(keys[0], (5, NLEV, ROWS, NLON), 1.0, 6.0, ((1, 4), (3, 8)), jnp.float32),
        "outer_rows": scatter_about(keys[1], (5, NLEV, 4, NLON), 1.0, 6.0, ((1, 4), (3, 8)), jnp.float32),
        "kappa": jnp.clip(jnp.exp(math.log(0.0005) - 2.3025852 * jax.random.uniform(keys[2], (NLEV,), jnp.float32) ** level_of(keys[2], (NLEV,), ((0, 4),), -0.2, 0.2)), 4.999999873689376e-05, 0.0005),
    }


first_coeffs = (0.8, -0.2, 4.0 / 105.0, -1.0 / 280.0)
second_coeffs = (-205.0 / 72.0, 1.6, -0.2, 8.0 / 315.0, -1.0 / 560.0)
time_step = 0.002
gamma_less_one = 0.4
radial_ratio = 3.0


def window(padded, offset, length, axis):
    return lax.slice_in_dim(padded, offset, offset + length, axis=axis)


def first_derivative(padded, length, axis):
    total = first_coeffs[0] * (window(padded, 5, length, axis) - window(padded, 3, length, axis))
    for reach in range(2, 5):
        total = total + first_coeffs[reach - 1] * (window(padded, 4 + reach, length, axis) - window(padded, 4 - reach, length, axis))
    return total


def second_derivative(padded, length, axis):
    total = second_coeffs[0] * window(padded, 4, length, axis)
    for reach in range(1, 5):
        total = total + second_coeffs[reach] * (window(padded, 4 + reach, length, axis) + window(padded, 4 - reach, length, axis))
    return total


def geometry(rows, nlon):
    index = jnp.arange(rows, dtype=jnp.float32)
    spacing = 2.0 * math.pi / nlon
    theta = (index + 0.5) * spacing
    metric = 1.0 / jnp.sin(theta)
    return metric[:, None], (jnp.cos(theta) * metric)[:, None]


def tendency(center, pad_lon, pad_row, pad_level, kappa_col, metric, curvature):
    levels, rows, width = center.shape[1], center.shape[2], center.shape[3]
    slope_lon = metric * first_derivative(pad_lon, width, 3)
    slope_row = first_derivative(pad_row, rows, 2)
    slope_level = radial_ratio * first_derivative(pad_level, levels, 1)
    wind_lon = center[1]
    wind_row = center[2]
    wind_level = center[3]
    temper = center[4]
    carried = wind_lon * slope_lon + wind_row * slope_row + wind_level * slope_level
    spread = slope_lon[1] + slope_row[2] + slope_level[3] + curvature * wind_row
    laplace = metric * metric * second_derivative(pad_lon[4], width, 2) + second_derivative(pad_row[4], rows, 1) + (radial_ratio * radial_ratio) * second_derivative(pad_level[4], levels, 0)
    return jnp.stack([
        -carried[0] - spread,
        -carried[1] - temper * slope_lon[0] - slope_lon[4],
        -carried[2] - temper * slope_row[0] - slope_row[4],
        -carried[3] - temper * slope_level[0] - slope_level[4],
        -carried[4] - gamma_less_one * temper * spread + kappa_col * laplace,
    ])


def section_tendency(fields, outer_rows, kappa, metric, curvature):
    flip_signs = jnp.array([1.0, -1.0, -1.0, 1.0, 1.0], dtype=jnp.float32).reshape(5, 1, 1, 1)
    pad_lon = jnp.concatenate([fields[..., -4:], fields, fields[..., :4]], axis=3)
    partner = jnp.roll(fields[:, :, :4, :], NLON // 2, axis=3)
    pad_row = jnp.concatenate([partner[:, :, ::-1, :] * flip_signs, fields, outer_rows], axis=2)
    pad_level = jnp.pad(fields, ((0, 0), (4, 4), (0, 0), (0, 0)))

    def block(start):
        center = lax.dynamic_slice_in_dim(fields, start, LEV_DEV, 1)
        piece_lon = lax.dynamic_slice_in_dim(pad_lon, start, LEV_DEV, 1)
        piece_row = lax.dynamic_slice_in_dim(pad_row, start, LEV_DEV, 1)
        piece_level = lax.dynamic_slice_in_dim(pad_level, start, LEV_DEV + 8, 1)
        kappa_col = lax.dynamic_slice_in_dim(kappa, start, LEV_DEV, 0).reshape(LEV_DEV, 1, 1)
        return tendency(center, piece_lon, piece_row, piece_level, kappa_col, metric, curvature)

    starts = jnp.arange(N_RAD, dtype=jnp.int32) * LEV_DEV
    blocks = lax.map(block, starts)
    return jnp.moveaxis(blocks, 0, 1).reshape(fields.shape)


def reference(state, outer_rows, kappa):
    metric, curvature = geometry(ROWS, NLON)
    first = section_tendency(state, outer_rows, kappa, metric, curvature)
    section = state + time_step * first
    second = section_tendency(section, outer_rows, kappa, metric, curvature)
    return 0.5 * time_step * (first + second)
```

```python
import functools
import math

import jax
import jax.numpy as jnp
import numpy as np
from jax import lax
from jax.experimental import pallas as pl
from jax.experimental.pallas import tpu as pltpu
from jax.sharding import PartitionSpec as P

first_coeffs = (0.8, -0.2, 4.0 / 105.0, -1.0 / 280.0)
second_coeffs = (-205.0 / 72.0, 1.6, -0.2, 8.0 / 315.0, -1.0 / 560.0)
time_step = 0.002
gamma_less_one = 0.4
radial_ratio = 3.0
FIELDS = 5
REACH = 4
TILE = 8
LANES = 128
GROUPS = LANES // (2 * REACH)
signs = (1.0, -1.0, -1.0, 1.0, 1.0)
first_whole = (672.0, -168.0, 32.0, -3.0)
second_whole = (8064.0, -1008.0, 128.0, -9.0)

level_first = tuple(radial_ratio * c for c in first_coeffs)
level_second = tuple(radial_ratio * radial_ratio * c for c in second_coeffs)

VMEM = pl.BlockSpec(memory_space=pltpu.VMEM)
SMEM = pl.BlockSpec(memory_space=pltpu.SMEM)
ANY = pl.BlockSpec(memory_space=pl.ANY)


def held(x):
    return pltpu.with_memory_space_constraint(x, pltpu.VMEM)


def in_vmem(*shape):
    return pltpu.VMEM(shape, jnp.float32)


def stencil_matrix(width):
    matrix = np.zeros((2 * width, 2 * width), np.float32)
    for out in range(width):
        for k in range(1, REACH + 1):
            for sign in (1, -1):
                at = out + sign * k
                if 0 <= at < width:
                    row = at
                elif at < 0:
                    row = width + REACH + at
                else:
                    row = width + REACH + (at - width)
                matrix[row, out] = sign * first_whole[k - 1]
                matrix[row, width + out] = second_whole[k - 1]
    return jnp.asarray(matrix, jnp.bfloat16)


def geometry(rows, nlon, width):
    theta = (np.arange(rows) + 0.5) * (2.0 * math.pi / nlon)
    metric = 1.0 / np.sin(theta)
    table = np.stack([metric / 840.0, metric * metric / 5040.0, np.cos(theta) * metric])
    return jnp.asarray(np.broadcast_to(table[:, :, None], (3, rows, width)), jnp.float32)


def packed(tiles, lane):
    total = None
    for g, tile in enumerate(tiles):
        moved = pltpu.roll(tile, (REACH + 2 * REACH * g) % LANES, 1)
        if total is None:
            total = moved
        else:
            total = jnp.where(lane >= 2 * REACH * g, moved, total)
    return total


def across_level(center_wind, center_temper, halo, kappa, above):
    out = [[None] * REACH for _ in range(FIELDS)]
    for a in range(REACH):
        slopes = []
        for f in range(FIELDS):
            total = None
            for b in range(REACH):
                k = b + REACH - a if above else a + REACH - b
                if 1 <= k <= REACH:
                    c = level_first[k - 1] if above else -level_first[k - 1]
                    term = c * halo[f][b]
                    total = term if total is None else total + term
            slopes.append(total)
        curve = None
        for b in range(REACH):
            k = b + REACH - a if above else a + REACH - b
            if 1 <= k <= REACH:
                term = level_second[k] * halo[4][b]
                curve = term if curve is None else curve + term
        wind, temper = center_wind[a], center_temper[a]
        out[0][a] = -wind * slopes[0] - slopes[3]
        out[1][a] = -wind * slopes[1]
        out[2][a] = -wind * slopes[2]
        out[3][a] = -wind * slopes[3] - temper * slopes[0] - slopes[4]
        out[4][a] = -wind * slopes[4] - (gamma_less_one * temper) * slopes[3] + kappa[a] * curve
    return out


def edges_kernel(levels, rows, state, outer, kappa, padded, low, high, edge, polar, sems, outer_sem):
    block = REACH * rows
    copies = []
    for f in range(FIELDS):
        copies.append(pltpu.make_async_copy(state.at[f], padded.at[f, :, pl.ds(TILE, rows)], sems.at[f]))
        copies[-1].start()
    last = pltpu.make_async_copy(outer, padded.at[:, :, pl.ds(TILE + rows, REACH)], outer_sem)
    last.start()
    for i in range(REACH):
        low[pl.ds(FIELDS * block + i, 1), :] = jnp.full((1, LANES), kappa[i], jnp.float32)
        high[pl.ds(FIELDS * block + i, 1), :] = jnp.full((1, LANES), kappa[levels - REACH + i], jnp.float32)
    low[pl.ds(FIELDS * block + REACH, REACH), :] = jnp.ones((REACH, LANES), jnp.float32)
    high[pl.ds(FIELDS * block + REACH, REACH), :] = jnp.ones((REACH, LANES), jnp.float32)
    lane = lax.broadcasted_iota(jnp.int32, (TILE, LANES), 1)
    for f in range(FIELDS):
        copies[f].wait()
        for l in range(REACH):
            low[pl.ds(f * block + l * rows, rows), :] = padded[f, l, pl.ds(TILE, rows), :]
            high[pl.ds(f * block + l * rows, rows), :] = padded[f, levels - REACH + l, pl.ds(TILE, rows), :]
        pack_edges(f, levels, rows, padded, edge, polar, lane)
    last.wait()


def pack_edges(f, levels, rows, padded, edge, polar, lane):
    per = GROUPS // levels
    for j in range(rows // TILE // per):
        tiles = [
            padded[f, l, pl.ds(TILE + (j * per + u) * TILE, TILE), :]
            for u in range(per)
            for l in range(levels)
        ]
        at = (f * (rows // TILE // per) + j) * TILE
        edge[pl.ds(at, TILE), :] = packed(tiles, lane)
    for l in range(levels):
        for i in range(REACH):
            row = padded[f, l, pl.ds(TILE + REACH - 1 - i, 1), :]
            polar[pl.ds((f * levels + l) * REACH + i, 1), :] = signs[f] * row


def longitude_slopes(levels, rows, padded, left, right, matrix, dlon, elon):
    lane = lax.broadcasted_iota(jnp.int32, (TILE, LANES), 1)
    from_left = (lane % (2 * REACH)) < REACH
    per = GROUPS // levels
    packs = rows // TILE // per
    for f in range(FIELDS):
        halos = [[None] * (rows // TILE) for _ in range(levels)]
        for j in range(packs):
            at = pl.ds((f * packs + j) * TILE, TILE)
            both = jnp.where(from_left, left[at, :], right[at, :])
            for u in range(per):
                for l in range(levels):
                    g = u * levels + l
                    halos[l][j * per + u] = pltpu.roll(both, (LANES - 2 * REACH * g) % LANES, 1)
        x = padded[f, :, pl.ds(TILE, rows), :].reshape(levels * rows, LANES)
        h = jnp.concatenate([halos[l][t] for l in range(levels) for t in range(rows // TILE)], axis=0)
        x = jnp.concatenate([x, h], axis=1)
        width = 2 * LANES if f == 4 else LANES
        m = matrix[:, pl.ds(0, width)]
        total = None
        for piece in range(3):
            part = x.astype(jnp.bfloat16)
            if piece < 2:
                x = x - part.astype(jnp.float32)
            term = jnp.dot(part, m, preferred_element_type=jnp.float32)
            total = term if total is None else total + term
        dlon[f] = total[:, :LANES].reshape(levels, rows, LANES)
        if f == 4:
            elon[...] = total[:, LANES:].reshape(levels, rows, LANES)


def interior(levels, rows, padded, dlon, elon, geo, kappa, store):
    def body(t, carry):
        r0 = pl.multiple_of(t * TILE, TILE)
        here = pl.ds(r0, TILE)
        metric = geo[0, here, :]
        metric2 = geo[1, here, :]
        curvature = geo[2, here, :]
        center = [[padded[f, l, pl.ds(r0 + TILE, TILE), :] for l in range(levels)] for f in range(FIELDS)]
        out = [[None] * levels for _ in range(FIELDS)]
        for l in range(levels):
            wlon, wrow, wlev, temper = (center[f][l] for f in (1, 2, 3, 4))
            slon, srow, slev = [], [], []
            for f in range(FIELDS):
                slon.append(metric * dlon[f, l, here, :])
                total = None
                for k in range(1, REACH + 1):
                    ahead = padded[f, l, pl.ds(r0 + TILE + k, TILE), :]
                    behind = padded[f, l, pl.ds(r0 + TILE - k, TILE), :]
                    term = first_coeffs[k - 1] * (ahead - behind)
                    total = term if total is None else total + term
                    if f == 4:
                        curve = second_coeffs[k] * (ahead + behind)
                        bend = curve if k == 1 else bend + curve
                srow.append(total)
                total = None
                for k in range(1, REACH + 1):
                    up = center[f][l + k] if l + k < levels else None
                    down = center[f][l - k] if l - k >= 0 else None
                    if up is not None and down is not None:
                        term = level_first[k - 1] * (up - down)
                    elif up is not None:
                        term = level_first[k - 1] * up
                    elif down is not None:
                        term = -level_first[k - 1] * down
                    else:
                        continue
                    total = term if total is None else total + term
                slev.append(total)
            lift = None
            for k in range(1, REACH + 1):
                near = [center[4][l + s * k] for s in (1, -1) if 0 <= l + s * k < levels]
                if near:
                    term = level_second[k] * (near[0] + near[1] if len(near) == 2 else near[0])
                    lift = term if lift is None else lift + term
            middle = second_coeffs[0]
            laplace = metric2 * (elon[l, here, :] + (5040.0 * middle) * temper) + bend
            laplace = laplace + (middle + level_second[0]) * temper + lift
            carried = [wlon * slon[f] + wrow * srow[f] + wlev * slev[f] for f in range(FIELDS)]
            spread = slon[1] + srow[2] + slev[3] + curvature * wrow
            out[0][l] = -carried[0] - spread
            out[1][l] = -carried[1] - temper * slon[0] - slon[4]
            out[2][l] = -carried[2] - temper * srow[0] - srow[4]
            out[3][l] = -carried[3] - temper * slev[0] - slev[4]
            out[4][l] = -carried[4] - (gamma_less_one * temper) * spread + kappa[l] * laplace
            for f in range(FIELDS):
                store(f, l, r0, center[f][l], out[f][l])
        return carry

    lax.fori_loop(0, rows // TILE, body, 0)


def fill_polar(levels, padded, polar):
    for f in range(FIELDS):
        for l in range(levels):
            padded[f, l, pl.ds(TILE - REACH, REACH), :] = polar[pl.ds((f * levels + l) * REACH, REACH), :]


def first_kernel(levels, rows, given, polar, left, right, matrix, geo, kappa, padded, rate, low, high, dlon, elon):
    fill_polar(levels, padded, polar)
    longitude_slopes(levels, rows, padded, left, right, matrix, dlon, elon)

    def store(f, l, r0, value, tendency):
        rate[f, l, pl.ds(r0, TILE), :] = tendency
        ahead = value + time_step * tendency
        if l < REACH:
            low[pl.ds((f * REACH + l) * rows + r0, TILE), :] = ahead
        if l >= levels - REACH:
            high[pl.ds((f * REACH + l - levels + REACH) * rows + r0, TILE), :] = ahead

    interior(levels, rows, padded, dlon, elon, geo, kappa, store)


def halo_tile(ref, rows, r0):
    return [
        [ref[pl.ds((f * REACH + b) * rows + r0, TILE), :] for b in range(REACH)] for f in range(FIELDS)
    ]


def section_kernel(levels, rows, padded, rate, below, above, kappa, full, ahead, edge, polar):
    def body(t, carry):
        r0 = pl.multiple_of(t * TILE, TILE)
        for halo_ref, at, up in ((below, 0, False), (above, levels - REACH, True)):
            halo = halo_tile(halo_ref, rows, r0)
            center = [
                [padded[f, at + a, pl.ds(r0 + TILE, TILE), :] for a in range(REACH)] for f in range(FIELDS)
            ]
            extra = across_level(center[3], center[4], halo, [kappa[at + a] for a in range(REACH)], up)
            for f in range(FIELDS):
                for a in range(REACH):
                    total = rate[f, at + a, pl.ds(r0, TILE), :] + extra[f][a]
                    full[f, at + a, pl.ds(r0, TILE), :] = total
                    ahead[f, at + a, pl.ds(r0 + TILE, TILE), :] = center[f][a] + time_step * total
        return carry

    lax.fori_loop(0, rows // TILE, body, 0)
    lane = lax.broadcasted_iota(jnp.int32, (TILE, LANES), 1)
    for f in range(FIELDS):
        pack_edges(f, levels, rows, ahead, edge, polar, lane)
        for l in range(levels):
            ahead[f, l, pl.ds(rows + TILE, REACH), :] = padded[f, l, pl.ds(rows + TILE, REACH), :]


def second_kernel(
    levels, rows, given, polar, left, right, matrix, geo, kappa, full, start, below, above,
    padded, both, low, high, dlon, elon,
):
    fill_polar(levels, padded, polar)
    longitude_slopes(levels, rows, padded, left, right, matrix, dlon, elon)

    def store(f, l, r0, value, tendency):
        at = pl.ds(r0, TILE)
        both[f, l, at, :] = (0.5 * time_step) * (full[f, l, at, :] + tendency)

    interior(levels, rows, padded, dlon, elon, geo, kappa, store)
    tail = FIELDS * REACH * rows

    def body(t, carry):
        r0 = pl.multiple_of(t * TILE, TILE)
        for halo_ref, out, at, up in ((below, low, 0, True), (above, high, levels - REACH, False)):
            beyond = halo_tile(halo_ref, rows, r0)
            mine = [
                [start[f, at + a, pl.ds(r0 + TILE, TILE), :] for a in range(REACH)] for f in range(FIELDS)
            ]
            kappas = [halo_ref[pl.ds(tail + a, 1), :] for a in range(REACH)]
            there = time_step * halo_ref[pl.ds(tail + REACH, 1), :]
            extra = across_level(beyond[3], beyond[4], mine, kappas, up)
            for f in range(FIELDS):
                for a in range(REACH):
                    out[pl.ds((f * REACH + a) * rows + r0, TILE), :] = there * extra[f][a]
        return carry

    lax.fori_loop(0, rows // TILE, body, 0)


def last_kernel(levels, rows, padded, both, below, above, low, high, kappa, out):
    def body(t, carry):
        r0 = pl.multiple_of(t * TILE, TILE)
        for halo_ref, more_ref, at, up in ((below, low, 0, False), (above, high, levels - REACH, True)):
            halo = halo_tile(halo_ref, rows, r0)
            more = halo_tile(more_ref, rows, r0)
            halo = [[halo[f][b] + more[f][b] for b in range(REACH)] for f in range(FIELDS)]
            wind = [padded[3, at + a, pl.ds(r0 + TILE, TILE), :] for a in range(REACH)]
            temper = [padded[4, at + a, pl.ds(r0 + TILE, TILE), :] for a in range(REACH)]
            extra = across_level(wind, temper, halo, [kappa[at + a] for a in range(REACH)], up)
            for f in range(FIELDS):
                for a in range(REACH):
                    old = both[f, at + a, pl.ds(r0, TILE), :]
                    out[f, at + a, pl.ds(r0, TILE), :] = old + (0.5 * time_step) * extra[f][a]
        return carry

    lax.fori_loop(0, rows // TILE, body, 0)


def on_device(state, outer_rows, kappa):
    levels, rows, width = state.shape[1:]
    ring, depth = lax.axis_size("lon"), lax.axis_size("rad")
    assert width == LANES and levels >= 2 * REACH and GROUPS % levels == 0
    assert rows % (TILE * (GROUPS // levels)) == 0
    matrix = stencil_matrix(width)
    geo = geometry(rows, width * ring, width)
    halo_rows = FIELDS * REACH * rows
    packs = FIELDS * levels * rows // GROUPS
    pad_shape = (FIELDS, levels, rows + 2 * TILE, width)
    full_shape = (FIELDS, levels, rows, width)

    def call(kernel, out_shape, in_specs, args, scratch=(), aliases=None, flops=0, name=None):
        args = [held(a) if s is VMEM else a for s, a in zip(in_specs, args)]
        return pl.pallas_call(
            functools.partial(kernel, levels, rows),
            out_shape=out_shape,
            in_specs=list(in_specs),
            out_specs=jax.tree.map(lambda _: VMEM, out_shape),
            scratch_shapes=list(scratch),
            input_output_aliases=aliases or {},
            cost_estimate=pl.CostEstimate(flops=flops, bytes_accessed=0, transcendentals=0),
            compiler_params=pltpu.CompilerParams(vmem_limit_bytes=16 * 2**20),
            name=name,
        )(*args)

    east = [(i, (i + 1) % ring) for i in range(ring)]
    west = [(b, a) for a, b in east]
    half = [(i, (i + ring // 2) % ring) for i in range(ring)]
    up = [(i, i + 1) for i in range(depth - 1)]
    down = [(b, a) for a, b in up]

    def around(edge, polar):
        left = lax.ppermute(edge, "lon", east)
        right = lax.ppermute(edge, "lon", west)
        return left, right, lax.ppermute(polar, "lon", half)

    padded, low, high, edge, polar = call(
        edges_kernel,
        [
            in_vmem(*pad_shape),
            in_vmem(halo_rows + TILE, width),
            in_vmem(halo_rows + TILE, width),
            in_vmem(packs, width),
            in_vmem(FIELDS * levels * REACH, width),
        ],
        (ANY, ANY, SMEM),
        (state, outer_rows, kappa),
        scratch=(pltpu.SemaphoreType.DMA((FIELDS,)), pltpu.SemaphoreType.DMA),
        name="edges",
    )
    below = lax.ppermute(high, "rad", up)
    above = lax.ppermute(low, "rad", down)
    left, right, beyond = around(edge, polar)
    lon_scratch = (in_vmem(*full_shape), in_vmem(*full_shape[1:]))
    padded, rate, low2, high2 = call(
        first_kernel,
        [in_vmem(*pad_shape), in_vmem(*full_shape), in_vmem(halo_rows, width), in_vmem(halo_rows, width)],
        (VMEM,) * 6 + (SMEM,),
        (padded, beyond, left, right, matrix, geo, kappa),
        scratch=lon_scratch,
        aliases={0: 0},
        name="first",
    )
    below2 = lax.ppermute(high2, "rad", up)
    above2 = lax.ppermute(low2, "rad", down)
    full, ahead, edge, polar = call(
        section_kernel,
        [
            in_vmem(*full_shape),
            in_vmem(*pad_shape),
            in_vmem(packs, width),
            in_vmem(FIELDS * levels * REACH, width),
        ],
        (VMEM,) * 4 + (SMEM,),
        (padded, rate, below, above, kappa),
        name="section",
    )
    left, right, beyond = around(edge, polar)
    ahead, both, low, high = call(
        second_kernel,
        [in_vmem(*pad_shape), in_vmem(*full_shape), in_vmem(halo_rows, width), in_vmem(halo_rows, width)],
        (VMEM,) * 6 + (SMEM,) + (VMEM,) * 4,
        (ahead, beyond, left, right, matrix, geo, kappa, full, padded, below, above),
        scratch=lon_scratch,
        aliases={0: 0},
        name="second",
    )
    return call(
        last_kernel,
        jax.ShapeDtypeStruct(full_shape, jnp.float32),
        (VMEM,) * 6 + (SMEM,),
        (ahead, both, below2, above2, low, high, kappa),
        name="last",
    )


def solution(mesh):
    placed = (P(None, "rad", None, "lon"), P(None, "rad", None, "lon"), P("rad"))
    return jax.shard_map(
        on_device,
        mesh=mesh,
        in_specs=placed,
        out_specs=P(None, "rad", None, "lon"),
        check_vma=False,
    )
```

```python
import functools
import math

import jax
import jax.numpy as jnp
import numpy as np
from jax import lax
from jax.experimental import pallas as pl
from jax.experimental.pallas import tpu as pltpu
from jax.sharding import PartitionSpec as P

first_coeffs = (0.8, -0.2, 4.0 / 105.0, -1.0 / 280.0)
second_coeffs = (-205.0 / 72.0, 1.6, -0.2, 8.0 / 315.0, -1.0 / 560.0)
time_step = 0.002
gamma_less_one = 0.4
radial_ratio = 3.0
FIELDS = 5
REACH = 4
TILE = 8
LANES = 128
GROUPS = LANES // (2 * REACH)
signs = (1.0, -1.0, -1.0, 1.0, 1.0)
first_whole = (672.0, -168.0, 32.0, -3.0)
second_whole = (8064.0, -1008.0, 128.0, -9.0)

level_first = tuple(radial_ratio * c for c in first_coeffs)
level_second = tuple(radial_ratio * radial_ratio * c for c in second_coeffs)

VMEM = pl.BlockSpec(memory_space=pltpu.VMEM)
HBM = pl.BlockSpec(memory_space=pltpu.HBM)


def in_vmem(*shape):
    return pltpu.VMEM(shape, jnp.float32)


def stencil_matrix(width):
    matrix = np.zeros((2 * width, 2 * width), np.float32)
    for out in range(width):
        for k in range(1, REACH + 1):
            for sign in (1, -1):
                at = out + sign * k
                if 0 <= at < width:
                    row = at
                elif at < 0:
                    row = width + REACH + at
                else:
                    row = width + REACH + (at - width)
                matrix[row, out] = sign * first_whole[k - 1]
                matrix[row, width + out] = second_whole[k - 1]
    return jnp.asarray(matrix, jnp.bfloat16)


def geometry(rows, nlon, width):
    theta = (np.arange(rows) + 0.5) * (2.0 * math.pi / nlon)
    metric = 1.0 / np.sin(theta)
    table = np.stack([metric / 840.0, metric * metric / 5040.0, np.cos(theta) * metric])
    return jnp.asarray(np.broadcast_to(table[:, :, None], (3, rows, width)), jnp.float32)


def packed(tiles, lane):
    total = None
    for g, tile in enumerate(tiles):
        moved = pltpu.roll(tile, (REACH + 2 * REACH * g) % LANES, 1)
        if total is None:
            total = moved
        else:
            total = jnp.where(lane >= 2 * REACH * g, moved, total)
    return total


def across_level(center_wind, center_temper, halo, kappa, above):
    out = [[None] * REACH for _ in range(FIELDS)]
    for a in range(REACH):
        slopes = []
        for f in range(FIELDS):
            total = None
            for b in range(REACH):
                k = b + REACH - a if above else a + REACH - b
                if 1 <= k <= REACH:
                    c = level_first[k - 1] if above else -level_first[k - 1]
                    term = c * halo[f][b]
                    total = term if total is None else total + term
            slopes.append(total)
        curve = None
        for b in range(REACH):
            k = b + REACH - a if above else a + REACH - b
            if 1 <= k <= REACH:
                term = level_second[k] * halo[4][b]
                curve = term if curve is None else curve + term
        wind, temper = center_wind[a], center_temper[a]
        out[0][a] = -wind * slopes[0] - slopes[3]
        out[1][a] = -wind * slopes[1]
        out[2][a] = -wind * slopes[2]
        out[3][a] = -wind * slopes[3] - temper * slopes[0] - slopes[4]
        out[4][a] = -wind * slopes[4] - (gamma_less_one * temper) * slopes[3] + kappa[a] * curve
    return out


def edges_kernel(
    levels, rows, state, outer, kappa, matrix_in, geo_in,
    padded, low, high, edge, polar, kap, matrix, geo,
    staged, outer_staged, kappa_scalars, sems,
):
    block = REACH * rows
    odd = lax.axis_index("rad") % 2
    mirror = jnp.where(odd == 1, -1.0, 1.0).astype(jnp.float32)
    reads = [(state.at[f], staged.at[f]) for f in range(FIELDS)]
    reads += [(outer, outer_staged), (kappa, kappa_scalars), (matrix_in, matrix), (geo_in, geo)]
    copies = [pltpu.make_async_copy(*read, sems.at[i]) for i, read in enumerate(reads)]
    for copy in copies:
        copy.start()
    lane = lax.broadcasted_iota(jnp.int32, (TILE, LANES), 1)
    for f in range(FIELDS):
        copies[f].wait()
        for l in range(levels):
            whole = staged[f, jnp.where(odd == 1, levels - 1 - l, l)]
            if f == 3:
                whole = mirror * whole
            padded[f, l, pl.ds(TILE, rows), :] = whole
            if l < REACH:
                low[pl.ds(f * block + l * rows, rows), :] = whole
            if l >= levels - REACH:
                high[pl.ds(f * block + (l - levels + REACH) * rows, rows), :] = whole
        pack_edges(f, levels, rows, padded, edge, polar, lane)
    for copy in copies[FIELDS:]:
        copy.wait()
    for l in range(levels):
        real = jnp.where(odd == 1, levels - 1 - l, l)
        value = kappa_scalars[real]
        kap[l] = jnp.full((TILE, LANES), value, jnp.float32)
        if l < REACH:
            low[pl.ds(FIELDS * block + l, 1), :] = jnp.full((1, LANES), value, jnp.float32)
        if l >= levels - REACH:
            high[pl.ds(FIELDS * block + l - levels + REACH, 1), :] = jnp.full((1, LANES), value, jnp.float32)
        for f in range(FIELDS):
            beyond = outer_staged[f, real]
            padded[f, l, pl.ds(TILE + rows, REACH), :] = mirror * beyond if f == 3 else beyond
    low[pl.ds(FIELDS * block + REACH, REACH), :] = jnp.ones((REACH, LANES), jnp.float32)
    high[pl.ds(FIELDS * block + REACH, REACH), :] = jnp.ones((REACH, LANES), jnp.float32)


def pack_edges(f, levels, rows, padded, edge, polar, lane):
    per = GROUPS // levels
    for j in range(rows // TILE // per):
        tiles = [
            padded[f, l, pl.ds(TILE + (j * per + u) * TILE, TILE), :]
            for u in range(per)
            for l in range(levels)
        ]
        at = (f * (rows // TILE // per) + j) * TILE
        edge[pl.ds(at, TILE), :] = packed(tiles, lane)
    for l in range(levels):
        for i in range(REACH):
            row = padded[f, l, pl.ds(TILE + REACH - 1 - i, 1), :]
            polar[pl.ds((f * levels + l) * REACH + i, 1), :] = signs[f] * row


def longitude_slopes(levels, rows, padded, left, right, matrix, dlon, elon):
    lane = lax.broadcasted_iota(jnp.int32, (TILE, LANES), 1)
    from_left = (lane % (2 * REACH)) < REACH
    per = GROUPS // levels
    packs = rows // TILE // per
    for f in range(FIELDS):
        halos = [[None] * (rows // TILE) for _ in range(levels)]
        for j in range(packs):
            at = pl.ds((f * packs + j) * TILE, TILE)
            both = jnp.where(from_left, left[at, :], right[at, :])
            for u in range(per):
                for l in range(levels):
                    g = u * levels + l
                    halos[l][j * per + u] = pltpu.roll(both, (LANES - 2 * REACH * g) % LANES, 1)
        x = padded[f, :, pl.ds(TILE, rows), :].reshape(levels * rows, LANES)
        h = jnp.concatenate([halos[l][t] for l in range(levels) for t in range(rows // TILE)], axis=0)
        x = jnp.concatenate([x, h], axis=1)
        width = 2 * LANES if f == 4 else LANES
        m = matrix[:, pl.ds(0, width)]
        total = None
        for piece in range(3):
            part = x.astype(jnp.bfloat16)
            if piece < 2:
                x = x - part.astype(jnp.float32)
            term = jnp.dot(part, m, preferred_element_type=jnp.float32)
            total = term if total is None else total + term
        dlon[f] = total[:, :LANES].reshape(levels, rows, LANES)
        if f == 4:
            elon[...] = total[:, LANES:].reshape(levels, rows, LANES)


def interior(levels, rows, padded, dlon, elon, geo, kappa, store):
    def body(t, carry):
        r0 = pl.multiple_of(t * TILE, TILE)
        here = pl.ds(r0, TILE)
        metric = geo[0, here, :]
        metric2 = geo[1, here, :]
        curvature = geo[2, here, :]
        center = [[padded[f, l, pl.ds(r0 + TILE, TILE), :] for l in range(levels)] for f in range(FIELDS)]
        out = [[None] * levels for _ in range(FIELDS)]
        for l in range(levels):
            wlon, wrow, wlev, temper = (center[f][l] for f in (1, 2, 3, 4))
            slon, srow, slev = [], [], []
            for f in range(FIELDS):
                slon.append(metric * dlon[f, l, here, :])
                total = None
                for k in range(1, REACH + 1):
                    ahead = padded[f, l, pl.ds(r0 + TILE + k, TILE), :]
                    behind = padded[f, l, pl.ds(r0 + TILE - k, TILE), :]
                    term = first_coeffs[k - 1] * (ahead - behind)
                    total = term if total is None else total + term
                    if f == 4:
                        curve = second_coeffs[k] * (ahead + behind)
                        bend = curve if k == 1 else bend + curve
                srow.append(total)
                total = None
                for k in range(1, REACH + 1):
                    up = center[f][l + k] if l + k < levels else None
                    down = center[f][l - k] if l - k >= 0 else None
                    if up is not None and down is not None:
                        term = level_first[k - 1] * (up - down)
                    elif up is not None:
                        term = level_first[k - 1] * up
                    elif down is not None:
                        term = -level_first[k - 1] * down
                    else:
                        continue
                    total = term if total is None else total + term
                slev.append(total)
            lift = None
            for k in range(1, REACH + 1):
                near = [center[4][l + s * k] for s in (1, -1) if 0 <= l + s * k < levels]
                if near:
                    term = level_second[k] * (near[0] + near[1] if len(near) == 2 else near[0])
                    lift = term if lift is None else lift + term
            middle = second_coeffs[0]
            laplace = metric2 * (elon[l, here, :] + (5040.0 * middle) * temper) + bend
            laplace = laplace + (middle + level_second[0]) * temper + lift
            carried = [wlon * slon[f] + wrow * srow[f] + wlev * slev[f] for f in range(FIELDS)]
            spread = slon[1] + srow[2] + slev[3] + curvature * wrow
            out[0][l] = -carried[0] - spread
            out[1][l] = -carried[1] - temper * slon[0] - slon[4]
            out[2][l] = -carried[2] - temper * srow[0] - srow[4]
            out[3][l] = -carried[3] - temper * slev[0] - slev[4]
            out[4][l] = -carried[4] - (gamma_less_one * temper) * spread + kappa[l] * laplace
            for f in range(FIELDS):
                store(f, l, r0, center[f][l], out[f][l])
        return carry

    lax.fori_loop(0, rows // TILE, body, 0)


def fill_polar(levels, padded, polar):
    for f in range(FIELDS):
        for l in range(levels):
            padded[f, l, pl.ds(TILE - REACH, REACH), :] = polar[pl.ds((f * levels + l) * REACH, REACH), :]


def first_kernel(levels, rows, given, polar, left, right, matrix, geo, kappa, padded, rate, low, high, dlon, elon):
    fill_polar(levels, padded, polar)
    longitude_slopes(levels, rows, padded, left, right, matrix, dlon, elon)

    def store(f, l, r0, value, tendency):
        rate[f, l, pl.ds(r0, TILE), :] = tendency
        ahead = value + time_step * tendency
        if l < REACH:
            low[pl.ds((f * REACH + l) * rows + r0, TILE), :] = ahead
        if l >= levels - REACH:
            high[pl.ds((f * REACH + l - levels + REACH) * rows + r0, TILE), :] = ahead

    interior(levels, rows, padded, dlon, elon, geo, kappa, store)


def halo_tile(ref, rows, r0):
    out = [
        [ref[pl.ds((f * REACH + REACH - 1 - b) * rows + r0, TILE), :] for b in range(REACH)]
        for f in range(FIELDS)
    ]
    out[3] = [-v for v in out[3]]
    return out


def own_tile(ref, rows, r0):
    return [
        [ref[pl.ds((f * REACH + b) * rows + r0, TILE), :] for b in range(REACH)] for f in range(FIELDS)
    ]


def section_kernel(levels, rows, padded, rate, below, above, kappa, full, ahead, edge, polar):
    def body(t, carry):
        r0 = pl.multiple_of(t * TILE, TILE)
        for halo_ref, at, up in ((below, 0, False), (above, levels - REACH, True)):
            halo = halo_tile(halo_ref, rows, r0)
            center = [
                [padded[f, at + a, pl.ds(r0 + TILE, TILE), :] for a in range(REACH)] for f in range(FIELDS)
            ]
            extra = across_level(center[3], center[4], halo, [kappa[at + a] for a in range(REACH)], up)
            for f in range(FIELDS):
                for a in range(REACH):
                    total = rate[f, at + a, pl.ds(r0, TILE), :] + extra[f][a]
                    full[f, at + a, pl.ds(r0, TILE), :] = total
                    ahead[f, at + a, pl.ds(r0 + TILE, TILE), :] = center[f][a] + time_step * total
        return carry

    lax.fori_loop(0, rows // TILE, body, 0)
    lane = lax.broadcasted_iota(jnp.int32, (TILE, LANES), 1)
    for f in range(FIELDS):
        pack_edges(f, levels, rows, ahead, edge, polar, lane)
        for l in range(levels):
            ahead[f, l, pl.ds(rows + TILE, REACH), :] = padded[f, l, pl.ds(rows + TILE, REACH), :]


def second_kernel(
    levels, rows, given, polar, left, right, matrix, geo, kappa, full, start, below, above,
    padded, both, low, high, dlon, elon,
):
    fill_polar(levels, padded, polar)
    longitude_slopes(levels, rows, padded, left, right, matrix, dlon, elon)

    def store(f, l, r0, value, tendency):
        at = pl.ds(r0, TILE)
        both[f, l, at, :] = (0.5 * time_step) * (full[f, l, at, :] + tendency)

    interior(levels, rows, padded, dlon, elon, geo, kappa, store)
    tail = FIELDS * REACH * rows

    def body(t, carry):
        r0 = pl.multiple_of(t * TILE, TILE)
        for halo_ref, out, at, up in ((below, low, 0, True), (above, high, levels - REACH, False)):
            beyond = halo_tile(halo_ref, rows, r0)
            mine = [
                [start[f, at + a, pl.ds(r0 + TILE, TILE), :] for a in range(REACH)] for f in range(FIELDS)
            ]
            kappas = [halo_ref[pl.ds(tail + REACH - 1 - a, 1), :] for a in range(REACH)]
            there = time_step * halo_ref[pl.ds(tail + REACH, 1), :]
            extra = across_level(beyond[3], beyond[4], mine, kappas, up)
            for f in range(FIELDS):
                for a in range(REACH):
                    out[pl.ds((f * REACH + a) * rows + r0, TILE), :] = there * extra[f][a]
        return carry

    lax.fori_loop(0, rows // TILE, body, 0)


def last_kernel(levels, rows, padded, both, below, above, low, high, kappa, out):
    odd = lax.axis_index("rad") % 2
    mirror = jnp.where(odd == 1, -1.0, 1.0).astype(jnp.float32)

    def body(t, carry):
        r0 = pl.multiple_of(t * TILE, TILE)
        for halo_ref, more_ref, at, up in ((below, low, 0, False), (above, high, levels - REACH, True)):
            halo = halo_tile(halo_ref, rows, r0)
            more = own_tile(more_ref, rows, r0)
            halo = [[halo[f][b] + more[f][b] for b in range(REACH)] for f in range(FIELDS)]
            wind = [padded[3, at + a, pl.ds(r0 + TILE, TILE), :] for a in range(REACH)]
            temper = [padded[4, at + a, pl.ds(r0 + TILE, TILE), :] for a in range(REACH)]
            extra = across_level(wind, temper, halo, [kappa[at + a] for a in range(REACH)], up)
            for f in range(FIELDS):
                for a in range(REACH):
                    old = both[f, at + a, pl.ds(r0, TILE), :]
                    new = old + (0.5 * time_step) * extra[f][a]
                    if f == 3:
                        new = mirror * new
                    real = jnp.where(odd == 1, levels - 1 - at - a, at + a)
                    out[f, real, pl.ds(r0, TILE), :] = new
        return carry

    lax.fori_loop(0, rows // TILE, body, 0)


def on_device(state, outer_rows, kappa):
    levels, rows, width = state.shape[1:]
    ring, depth = lax.axis_size("lon"), lax.axis_size("rad")
    assert width == LANES and levels >= 2 * REACH and GROUPS % levels == 0
    assert rows % (TILE * (GROUPS // levels)) == 0
    matrix = stencil_matrix(width)
    geo = geometry(rows, width * ring, width)
    halo_rows = FIELDS * REACH * rows
    packs = FIELDS * levels * rows // GROUPS
    pad_shape = (FIELDS, levels, rows + 2 * TILE, width)
    full_shape = (FIELDS, levels, rows, width)

    def call(kernel, out_shape, in_specs, args, scratch=(), aliases=None, name=None):
        spaces = {id(VMEM): pltpu.VMEM, id(HBM): pltpu.HBM}
        args = [pltpu.with_memory_space_constraint(x, spaces[id(s)]) for s, x in zip(in_specs, args)]
        return pl.pallas_call(
            functools.partial(kernel, levels, rows),
            out_shape=out_shape,
            in_specs=list(in_specs),
            out_specs=jax.tree.map(lambda _: VMEM, out_shape),
            scratch_shapes=list(scratch),
            input_output_aliases=aliases or {},
            compiler_params=pltpu.CompilerParams(vmem_limit_bytes=16 * 2**20),
            name=name,
        )(*args)

    east = [(i, (i + 1) % ring) for i in range(ring)]
    west = [(b, a) for a, b in east]
    half = [(i, (i + ring // 2) % ring) for i in range(ring)]
    swap_high = [p for i in range(0, depth - 1, 2) for p in ((i, i + 1), (i + 1, i))]
    swap_low = [p for i in range(1, depth - 1, 2) for p in ((i, i + 1), (i + 1, i))]

    def around(edge, polar):
        left = lax.ppermute(edge, "lon", east)
        right = lax.ppermute(edge, "lon", west)
        return left, right, lax.ppermute(polar, "lon", half)

    padded, low, high, edge, polar, kap, matrix, geo = call(
        edges_kernel,
        [
            in_vmem(*pad_shape),
            in_vmem(halo_rows + TILE, width),
            in_vmem(halo_rows + TILE, width),
            in_vmem(packs, width),
            in_vmem(FIELDS * levels * REACH, width),
            in_vmem(levels, TILE, width),
            pltpu.VMEM(matrix.shape, matrix.dtype),
            in_vmem(*geo.shape),
        ],
        (HBM,) * 5,
        (state, outer_rows, kappa, matrix, geo),
        scratch=(
            in_vmem(*full_shape),
            in_vmem(*outer_rows.shape),
            pltpu.SMEM(kappa.shape, jnp.float32),
            pltpu.SemaphoreType.DMA((FIELDS + 4,)),
        ),
        name="edges",
    )
    below = lax.ppermute(low, "rad", swap_low)
    above = lax.ppermute(high, "rad", swap_high)
    left, right, beyond = around(edge, polar)
    lon_scratch = (in_vmem(*full_shape), in_vmem(*full_shape[1:]))
    padded, rate, low, high = call(
        first_kernel,
        [in_vmem(*pad_shape), in_vmem(*full_shape), in_vmem(halo_rows, width), in_vmem(halo_rows, width)],
        (VMEM,) * 7,
        (padded, beyond, left, right, matrix, geo, kap),
        scratch=lon_scratch,
        aliases={0: 0},
        name="first",
    )
    below2 = lax.ppermute(low, "rad", swap_low)
    above2 = lax.ppermute(high, "rad", swap_high)
    full, ahead, edge, polar = call(
        section_kernel,
        [
            in_vmem(*full_shape),
            in_vmem(*pad_shape),
            in_vmem(packs, width),
            in_vmem(FIELDS * levels * REACH, width),
        ],
        (VMEM,) * 5,
        (padded, rate, below, above, kap),
        name="section",
    )
    left, right, beyond = around(edge, polar)
    ahead, both, low, high = call(
        second_kernel,
        [in_vmem(*pad_shape), in_vmem(*full_shape), in_vmem(halo_rows, width), in_vmem(halo_rows, width)],
        (VMEM,) * 11,
        (ahead, beyond, left, right, matrix, geo, kap, full, padded, below, above),
        scratch=lon_scratch,
        aliases={0: 0},
        name="second",
    )
    return call(
        last_kernel,
        jax.ShapeDtypeStruct(full_shape, jnp.float32),
        (VMEM,) * 7,
        (ahead, both, below2, above2, low, high, kap),
        name="last",
    )


def solution(mesh):
    placed = (P(None, "rad", None, "lon"), P(None, "rad", None, "lon"), P("rad"))
    return jax.shard_map(
        on_device,
        mesh=mesh,
        in_specs=placed,
        out_specs=P(None, "rad", None, "lon"),
        check_vma=False,
    )
```

```python
import functools
import math

import jax
import jax.numpy as jnp
import numpy as np
from jax import lax
from jax.experimental import pallas as pl
from jax.experimental.pallas import tpu as pltpu
from jax.sharding import PartitionSpec as P

first_coeffs = (0.8, -0.2, 4.0 / 105.0, -1.0 / 280.0)
second_coeffs = (-205.0 / 72.0, 1.6, -0.2, 8.0 / 315.0, -1.0 / 560.0)
time_step = 0.002
gamma_less_one = 0.4
radial_ratio = 3.0
FIELDS = 5
REACH = 4
TILE = 8
LANES = 128
GROUPS = LANES // (2 * REACH)
signs = (1.0, -1.0, -1.0, 1.0, 1.0)
first_whole = (672.0, -168.0, 32.0, -3.0)
second_whole = (8064.0, -1008.0, 128.0, -9.0)

level_first = tuple(radial_ratio * c for c in first_coeffs)
level_second = tuple(radial_ratio * radial_ratio * c for c in second_coeffs)

VMEM = pl.BlockSpec(memory_space=pltpu.VMEM)
HBM = pl.BlockSpec(memory_space=pltpu.HBM)


def in_vmem(*shape):
    return pltpu.VMEM(shape, jnp.float32)


def stencil_matrices(width):
    own = np.zeros((width, 2 * width), np.float32)
    first = np.zeros((width, GROUPS * width), np.float32)
    second = np.zeros((width, GROUPS * width), np.float32)
    for out in range(width):
        for k in range(1, REACH + 1):
            for sign in (1, -1):
                at = out + sign * k
                if 0 <= at < width:
                    own[at, out] = sign * first_whole[k - 1]
                    own[at, width + out] = second_whole[k - 1]
                    continue
                row = REACH + at if at < 0 else REACH + at - width
                for g in range(GROUPS):
                    first[2 * REACH * g + row, g * width + out] = sign * first_whole[k - 1]
                    second[2 * REACH * g + row, g * width + out] = second_whole[k - 1]
    return tuple(jnp.asarray(m, jnp.bfloat16) for m in (own, first, second))


def geometry(rows, nlon, width):
    theta = (np.arange(rows) + 0.5) * (2.0 * math.pi / nlon)
    metric = 1.0 / np.sin(theta)
    table = np.stack([metric / 840.0, metric * metric / 5040.0, np.cos(theta) * metric])
    return jnp.asarray(np.broadcast_to(table[:, :, None], (3, rows, width)), jnp.float32)


def packed(tiles, lane):
    total = None
    for g, tile in enumerate(tiles):
        moved = pltpu.roll(tile, (REACH + 2 * REACH * g) % LANES, 1)
        if total is None:
            total = moved
        else:
            total = jnp.where(lane >= 2 * REACH * g, moved, total)
    return total


def across_level(center_wind, center_temper, halo, kappa, above):
    out = [[None] * REACH for _ in range(FIELDS)]
    for a in range(REACH):
        slopes = []
        for f in range(FIELDS):
            total = None
            for b in range(REACH):
                k = b + REACH - a if above else a + REACH - b
                if 1 <= k <= REACH:
                    c = level_first[k - 1] if above else -level_first[k - 1]
                    term = c * halo[f][b]
                    total = term if total is None else total + term
            slopes.append(total)
        curve = None
        for b in range(REACH):
            k = b + REACH - a if above else a + REACH - b
            if 1 <= k <= REACH:
                term = level_second[k] * halo[4][b]
                curve = term if curve is None else curve + term
        wind, temper = center_wind[a], center_temper[a]
        out[0][a] = -wind * slopes[0] - slopes[3]
        out[1][a] = -wind * slopes[1]
        out[2][a] = -wind * slopes[2]
        out[3][a] = -wind * slopes[3] - temper * slopes[0] - slopes[4]
        out[4][a] = -wind * slopes[4] - (gamma_less_one * temper) * slopes[3] + kappa[a] * curve
    return out


def edges_kernel(
    levels, rows, state, outer, kappa, matrix_in, halo1_in, halo2_in, geo_in,
    padded, low, high, edge, polar, kap, matrix, halo1, halo2, geo,
    staged, outer_staged, kappa_scalars, sems,
):
    block = REACH * rows
    odd = lax.axis_index("rad") % 2
    mirror = jnp.where(odd == 1, -1.0, 1.0).astype(jnp.float32)
    reads = [(state.at[f], staged.at[f]) for f in range(FIELDS)]
    reads += [(outer, outer_staged), (kappa, kappa_scalars), (matrix_in, matrix), (geo_in, geo)]
    reads += [(halo1_in, halo1), (halo2_in, halo2)]
    copies = [pltpu.make_async_copy(*read, sems.at[i]) for i, read in enumerate(reads)]
    for copy in copies:
        copy.start()
    lane = lax.broadcasted_iota(jnp.int32, (TILE, LANES), 1)
    for f in range(FIELDS):
        copies[f].wait()
        for l in range(levels):
            whole = staged[f, jnp.where(odd == 1, levels - 1 - l, l)]
            if f == 3:
                whole = mirror * whole
            padded[f, l, pl.ds(TILE, rows), :] = whole
            padded[f, l, pl.ds(0, TILE), :] = jnp.zeros((TILE, LANES), jnp.float32)
            if l < REACH:
                low[pl.ds(f * block + l * rows, rows), :] = whole
            if l >= levels - REACH:
                high[pl.ds(f * block + (l - levels + REACH) * rows, rows), :] = whole
        pack_edges(f, levels, rows, padded, edge, polar, lane)
    for copy in copies[FIELDS:]:
        copy.wait()
    for l in range(levels):
        real = jnp.where(odd == 1, levels - 1 - l, l)
        value = kappa_scalars[real]
        kap[l] = jnp.full((TILE, LANES), value, jnp.float32)
        if l < REACH:
            low[pl.ds(FIELDS * block + l, 1), :] = jnp.full((1, LANES), value, jnp.float32)
        if l >= levels - REACH:
            high[pl.ds(FIELDS * block + l - levels + REACH, 1), :] = jnp.full((1, LANES), value, jnp.float32)
        for f in range(FIELDS):
            beyond = outer_staged[f, real]
            padded[f, l, pl.ds(TILE + rows, REACH), :] = mirror * beyond if f == 3 else beyond
    low[pl.ds(FIELDS * block + REACH, REACH), :] = jnp.ones((REACH, LANES), jnp.float32)
    high[pl.ds(FIELDS * block + REACH, REACH), :] = jnp.ones((REACH, LANES), jnp.float32)


def pack_edges(f, levels, rows, padded, edge, polar, lane):
    per = GROUPS // levels
    for j in range(rows // TILE // per):
        tiles = [
            padded[f, l, pl.ds(TILE + (j * per + u) * TILE, TILE), :]
            for u in range(per)
            for l in range(levels)
        ]
        at = (f * (rows // TILE // per) + j) * TILE
        edge[pl.ds(at, TILE), :] = packed(tiles, lane)
    for l in range(levels):
        for i in range(REACH):
            row = padded[f, l, pl.ds(TILE + REACH - 1 - i, 1), :]
            polar[pl.ds((f * levels + l) * REACH + i, 1), :] = signs[f] * row


def pieces_of(x):
    out = []
    for piece in range(3):
        out.append(x.astype(jnp.bfloat16))
        if piece < 2:
            x = x - out[-1].astype(jnp.float32)
    return out


def times_whole(pieces, m):
    total = None
    for piece in pieces:
        term = jnp.dot(piece, m, preferred_element_type=jnp.float32)
        total = term if total is None else total + term
    return total


def longitude_slopes(levels, rows, padded, matrix, dlon, elon):
    for f in range(FIELDS):
        x = padded[f, :, pl.ds(TILE, rows), :].reshape(levels * rows, LANES)
        total = times_whole(pieces_of(x), matrix[:, pl.ds(0, 2 * LANES if f == 4 else LANES)])
        dlon[f] = total[:, :LANES].reshape(levels, rows, LANES)
        if f == 4:
            elon[...] = total[:, LANES:].reshape(levels, rows, LANES)


def add_halo(levels, rows, padded, polar, left, right, halo1, halo2, geo, kap, d1, d2, caps, store):
    lane = lax.broadcasted_iota(jnp.int32, left.shape, 1)
    both = jnp.where((lane % (2 * REACH)) < REACH, left[...], right[...])
    split = pieces_of(both)
    packs = rows // TILE // (GROUPS // levels)
    last = slice(4 * packs * TILE, None)
    d1[...] = times_whole(split, halo1[...])
    d2[...] = times_whole([piece[last] for piece in pieces_of(both)], halo2[...])
    for f in range(FIELDS):
        for l in range(levels):
            caps[f, l, pl.ds(TILE - REACH, REACH), :] = polar[pl.ds((f * levels + l) * REACH, REACH), :]
            caps[f, l, pl.ds(TILE, TILE), :] = jnp.zeros((TILE, LANES), jnp.float32)
    for t in range(rows // TILE):
        j, u = divmod(t, GROUPS // levels)
        here = pl.ds(t * TILE, TILE)
        metric, metric2 = geo[0, here, :], geo[1, here, :]
        for l in range(levels):
            columns = pl.ds((u * levels + l) * LANES, LANES)
            center = [padded[f, l, pl.ds((t + 1) * TILE, TILE), :] for f in range(FIELDS)]
            wlon, wrow, temper = center[1], center[2], center[4]
            slon = [metric * d1[pl.ds((f * packs + j) * TILE, TILE), columns] for f in range(FIELDS)]
            laplace = metric2 * d2[pl.ds(j * TILE, TILE), columns]
            extra = [-wlon * slope for slope in slon]
            extra[1] = extra[1] - temper * slon[0] - slon[4]
            spread = slon[1]
            if t == 0:
                srow = []
                for f in range(FIELDS):
                    total = None
                    for k in range(1, REACH + 1):
                        behind = caps[f, l, pl.ds(TILE - k, TILE), :]
                        term = -first_coeffs[k - 1] * behind
                        total = term if total is None else total + term
                        if f == 4:
                            laplace = laplace + second_coeffs[k] * behind
                    srow.append(total)
                extra = [e - wrow * slope for e, slope in zip(extra, srow)]
                extra[2] = extra[2] - temper * srow[0] - srow[4]
                spread = spread + srow[2]
            extra[0] = extra[0] - spread
            extra[4] = extra[4] - (gamma_less_one * temper) * spread + kap[l] * laplace
            for f in range(FIELDS):
                store(f, l, t * TILE, center[f], extra[f])


def interior(levels, rows, padded, dlon, elon, geo, kappa, store):
    def body(t, carry):
        r0 = pl.multiple_of(t * TILE, TILE)
        here = pl.ds(r0, TILE)
        metric = geo[0, here, :]
        metric2 = geo[1, here, :]
        curvature = geo[2, here, :]
        center = [[padded[f, l, pl.ds(r0 + TILE, TILE), :] for l in range(levels)] for f in range(FIELDS)]
        out = [[None] * levels for _ in range(FIELDS)]
        for l in range(levels):
            wlon, wrow, wlev, temper = (center[f][l] for f in (1, 2, 3, 4))
            slon, srow, slev = [], [], []
            for f in range(FIELDS):
                slon.append(metric * dlon[f, l, here, :])
                total = None
                for k in range(1, REACH + 1):
                    ahead = padded[f, l, pl.ds(r0 + TILE + k, TILE), :]
                    behind = padded[f, l, pl.ds(r0 + TILE - k, TILE), :]
                    term = first_coeffs[k - 1] * (ahead - behind)
                    total = term if total is None else total + term
                    if f == 4:
                        curve = second_coeffs[k] * (ahead + behind)
                        bend = curve if k == 1 else bend + curve
                srow.append(total)
                total = None
                for k in range(1, REACH + 1):
                    up = center[f][l + k] if l + k < levels else None
                    down = center[f][l - k] if l - k >= 0 else None
                    if up is not None and down is not None:
                        term = level_first[k - 1] * (up - down)
                    elif up is not None:
                        term = level_first[k - 1] * up
                    elif down is not None:
                        term = -level_first[k - 1] * down
                    else:
                        continue
                    total = term if total is None else total + term
                slev.append(total)
            lift = None
            for k in range(1, REACH + 1):
                near = [center[4][l + s * k] for s in (1, -1) if 0 <= l + s * k < levels]
                if near:
                    term = level_second[k] * (near[0] + near[1] if len(near) == 2 else near[0])
                    lift = term if lift is None else lift + term
            middle = second_coeffs[0]
            laplace = metric2 * (elon[l, here, :] + (5040.0 * middle) * temper) + bend
            laplace = laplace + (middle + level_second[0]) * temper + lift
            carried = [wlon * slon[f] + wrow * srow[f] + wlev * slev[f] for f in range(FIELDS)]
            spread = slon[1] + srow[2] + slev[3] + curvature * wrow
            out[0][l] = -carried[0] - spread
            out[1][l] = -carried[1] - temper * slon[0] - slon[4]
            out[2][l] = -carried[2] - temper * srow[0] - srow[4]
            out[3][l] = -carried[3] - temper * slev[0] - slev[4]
            out[4][l] = -carried[4] - (gamma_less_one * temper) * spread + kappa[l] * laplace
            for f in range(FIELDS):
                store(f, l, r0, out[f][l])
        return carry

    lax.fori_loop(0, rows // TILE, body, 0)


def first_kernel(levels, rows, padded, matrix, geo, kap, rate, dlon, elon):
    longitude_slopes(levels, rows, padded, matrix, dlon, elon)

    def store(f, l, r0, tendency):
        rate[f, l, pl.ds(r0, TILE), :] = tendency

    interior(levels, rows, padded, dlon, elon, geo, kap, store)


def first_halo_kernel(
    levels, rows, given, padded, polar, left, right, halo1, halo2, geo, kap, rate, low, high, d1, d2, caps
):
    def store(f, l, r0, value, extra):
        tendency = given[f, l, pl.ds(r0, TILE), :] + extra
        rate[f, l, pl.ds(r0, TILE), :] = tendency
        ahead = value + time_step * tendency
        if l < REACH:
            low[pl.ds((f * REACH + l) * rows + r0, TILE), :] = ahead
        if l >= levels - REACH:
            high[pl.ds((f * REACH + l - levels + REACH) * rows + r0, TILE), :] = ahead

    add_halo(levels, rows, padded, polar, left, right, halo1, halo2, geo, kap, d1, d2, caps, store)


def halo_tile(ref, rows, r0):
    out = [
        [ref[pl.ds((f * REACH + REACH - 1 - b) * rows + r0, TILE), :] for b in range(REACH)]
        for f in range(FIELDS)
    ]
    out[3] = [-v for v in out[3]]
    return out


def own_tile(ref, rows, r0):
    return [
        [ref[pl.ds((f * REACH + b) * rows + r0, TILE), :] for b in range(REACH)] for f in range(FIELDS)
    ]


def section_kernel(levels, rows, padded, rate, below, above, kappa, full, ahead, edge, polar):
    def body(t, carry):
        r0 = pl.multiple_of(t * TILE, TILE)
        for halo_ref, at, up in ((below, 0, False), (above, levels - REACH, True)):
            halo = halo_tile(halo_ref, rows, r0)
            center = [
                [padded[f, at + a, pl.ds(r0 + TILE, TILE), :] for a in range(REACH)] for f in range(FIELDS)
            ]
            extra = across_level(center[3], center[4], halo, [kappa[at + a] for a in range(REACH)], up)
            for f in range(FIELDS):
                for a in range(REACH):
                    total = rate[f, at + a, pl.ds(r0, TILE), :] + extra[f][a]
                    full[f, at + a, pl.ds(r0, TILE), :] = total
                    ahead[f, at + a, pl.ds(r0 + TILE, TILE), :] = center[f][a] + time_step * total
        return carry

    lax.fori_loop(0, rows // TILE, body, 0)
    lane = lax.broadcasted_iota(jnp.int32, (TILE, LANES), 1)
    for f in range(FIELDS):
        pack_edges(f, levels, rows, ahead, edge, polar, lane)
        for l in range(levels):
            ahead[f, l, pl.ds(0, TILE), :] = jnp.zeros((TILE, LANES), jnp.float32)
            ahead[f, l, pl.ds(rows + TILE, REACH), :] = padded[f, l, pl.ds(rows + TILE, REACH), :]


def second_kernel(
    levels, rows, padded, matrix, geo, kap, full, start, below, above, both, low, high, dlon, elon
):
    longitude_slopes(levels, rows, padded, matrix, dlon, elon)

    def store(f, l, r0, tendency):
        at = pl.ds(r0, TILE)
        both[f, l, at, :] = (0.5 * time_step) * (full[f, l, at, :] + tendency)

    interior(levels, rows, padded, dlon, elon, geo, kap, store)
    tail = FIELDS * REACH * rows

    def body(t, carry):
        r0 = pl.multiple_of(t * TILE, TILE)
        for halo_ref, out, at, up in ((below, low, 0, True), (above, high, levels - REACH, False)):
            beyond = halo_tile(halo_ref, rows, r0)
            mine = [
                [start[f, at + a, pl.ds(r0 + TILE, TILE), :] for a in range(REACH)] for f in range(FIELDS)
            ]
            kappas = [halo_ref[pl.ds(tail + REACH - 1 - a, 1), :] for a in range(REACH)]
            there = time_step * halo_ref[pl.ds(tail + REACH, 1), :]
            extra = across_level(beyond[3], beyond[4], mine, kappas, up)
            for f in range(FIELDS):
                for a in range(REACH):
                    out[pl.ds((f * REACH + a) * rows + r0, TILE), :] = there * extra[f][a]
        return carry

    lax.fori_loop(0, rows // TILE, body, 0)


def second_halo_kernel(
    levels, rows, given, padded, polar, left, right, halo1, halo2, geo, kap, both, d1, d2, caps
):
    def store(f, l, r0, value, extra):
        at = pl.ds(r0, TILE)
        both[f, l, at, :] = given[f, l, at, :] + (0.5 * time_step) * extra

    add_halo(levels, rows, padded, polar, left, right, halo1, halo2, geo, kap, d1, d2, caps, store)


def last_kernel(levels, rows, padded, both, below, above, low, high, kappa, out):
    odd = lax.axis_index("rad") % 2
    mirror = jnp.where(odd == 1, -1.0, 1.0).astype(jnp.float32)

    def body(t, carry):
        r0 = pl.multiple_of(t * TILE, TILE)
        for halo_ref, more_ref, at, up in ((below, low, 0, False), (above, high, levels - REACH, True)):
            halo = halo_tile(halo_ref, rows, r0)
            more = own_tile(more_ref, rows, r0)
            halo = [[halo[f][b] + more[f][b] for b in range(REACH)] for f in range(FIELDS)]
            wind = [padded[3, at + a, pl.ds(r0 + TILE, TILE), :] for a in range(REACH)]
            temper = [padded[4, at + a, pl.ds(r0 + TILE, TILE), :] for a in range(REACH)]
            extra = across_level(wind, temper, halo, [kappa[at + a] for a in range(REACH)], up)
            for f in range(FIELDS):
                for a in range(REACH):
                    old = both[f, at + a, pl.ds(r0, TILE), :]
                    new = old + (0.5 * time_step) * extra[f][a]
                    if f == 3:
                        new = mirror * new
                    real = jnp.where(odd == 1, levels - 1 - at - a, at + a)
                    out[f, real, pl.ds(r0, TILE), :] = new
        return carry

    lax.fori_loop(0, rows // TILE, body, 0)


def on_device(state, outer_rows, kappa):
    levels, rows, width = state.shape[1:]
    ring, depth = lax.axis_size("lon"), lax.axis_size("rad")
    assert width == LANES and levels >= 2 * REACH and GROUPS % levels == 0
    assert rows % (TILE * (GROUPS // levels)) == 0
    matrices = stencil_matrices(width)
    geo = geometry(rows, width * ring, width)
    halo_rows = FIELDS * REACH * rows
    packs = FIELDS * levels * rows // GROUPS
    pad_shape = (FIELDS, levels, rows + 2 * TILE, width)
    full_shape = (FIELDS, levels, rows, width)

    def call(kernel, out_shape, in_specs, args, scratch=(), aliases=None, cost=1.0, name=None):
        spaces = {id(VMEM): pltpu.VMEM, id(HBM): pltpu.HBM}
        args = [pltpu.with_memory_space_constraint(x, spaces[id(s)]) for s, x in zip(in_specs, args)]
        return pl.pallas_call(
            functools.partial(kernel, levels, rows),
            out_shape=out_shape,
            in_specs=list(in_specs),
            out_specs=jax.tree.map(lambda _: VMEM, out_shape),
            scratch_shapes=list(scratch),
            input_output_aliases=aliases or {},
            cost_estimate=pl.CostEstimate(flops=0, bytes_accessed=int(cost * 3.69e6), transcendentals=0),
            compiler_params=pltpu.CompilerParams(vmem_limit_bytes=16 * 2**20),
            name=name,
        )(*args)

    east = [(i, (i + 1) % ring) for i in range(ring)]
    west = [(b, a) for a, b in east]
    half = [(i, (i + ring // 2) % ring) for i in range(ring)]
    swap_high = [p for i in range(0, depth - 1, 2) for p in ((i, i + 1), (i + 1, i))]
    swap_low = [p for i in range(1, depth - 1, 2) for p in ((i, i + 1), (i + 1, i))]

    def around(edge, polar):
        left = lax.ppermute(edge, "lon", east)
        right = lax.ppermute(edge, "lon", west)
        return left, right, lax.ppermute(polar, "lon", half)

    padded, low, high, edge, polar, kap, matrix, halo1, halo2, geo = call(
        edges_kernel,
        [
            in_vmem(*pad_shape),
            in_vmem(halo_rows + TILE, width),
            in_vmem(halo_rows + TILE, width),
            in_vmem(packs, width),
            in_vmem(FIELDS * levels * REACH, width),
            in_vmem(levels, TILE, width),
            *(pltpu.VMEM(m.shape, m.dtype) for m in matrices),
            in_vmem(*geo.shape),
        ],
        (HBM,) * 7,
        (state, outer_rows, kappa, *matrices, geo),
        scratch=(
            in_vmem(*full_shape),
            in_vmem(*outer_rows.shape),
            pltpu.SMEM(kappa.shape, jnp.float32),
            pltpu.SemaphoreType.DMA((FIELDS + 6,)),
        ),
        name="edges",
    )
    below = lax.ppermute(low, "rad", swap_low)
    above = lax.ppermute(high, "rad", swap_high)
    left, right, beyond = around(edge, polar)
    lon_scratch = (in_vmem(*full_shape), in_vmem(*full_shape[1:]))
    halo_scratch = (
        in_vmem(packs, GROUPS * width),
        in_vmem(packs // FIELDS, GROUPS * width),
        in_vmem(FIELDS, levels, 2 * TILE, width),
    )
    side = in_vmem(halo_rows, width)
    rate = call(
        first_kernel,
        in_vmem(*full_shape),
        (VMEM,) * 4,
        (padded, matrix, geo, kap),
        scratch=lon_scratch,
        cost=2.0,
        name="first",
    )
    rate, low, high = call(
        first_halo_kernel,
        [in_vmem(*full_shape), side, side],
        (VMEM,) * 9,
        (rate, padded, beyond, left, right, halo1, halo2, geo, kap),
        scratch=halo_scratch,
        aliases={0: 0},
        name="first_halo",
    )
    below2 = lax.ppermute(low, "rad", swap_low)
    above2 = lax.ppermute(high, "rad", swap_high)
    full, ahead, edge, polar = call(
        section_kernel,
        [
            in_vmem(*full_shape),
            in_vmem(*pad_shape),
            in_vmem(packs, width),
            in_vmem(FIELDS * levels * REACH, width),
        ],
        (VMEM,) * 5,
        (padded, rate, below, above, kap),
        name="section",
    )
    left, right, beyond = around(edge, polar)
    both, low, high = call(
        second_kernel,
        [in_vmem(*full_shape), side, side],
        (VMEM,) * 8,
        (ahead, matrix, geo, kap, full, padded, below, above),
        scratch=lon_scratch,
        cost=2.5,
        name="second",
    )
    both = call(
        second_halo_kernel,
        in_vmem(*full_shape),
        (VMEM,) * 9,
        (both, ahead, beyond, left, right, halo1, halo2, geo, kap),
        scratch=halo_scratch,
        aliases={0: 0},
        name="second_halo",
    )
    return call(
        last_kernel,
        jax.ShapeDtypeStruct(full_shape, jnp.float32),
        (VMEM,) * 7,
        (ahead, both, below2, above2, low, high, kap),
        name="last",
    )


def solution(mesh):
    placed = (P(None, "rad", None, "lon"), P(None, "rad", None, "lon"), P("rad"))
    return jax.shard_map(
        on_device,
        mesh=mesh,
        in_specs=placed,
        out_specs=P(None, "rad", None, "lon"),
        check_vma=False,
    )
```

```python
import functools
import math

import jax
import jax.numpy as jnp
import numpy as np
from jax import lax
from jax.experimental import pallas as pl
from jax.experimental.pallas import tpu as pltpu
from jax.sharding import PartitionSpec as P

first_coeffs = (0.8, -0.2, 4.0 / 105.0, -1.0 / 280.0)
second_coeffs = (-205.0 / 72.0, 1.6, -0.2, 8.0 / 315.0, -1.0 / 560.0)
time_step = 0.002
gamma_less_one = 0.4
radial_ratio = 3.0
FIELDS = 5
REACH = 4
TILE = 8
LANES = 128
GROUPS = LANES // (2 * REACH)
signs = (1.0, -1.0, -1.0, 1.0, 1.0)
first_whole = (672.0, -168.0, 32.0, -3.0)
second_whole = (8064.0, -1008.0, 128.0, -9.0)

level_first = tuple(radial_ratio * c for c in first_coeffs)
level_second = tuple(radial_ratio * radial_ratio * c for c in second_coeffs)

VMEM = pl.BlockSpec(memory_space=pltpu.VMEM)
HBM = pl.BlockSpec(memory_space=pltpu.HBM)


def in_vmem(*shape):
    return pltpu.VMEM(shape, jnp.float32)


def stencil_matrices(width):
    own = np.zeros((width, 2 * width), np.float32)
    first = np.zeros((width, GROUPS * width), np.float32)
    second = np.zeros((width, GROUPS * width), np.float32)
    for out in range(width):
        for k in range(1, REACH + 1):
            for sign in (1, -1):
                at = out + sign * k
                if 0 <= at < width:
                    own[at, out] = sign * first_whole[k - 1]
                    own[at, width + out] = second_whole[k - 1]
                    continue
                row = REACH + at if at < 0 else REACH + at - width
                for g in range(GROUPS):
                    first[2 * REACH * g + row, g * width + out] = sign * first_whole[k - 1]
                    second[2 * REACH * g + row, g * width + out] = second_whole[k - 1]
    return tuple(jnp.asarray(m, jnp.bfloat16) for m in (own, first, second))


def geometry(rows, nlon, width):
    theta = (np.arange(rows) + 0.5) * (2.0 * math.pi / nlon)
    metric = 1.0 / np.sin(theta)
    table = np.stack([metric / 840.0, metric * metric / 5040.0, np.cos(theta) * metric])
    return jnp.asarray(np.broadcast_to(table[:, :, None], (3, rows, width)), jnp.float32)


def packed(tiles, lane):
    total = None
    for g, tile in enumerate(tiles):
        moved = pltpu.roll(tile, (REACH + 2 * REACH * g) % LANES, 1)
        if total is None:
            total = moved
        else:
            total = jnp.where(lane >= 2 * REACH * g, moved, total)
    return total


def across_level(center_wind, center_temper, halo, kappa, above):
    out = [[None] * REACH for _ in range(FIELDS)]
    for a in range(REACH):
        slopes = []
        for f in range(FIELDS):
            total = None
            for b in range(REACH):
                k = b + REACH - a if above else a + REACH - b
                if 1 <= k <= REACH:
                    c = level_first[k - 1] if above else -level_first[k - 1]
                    term = c * halo[f][b]
                    total = term if total is None else total + term
            slopes.append(total)
        curve = None
        for b in range(REACH):
            k = b + REACH - a if above else a + REACH - b
            if 1 <= k <= REACH:
                term = level_second[k] * halo[4][b]
                curve = term if curve is None else curve + term
        wind, temper = center_wind[a], center_temper[a]
        out[0][a] = -wind * slopes[0] - slopes[3]
        out[1][a] = -wind * slopes[1]
        out[2][a] = -wind * slopes[2]
        out[3][a] = -wind * slopes[3] - temper * slopes[0] - slopes[4]
        out[4][a] = -wind * slopes[4] - (gamma_less_one * temper) * slopes[3] + kappa[a] * curve
    return out


def mirrored():
    odd = (lax.axis_index("rad") + lax.axis_index("lon")) % 2
    return odd, jnp.where(odd == 1, -1.0, 1.0).astype(jnp.float32)


def edges_kernel(
    levels, rows, state, outer, kappa, matrix_in, geo_in,
    padded, low, high, edge, polar, kap, matrix, geo,
    staged, outer_staged, kappa_scalars, sems,
):
    block, field = REACH * rows, levels * rows
    odd, mirror = mirrored()
    starts = [jnp.where(odd == side, 0, levels - REACH) for side in (0, 1)]
    reads = [(kappa, kappa_scalars)]
    for start, side in zip(starts[::-1], (high, low)):
        for f in range(FIELDS):
            at = pl.multiple_of(f * field + start * rows, TILE)
            reads.append((state.at[pl.ds(at, block)], side.at[pl.ds(f * block, block)]))
    for f in range(FIELDS):
        at = pl.ds(f * field, field)
        reads.append((state.at[at], staged.at[at]))
    reads += [(outer, outer_staged), (matrix_in, matrix), (geo_in, geo)]
    copies = [pltpu.make_async_copy(*read, sems.at[i]) for i, read in enumerate(reads)]
    for copy in copies:
        copy.start()
    copies[0].wait()
    for l in range(levels):
        kap[l] = jnp.full((TILE, LANES), kappa_scalars[jnp.where(odd == 1, levels - 1 - l, l)], jnp.float32)
    for start, side in zip(starts, (low, high)):
        for i in range(REACH):
            value = kappa_scalars[start + i]
            side[pl.ds(FIELDS * block + i, 1), :] = jnp.full((1, LANES), value, jnp.float32)
        side[pl.ds(FIELDS * block + REACH, REACH), :] = jnp.ones((REACH, LANES), jnp.float32)
    lane = lax.broadcasted_iota(jnp.int32, (TILE, LANES), 1)
    for f in range(FIELDS):
        copies[1 + 2 * FIELDS + f].wait()
        for l in range(levels):
            at = f * field + jnp.where(odd == 1, levels - 1 - l, l) * rows
            whole = staged[pl.ds(pl.multiple_of(at, TILE), rows), :]
            padded[f, l, pl.ds(TILE, rows), :] = mirror * whole if f == 3 else whole
            padded[f, l, pl.ds(0, TILE), :] = jnp.zeros((TILE, LANES), jnp.float32)
        pack_edges(f, levels, rows, padded, edge, polar, lane)
    for i, copy in enumerate(copies):
        if 1 <= i <= 2 * FIELDS or i > 3 * FIELDS:
            copy.wait()
    for l in range(levels):
        for f in range(FIELDS):
            beyond = outer_staged[f, jnp.where(odd == 1, levels - 1 - l, l)]
            padded[f, l, pl.ds(TILE + rows, REACH), :] = mirror * beyond if f == 3 else beyond


def pack_edges(f, levels, rows, padded, edge, polar, lane):
    per = GROUPS // levels
    for j in range(rows // TILE // per):
        tiles = [
            padded[f, l, pl.ds(TILE + (j * per + u) * TILE, TILE), :]
            for u in range(per)
            for l in range(levels)
        ]
        at = (f * (rows // TILE // per) + j) * TILE
        edge[pl.ds(at, TILE), :] = packed(tiles, lane)
    for l in range(levels):
        for i in range(REACH):
            row = padded[f, l, pl.ds(TILE + REACH - 1 - i, 1), :]
            polar[pl.ds((f * levels + l) * REACH + i, 1), :] = signs[f] * row


def pieces_of(x):
    out = []
    for piece in range(3):
        out.append(x.astype(jnp.bfloat16))
        if piece < 2:
            x = x - out[-1].astype(jnp.float32)
    return out


def times_whole(pieces, m):
    total = None
    for piece in pieces:
        term = jnp.dot(piece, m, preferred_element_type=jnp.float32)
        total = term if total is None else total + term
    return total


def longitude_slopes(levels, rows, padded, matrix, dlon, elon):
    for f in range(FIELDS):
        x = padded[f, :, pl.ds(TILE, rows), :].reshape(levels * rows, LANES)
        total = times_whole(pieces_of(x), matrix[:, pl.ds(0, 2 * LANES if f == 4 else LANES)])
        dlon[f] = total[:, :LANES].reshape(levels, rows, LANES)
        if f == 4:
            elon[...] = total[:, LANES:].reshape(levels, rows, LANES)


def add_halo(levels, rows, padded, polar, left, right, halo1, halo2, geo, kap, d1, d2, caps, store):
    lane = lax.broadcasted_iota(jnp.int32, left.shape, 1)
    both = jnp.where((lane % (2 * REACH)) < REACH, left[...], right[...])
    split = pieces_of(both)
    packs = rows // TILE // (GROUPS // levels)
    last = slice(4 * packs * TILE, None)
    d1[...] = times_whole(split, halo1[...])
    d2[...] = times_whole([piece[last] for piece in pieces_of(both)], halo2[...])
    for f in range(FIELDS):
        for l in range(levels):
            caps[f, l, pl.ds(TILE - REACH, REACH), :] = polar[pl.ds((f * levels + l) * REACH, REACH), :]
            caps[f, l, pl.ds(TILE, TILE), :] = jnp.zeros((TILE, LANES), jnp.float32)
    for t in range(rows // TILE):
        j, u = divmod(t, GROUPS // levels)
        here = pl.ds(t * TILE, TILE)
        metric, metric2 = geo[0, here, :], geo[1, here, :]
        for l in range(levels):
            columns = pl.ds((u * levels + levels - 1 - l) * LANES, LANES)
            center = [padded[f, l, pl.ds((t + 1) * TILE, TILE), :] for f in range(FIELDS)]
            wlon, wrow, temper = center[1], center[2], center[4]
            slon = [metric * d1[pl.ds((f * packs + j) * TILE, TILE), columns] for f in range(FIELDS)]
            slon[3] = -slon[3]
            laplace = metric2 * d2[pl.ds(j * TILE, TILE), columns]
            extra = [-wlon * slope for slope in slon]
            extra[1] = extra[1] - temper * slon[0] - slon[4]
            spread = slon[1]
            if t == 0:
                srow = []
                for f in range(FIELDS):
                    total = None
                    for k in range(1, REACH + 1):
                        behind = caps[f, l, pl.ds(TILE - k, TILE), :]
                        term = -first_coeffs[k - 1] * behind
                        total = term if total is None else total + term
                        if f == 4:
                            laplace = laplace + second_coeffs[k] * behind
                    srow.append(total)
                extra = [e - wrow * slope for e, slope in zip(extra, srow)]
                extra[2] = extra[2] - temper * srow[0] - srow[4]
                spread = spread + srow[2]
            extra[0] = extra[0] - spread
            extra[4] = extra[4] - (gamma_less_one * temper) * spread + kap[l] * laplace
            for f in range(FIELDS):
                store(f, l, t * TILE, center[f], extra[f])


def interior(levels, rows, padded, dlon, elon, geo, kappa, store):
    def body(t, carry):
        r0 = pl.multiple_of(t * TILE, TILE)
        here = pl.ds(r0, TILE)
        metric = geo[0, here, :]
        metric2 = geo[1, here, :]
        curvature = geo[2, here, :]
        center = [[padded[f, l, pl.ds(r0 + TILE, TILE), :] for l in range(levels)] for f in range(FIELDS)]
        out = [[None] * levels for _ in range(FIELDS)]
        for l in range(levels):
            wlon, wrow, wlev, temper = (center[f][l] for f in (1, 2, 3, 4))
            slon, srow, slev = [], [], []
            for f in range(FIELDS):
                slon.append(metric * dlon[f, l, here, :])
                total = None
                for k in range(1, REACH + 1):
                    ahead = padded[f, l, pl.ds(r0 + TILE + k, TILE), :]
                    behind = padded[f, l, pl.ds(r0 + TILE - k, TILE), :]
                    term = first_coeffs[k - 1] * (ahead - behind)
                    total = term if total is None else total + term
                    if f == 4:
                        curve = second_coeffs[k] * (ahead + behind)
                        bend = curve if k == 1 else bend + curve
                srow.append(total)
                total = None
                for k in range(1, REACH + 1):
                    up = center[f][l + k] if l + k < levels else None
                    down = center[f][l - k] if l - k >= 0 else None
                    if up is not None and down is not None:
                        term = level_first[k - 1] * (up - down)
                    elif up is not None:
                        term = level_first[k - 1] * up
                    elif down is not None:
                        term = -level_first[k - 1] * down
                    else:
                        continue
                    total = term if total is None else total + term
                slev.append(total)
            lift = None
            for k in range(1, REACH + 1):
                near = [center[4][l + s * k] for s in (1, -1) if 0 <= l + s * k < levels]
                if near:
                    term = level_second[k] * (near[0] + near[1] if len(near) == 2 else near[0])
                    lift = term if lift is None else lift + term
            middle = second_coeffs[0]
            laplace = metric2 * (elon[l, here, :] + (5040.0 * middle) * temper) + bend
            laplace = laplace + (middle + level_second[0]) * temper + lift
            carried = [wlon * slon[f] + wrow * srow[f] + wlev * slev[f] for f in range(FIELDS)]
            spread = slon[1] + srow[2] + slev[3] + curvature * wrow
            out[0][l] = -carried[0] - spread
            out[1][l] = -carried[1] - temper * slon[0] - slon[4]
            out[2][l] = -carried[2] - temper * srow[0] - srow[4]
            out[3][l] = -carried[3] - temper * slev[0] - slev[4]
            out[4][l] = -carried[4] - (gamma_less_one * temper) * spread + kappa[l] * laplace
            for f in range(FIELDS):
                store(f, l, r0, out[f][l])
        return carry

    lax.fori_loop(0, rows // TILE, body, 0)


def first_kernel(
    levels, rows, padded, matrix, geo, kap, halo1_in, halo2_in, rate, halo1, halo2, dlon, elon, sems
):
    reads = ((halo1_in, halo1), (halo2_in, halo2))
    copies = [pltpu.make_async_copy(*read, sems.at[i]) for i, read in enumerate(reads)]
    for copy in copies:
        copy.start()
    longitude_slopes(levels, rows, padded, matrix, dlon, elon)

    def store(f, l, r0, tendency):
        rate[f, l, pl.ds(r0, TILE), :] = tendency

    interior(levels, rows, padded, dlon, elon, geo, kap, store)
    for copy in copies:
        copy.wait()


def first_halo_kernel(
    levels, rows, given, padded, polar, left, right, halo1, halo2, geo, kap, rate, low, high, d1, d2, caps
):
    def store(f, l, r0, value, extra):
        tendency = given[f, l, pl.ds(r0, TILE), :] + extra
        rate[f, l, pl.ds(r0, TILE), :] = tendency
        ahead = value + time_step * tendency
        if l < REACH:
            low[pl.ds((f * REACH + l) * rows + r0, TILE), :] = ahead
        if l >= levels - REACH:
            high[pl.ds((f * REACH + l - levels + REACH) * rows + r0, TILE), :] = ahead

    add_halo(levels, rows, padded, polar, left, right, halo1, halo2, geo, kap, d1, d2, caps, store)


def raw_tile(ref, rows, r0, odd, mirror):
    out = []
    for f in range(FIELDS):
        ats = [(f * REACH + jnp.where(odd == 1, REACH - 1 - b, b)) * rows + r0 for b in range(REACH)]
        out.append([ref[pl.ds(pl.multiple_of(at, TILE), TILE), :] for at in ats])
    out[3] = [mirror * v for v in out[3]]
    return out


def halo_tile(ref, rows, r0):
    out = [
        [ref[pl.ds((f * REACH + REACH - 1 - b) * rows + r0, TILE), :] for b in range(REACH)]
        for f in range(FIELDS)
    ]
    out[3] = [-v for v in out[3]]
    return out


def own_tile(ref, rows, r0):
    return [
        [ref[pl.ds((f * REACH + b) * rows + r0, TILE), :] for b in range(REACH)] for f in range(FIELDS)
    ]


def section_kernel(levels, rows, padded, rate, below, above, kappa, full, ahead, edge, polar):
    odd, mirror = mirrored()

    def body(t, carry):
        r0 = pl.multiple_of(t * TILE, TILE)
        for halo_ref, at, up in ((below, 0, False), (above, levels - REACH, True)):
            halo = raw_tile(halo_ref, rows, r0, odd, mirror)
            center = [
                [padded[f, at + a, pl.ds(r0 + TILE, TILE), :] for a in range(REACH)] for f in range(FIELDS)
            ]
            extra = across_level(center[3], center[4], halo, [kappa[at + a] for a in range(REACH)], up)
            for f in range(FIELDS):
                for a in range(REACH):
                    total = rate[f, at + a, pl.ds(r0, TILE), :] + extra[f][a]
                    full[f, at + a, pl.ds(r0, TILE), :] = total
                    ahead[f, at + a, pl.ds(r0 + TILE, TILE), :] = center[f][a] + time_step * total
        return carry

    lax.fori_loop(0, rows // TILE, body, 0)
    lane = lax.broadcasted_iota(jnp.int32, (TILE, LANES), 1)
    for f in range(FIELDS):
        pack_edges(f, levels, rows, ahead, edge, polar, lane)
        for l in range(levels):
            ahead[f, l, pl.ds(0, TILE), :] = jnp.zeros((TILE, LANES), jnp.float32)
            ahead[f, l, pl.ds(rows + TILE, REACH), :] = padded[f, l, pl.ds(rows + TILE, REACH), :]


def second_kernel(
    levels, rows, padded, matrix, geo, kap, full, start, below, above, both, low, high, dlon, elon
):
    longitude_slopes(levels, rows, padded, matrix, dlon, elon)

    def store(f, l, r0, tendency):
        at = pl.ds(r0, TILE)
        both[f, l, at, :] = (0.5 * time_step) * (full[f, l, at, :] + tendency)

    interior(levels, rows, padded, dlon, elon, geo, kap, store)
    tail = FIELDS * REACH * rows
    odd, mirror = mirrored()

    def body(t, carry):
        r0 = pl.multiple_of(t * TILE, TILE)
        for halo_ref, out, at, up in ((below, low, 0, True), (above, high, levels - REACH, False)):
            beyond = raw_tile(halo_ref, rows, r0, odd, mirror)
            mine = [
                [start[f, at + a, pl.ds(r0 + TILE, TILE), :] for a in range(REACH)] for f in range(FIELDS)
            ]
            kappas = [
                halo_ref[pl.ds(tail + jnp.where(odd == 1, REACH - 1 - a, a), 1), :] for a in range(REACH)
            ]
            there = time_step * halo_ref[pl.ds(tail + REACH, 1), :]
            extra = across_level(beyond[3], beyond[4], mine, kappas, up)
            for f in range(FIELDS):
                for a in range(REACH):
                    out[pl.ds((f * REACH + a) * rows + r0, TILE), :] = there * extra[f][a]
        return carry

    lax.fori_loop(0, rows // TILE, body, 0)


def second_halo_kernel(
    levels, rows, given, padded, polar, left, right, halo1, halo2, geo, kap, both, d1, d2, caps
):
    def store(f, l, r0, value, extra):
        at = pl.ds(r0, TILE)
        both[f, l, at, :] = given[f, l, at, :] + (0.5 * time_step) * extra

    add_halo(levels, rows, padded, polar, left, right, halo1, halo2, geo, kap, d1, d2, caps, store)


def last_kernel(levels, rows, padded, both, below, above, low, high, kappa, out):
    odd, mirror = mirrored()

    def body(t, carry):
        r0 = pl.multiple_of(t * TILE, TILE)
        for halo_ref, more_ref, at, up in ((below, low, 0, False), (above, high, levels - REACH, True)):
            halo = halo_tile(halo_ref, rows, r0)
            more = own_tile(more_ref, rows, r0)
            halo = [[halo[f][b] + more[f][b] for b in range(REACH)] for f in range(FIELDS)]
            wind = [padded[3, at + a, pl.ds(r0 + TILE, TILE), :] for a in range(REACH)]
            temper = [padded[4, at + a, pl.ds(r0 + TILE, TILE), :] for a in range(REACH)]
            extra = across_level(wind, temper, halo, [kappa[at + a] for a in range(REACH)], up)
            for f in range(FIELDS):
                for a in range(REACH):
                    old = both[f, at + a, pl.ds(r0, TILE), :]
                    new = old + (0.5 * time_step) * extra[f][a]
                    if f == 3:
                        new = mirror * new
                    real = jnp.where(odd == 1, levels - 1 - at - a, at + a)
                    out[f, real, pl.ds(r0, TILE), :] = new
        return carry

    lax.fori_loop(0, rows // TILE, body, 0)


def on_device(state, outer_rows, kappa):
    levels, rows, width = state.shape[1:]
    ring, depth = lax.axis_size("lon"), lax.axis_size("rad")
    assert ring % 4 == 0
    assert width == LANES and levels >= 2 * REACH and GROUPS % levels == 0
    assert rows % (TILE * (GROUPS // levels)) == 0
    matrices = stencil_matrices(width)
    geo = geometry(rows, width * ring, width)
    halo_rows = FIELDS * REACH * rows
    packs = FIELDS * levels * rows // GROUPS
    pad_shape = (FIELDS, levels, rows + 2 * TILE, width)
    full_shape = (FIELDS, levels, rows, width)

    def call(kernel, out_shape, in_specs, args, scratch=(), aliases=None, cost=1.0, name=None):
        spaces = {id(VMEM): pltpu.VMEM, id(HBM): pltpu.HBM}
        args = [pltpu.with_memory_space_constraint(x, spaces[id(s)]) for s, x in zip(in_specs, args)]
        return pl.pallas_call(
            functools.partial(kernel, levels, rows),
            out_shape=out_shape,
            in_specs=list(in_specs),
            out_specs=jax.tree.map(lambda _: VMEM, out_shape),
            scratch_shapes=list(scratch),
            input_output_aliases=aliases or {},
            cost_estimate=pl.CostEstimate(flops=0, bytes_accessed=int(cost * 3.69e6), transcendentals=0),
            compiler_params=pltpu.CompilerParams(vmem_limit_bytes=16 * 2**20),
            name=name,
        )(*args)

    east = [(i, (i + 1) % ring) for i in range(ring)]
    west = [(b, a) for a, b in east]
    half = [(i, (i + ring // 2) % ring) for i in range(ring)]
    def swaps(first):
        pairs = [
            (lon * depth + i, lon * depth + i + 1)
            for lon in range(ring)
            for i in range((lon + first) % 2, depth - 1, 2)
        ]
        return pairs + [(b, a) for a, b in pairs]

    swap_high, swap_low = swaps(0), swaps(1)

    def around(edge, polar):
        left = lax.ppermute(edge, "lon", east)
        right = lax.ppermute(edge, "lon", west)
        return left, right, lax.ppermute(polar, "lon", half)

    padded, low, high, edge, polar, kap, matrix, geo = call(
        edges_kernel,
        [
            in_vmem(*pad_shape),
            in_vmem(halo_rows + TILE, width),
            in_vmem(halo_rows + TILE, width),
            in_vmem(packs, width),
            in_vmem(FIELDS * levels * REACH, width),
            in_vmem(levels, TILE, width),
            pltpu.VMEM(matrices[0].shape, matrices[0].dtype),
            in_vmem(*geo.shape),
        ],
        (HBM,) * 5,
        (state.reshape(-1, width), outer_rows, kappa, matrices[0], geo),
        scratch=(
            in_vmem(FIELDS * levels * rows, width),
            in_vmem(*outer_rows.shape),
            pltpu.SMEM(kappa.shape, jnp.float32),
            pltpu.SemaphoreType.DMA((3 * FIELDS + 4,)),
        ),
        name="edges",
    )
    below = lax.ppermute(low, ("lon", "rad"), swap_low)
    above = lax.ppermute(high, ("lon", "rad"), swap_high)
    left, right, beyond = around(edge, polar)
    lon_scratch = (in_vmem(*full_shape), in_vmem(*full_shape[1:]))
    halo_scratch = (
        in_vmem(packs, GROUPS * width),
        in_vmem(packs // FIELDS, GROUPS * width),
        in_vmem(FIELDS, levels, 2 * TILE, width),
    )
    side = in_vmem(halo_rows, width)
    rate, halo1, halo2 = call(
        first_kernel,
        [in_vmem(*full_shape), *(pltpu.VMEM(m.shape, m.dtype) for m in matrices[1:])],
        (VMEM,) * 4 + (HBM,) * 2,
        (padded, matrix, geo, kap, *matrices[1:]),
        scratch=(*lon_scratch, pltpu.SemaphoreType.DMA((2,))),
        cost=2.0,
        name="first",
    )
    rate, low, high = call(
        first_halo_kernel,
        [in_vmem(*full_shape), side, side],
        (VMEM,) * 9,
        (rate, padded, beyond, left, right, halo1, halo2, geo, kap),
        scratch=halo_scratch,
        aliases={0: 0},
        name="first_halo",
    )
    below2 = lax.ppermute(low, ("lon", "rad"), swap_low)
    above2 = lax.ppermute(high, ("lon", "rad"), swap_high)
    full, ahead, edge, polar = call(
        section_kernel,
        [
            in_vmem(*full_shape),
            in_vmem(*pad_shape),
            in_vmem(packs, width),
            in_vmem(FIELDS * levels * REACH, width),
        ],
        (VMEM,) * 5,
        (padded, rate, below, above, kap),
        name="section",
    )
    left, right, beyond = around(edge, polar)
    both, low, high = call(
        second_kernel,
        [in_vmem(*full_shape), side, side],
        (VMEM,) * 8,
        (ahead, matrix, geo, kap, full, padded, below, above),
        scratch=lon_scratch,
        cost=2.5,
        name="second",
    )
    both = call(
        second_halo_kernel,
        in_vmem(*full_shape),
        (VMEM,) * 9,
        (both, ahead, beyond, left, right, halo1, halo2, geo, kap),
        scratch=halo_scratch,
        aliases={0: 0},
        name="second_halo",
    )
    return call(
        last_kernel,
        jax.ShapeDtypeStruct(full_shape, jnp.float32),
        (VMEM,) * 7,
        (ahead, both, below2, above2, low, high, kap),
        name="last",
    )


def solution(mesh):
    placed = (P(None, "rad", None, "lon"), P(None, "rad", None, "lon"), P("rad"))
    return jax.shard_map(
        on_device,
        mesh=mesh,
        in_specs=placed,
        out_specs=P(None, "rad", None, "lon"),
        check_vma=False,
    )
```

```python
import functools
import math

import jax
import jax.numpy as jnp
import numpy as np
from jax import lax
from jax.experimental import pallas as pl
from jax.experimental.pallas import tpu as pltpu
from jax.sharding import PartitionSpec as P

first_coeffs = (0.8, -0.2, 4.0 / 105.0, -1.0 / 280.0)
second_coeffs = (-205.0 / 72.0, 1.6, -0.2, 8.0 / 315.0, -1.0 / 560.0)
time_step = 0.002
gamma_less_one = 0.4
radial_ratio = 3.0
FIELDS = 5
REACH = 4
TILE = 8
LANES = 128
GROUPS = LANES // (2 * REACH)
signs = (1.0, -1.0, -1.0, 1.0, 1.0)
first_whole = (672.0, -168.0, 32.0, -3.0)
second_whole = (8064.0, -1008.0, 128.0, -9.0)

level_first = tuple(radial_ratio * c for c in first_coeffs)
level_second = tuple(radial_ratio * radial_ratio * c for c in second_coeffs)

VMEM = pl.BlockSpec(memory_space=pltpu.VMEM)
HBM = pl.BlockSpec(memory_space=pltpu.HBM)


def in_vmem(*shape):
    return pltpu.VMEM(shape, jnp.float32)


def stencil_matrices(width):
    own = np.zeros((width, 2 * width), np.float32)
    first = np.zeros((width, GROUPS * width), np.float32)
    second = np.zeros((width, GROUPS * width), np.float32)
    for out in range(width):
        for k in range(1, REACH + 1):
            for sign in (1, -1):
                at = out + sign * k
                if 0 <= at < width:
                    own[at, out] = sign * first_whole[k - 1]
                    own[at, width + out] = second_whole[k - 1]
                    continue
                row = REACH + at if at < 0 else REACH + at - width
                for g in range(GROUPS):
                    first[2 * REACH * g + row, g * width + out] = sign * first_whole[k - 1]
                    second[2 * REACH * g + row, g * width + out] = second_whole[k - 1]
    return tuple(jnp.asarray(m, jnp.bfloat16) for m in (own, first, second))


def geometry(rows, nlon, width):
    theta = (np.arange(rows) + 0.5) * (2.0 * math.pi / nlon)
    metric = 1.0 / np.sin(theta)
    table = np.stack([metric / 840.0, metric * metric / 5040.0, np.cos(theta) * metric])
    return jnp.asarray(np.broadcast_to(table[:, :, None], (3, rows, width)), jnp.float32)


def packed(tiles, lane):
    total = None
    for g, tile in enumerate(tiles):
        moved = pltpu.roll(tile, (REACH + 2 * REACH * g) % LANES, 1)
        if total is None:
            total = moved
        else:
            total = jnp.where(lane >= 2 * REACH * g, moved, total)
    return total


def across_level(center_wind, center_temper, halo, kappa, above):
    out = [[None] * REACH for _ in range(FIELDS)]
    for a in range(REACH):
        slopes = []
        for f in range(FIELDS):
            total = None
            for b in range(REACH):
                k = b + REACH - a if above else a + REACH - b
                if 1 <= k <= REACH:
                    c = level_first[k - 1] if above else -level_first[k - 1]
                    term = c * halo[f][b]
                    total = term if total is None else total + term
            slopes.append(total)
        curve = None
        for b in range(REACH):
            k = b + REACH - a if above else a + REACH - b
            if 1 <= k <= REACH:
                term = level_second[k] * halo[4][b]
                curve = term if curve is None else curve + term
        wind, temper = center_wind[a], center_temper[a]
        out[0][a] = -wind * slopes[0] - slopes[3]
        out[1][a] = -wind * slopes[1]
        out[2][a] = -wind * slopes[2]
        out[3][a] = -wind * slopes[3] - temper * slopes[0] - slopes[4]
        out[4][a] = -wind * slopes[4] - (gamma_less_one * temper) * slopes[3] + kappa[a] * curve
    return out


def edges_kernel(
    levels, rows, state, outer, kappa, matrix_in, geo_in,
    padded, low, high, edge, polar, kap, matrix, geo,
    staged, outer_staged, kappa_scalars, sems,
):
    block = REACH * rows
    odd = lax.axis_index("rad") % 2
    mirror = jnp.where(odd == 1, -1.0, 1.0).astype(jnp.float32)
    reads = [(state.at[f], staged.at[f]) for f in range(FIELDS)]
    reads += [(outer, outer_staged), (kappa, kappa_scalars), (matrix_in, matrix), (geo_in, geo)]
    copies = [pltpu.make_async_copy(*read, sems.at[i]) for i, read in enumerate(reads)]
    for copy in copies:
        copy.start()
    lane = lax.broadcasted_iota(jnp.int32, (TILE, LANES), 1)
    for f in range(FIELDS):
        copies[f].wait()
        for l in range(levels):
            whole = staged[f, jnp.where(odd == 1, levels - 1 - l, l)]
            if f == 3:
                whole = mirror * whole
            padded[f, l, pl.ds(TILE, rows), :] = whole
            padded[f, l, pl.ds(0, TILE), :] = jnp.zeros((TILE, LANES), jnp.float32)
            if l < REACH:
                low[pl.ds(f * block + l * rows, rows), :] = whole
            if l >= levels - REACH:
                high[pl.ds(f * block + (l - levels + REACH) * rows, rows), :] = whole
        pack_edges(f, levels, rows, padded, edge, polar, lane)
    for copy in copies[FIELDS:]:
        copy.wait()
    for l in range(levels):
        real = jnp.where(odd == 1, levels - 1 - l, l)
        value = kappa_scalars[real]
        kap[l] = jnp.full((TILE, LANES), value, jnp.float32)
        if l < REACH:
            low[pl.ds(FIELDS * block + l, 1), :] = jnp.full((1, LANES), value, jnp.float32)
        if l >= levels - REACH:
            high[pl.ds(FIELDS * block + l - levels + REACH, 1), :] = jnp.full((1, LANES), value, jnp.float32)
        for f in range(FIELDS):
            beyond = outer_staged[f, real]
            padded[f, l, pl.ds(TILE + rows, REACH), :] = mirror * beyond if f == 3 else beyond
    low[pl.ds(FIELDS * block + REACH, REACH), :] = jnp.ones((REACH, LANES), jnp.float32)
    high[pl.ds(FIELDS * block + REACH, REACH), :] = jnp.ones((REACH, LANES), jnp.float32)


def pack_edges(f, levels, rows, padded, edge, polar, lane):
    per = GROUPS // levels
    for j in range(rows // TILE // per):
        tiles = [
            padded[f, l, pl.ds(TILE + (j * per + u) * TILE, TILE), :]
            for u in range(per)
            for l in range(levels)
        ]
        at = (f * (rows // TILE // per) + j) * TILE
        edge[pl.ds(at, TILE), :] = packed(tiles, lane)
    for l in range(levels):
        for i in range(REACH):
            row = padded[f, l, pl.ds(TILE + REACH - 1 - i, 1), :]
            polar[pl.ds((f * levels + l) * REACH + i, 1), :] = signs[f] * row


def pieces_of(x):
    out = []
    for piece in range(3):
        out.append(x.astype(jnp.bfloat16))
        if piece < 2:
            x = x - out[-1].astype(jnp.float32)
    return out


def times_whole(pieces, m):
    total = None
    for piece in pieces:
        term = jnp.dot(piece, m, preferred_element_type=jnp.float32)
        total = term if total is None else total + term
    return total


def longitude_slopes(levels, rows, padded, matrix, dlon, elon):
    for f in range(FIELDS):
        x = padded[f, :, pl.ds(TILE, rows), :].reshape(levels * rows, LANES)
        total = times_whole(pieces_of(x), matrix[:, pl.ds(0, 2 * LANES if f == 4 else LANES)])
        dlon[f] = total[:, :LANES].reshape(levels, rows, LANES)
        if f == 4:
            elon[...] = total[:, LANES:].reshape(levels, rows, LANES)


def add_halo(levels, rows, padded, polar, left, right, halo1, halo2, geo, kap, d1, d2, caps, store):
    lane = lax.broadcasted_iota(jnp.int32, left.shape, 1)
    both = jnp.where((lane % (2 * REACH)) < REACH, left[...], right[...])
    split = pieces_of(both)
    packs = rows // TILE // (GROUPS // levels)
    last = slice(4 * packs * TILE, None)
    d1[...] = times_whole(split, halo1[...])
    d2[...] = times_whole([piece[last] for piece in pieces_of(both)], halo2[...])
    for f in range(FIELDS):
        for l in range(levels):
            caps[f, l, pl.ds(TILE - REACH, REACH), :] = polar[pl.ds((f * levels + l) * REACH, REACH), :]
            caps[f, l, pl.ds(TILE, TILE), :] = jnp.zeros((TILE, LANES), jnp.float32)
    for t in range(rows // TILE):
        j, u = divmod(t, GROUPS // levels)
        here = pl.ds(t * TILE, TILE)
        metric, metric2 = geo[0, here, :], geo[1, here, :]
        for l in range(levels):
            columns = pl.ds((u * levels + l) * LANES, LANES)
            center = [padded[f, l, pl.ds((t + 1) * TILE, TILE), :] for f in range(FIELDS)]
            wlon, wrow, temper = center[1], center[2], center[4]
            slon = [metric * d1[pl.ds((f * packs + j) * TILE, TILE), columns] for f in range(FIELDS)]
            laplace = metric2 * d2[pl.ds(j * TILE, TILE), columns]
            extra = [-wlon * slope for slope in slon]
            extra[1] = extra[1] - temper * slon[0] - slon[4]
            spread = slon[1]
            if t == 0:
                srow = []
                for f in range(FIELDS):
                    total = None
                    for k in range(1, REACH + 1):
                        behind = caps[f, l, pl.ds(TILE - k, TILE), :]
                        term = -first_coeffs[k - 1] * behind
                        total = term if total is None else total + term
                        if f == 4:
                            laplace = laplace + second_coeffs[k] * behind
                    srow.append(total)
                extra = [e - wrow * slope for e, slope in zip(extra, srow)]
                extra[2] = extra[2] - temper * srow[0] - srow[4]
                spread = spread + srow[2]
            extra[0] = extra[0] - spread
            extra[4] = extra[4] - (gamma_less_one * temper) * spread + kap[l] * laplace
            for f in range(FIELDS):
                store(f, l, t * TILE, center[f], extra[f])


def interior(levels, rows, padded, dlon, elon, geo, kappa, store):
    def body(t, carry):
        r0 = pl.multiple_of(t * TILE, TILE)
        here = pl.ds(r0, TILE)
        metric = geo[0, here, :]
        metric2 = geo[1, here, :]
        curvature = geo[2, here, :]
        center = [[padded[f, l, pl.ds(r0 + TILE, TILE), :] for l in range(levels)] for f in range(FIELDS)]
        out = [[None] * levels for _ in range(FIELDS)]
        for l in range(levels):
            wlon, wrow, wlev, temper = (center[f][l] for f in (1, 2, 3, 4))
            slon, srow, slev = [], [], []
            for f in range(FIELDS):
                slon.append(metric * dlon[f, l, here, :])
                total = None
                for k in range(1, REACH + 1):
                    ahead = padded[f, l, pl.ds(r0 + TILE + k, TILE), :]
                    behind = padded[f, l, pl.ds(r0 + TILE - k, TILE), :]
                    term = first_coeffs[k - 1] * (ahead - behind)
                    total = term if total is None else total + term
                    if f == 4:
                        curve = second_coeffs[k] * (ahead + behind)
                        bend = curve if k == 1 else bend + curve
                srow.append(total)
                total = None
                for k in range(1, REACH + 1):
                    up = center[f][l + k] if l + k < levels else None
                    down = center[f][l - k] if l - k >= 0 else None
                    if up is not None and down is not None:
                        term = level_first[k - 1] * (up - down)
                    elif up is not None:
                        term = level_first[k - 1] * up
                    elif down is not None:
                        term = -level_first[k - 1] * down
                    else:
                        continue
                    total = term if total is None else total + term
                slev.append(total)
            lift = None
            for k in range(1, REACH + 1):
                near = [center[4][l + s * k] for s in (1, -1) if 0 <= l + s * k < levels]
                if near:
                    term = level_second[k] * (near[0] + near[1] if len(near) == 2 else near[0])
                    lift = term if lift is None else lift + term
            middle = second_coeffs[0]
            laplace = metric2 * (elon[l, here, :] + (5040.0 * middle) * temper) + bend
            laplace = laplace + (middle + level_second[0]) * temper + lift
            carried = [wlon * slon[f] + wrow * srow[f] + wlev * slev[f] for f in range(FIELDS)]
            spread = slon[1] + srow[2] + slev[3] + curvature * wrow
            out[0][l] = -carried[0] - spread
            out[1][l] = -carried[1] - temper * slon[0] - slon[4]
            out[2][l] = -carried[2] - temper * srow[0] - srow[4]
            out[3][l] = -carried[3] - temper * slev[0] - slev[4]
            out[4][l] = -carried[4] - (gamma_less_one * temper) * spread + kappa[l] * laplace
            for f in range(FIELDS):
                store(f, l, r0, out[f][l])
        return carry

    lax.fori_loop(0, rows // TILE, body, 0)


def first_kernel(
    levels, rows, padded, matrix, geo, kap, halo1_in, halo2_in, rate, halo1, halo2, dlon, elon, sems
):
    reads = ((halo1_in, halo1), (halo2_in, halo2))
    copies = [pltpu.make_async_copy(*read, sems.at[i]) for i, read in enumerate(reads)]
    for copy in copies:
        copy.start()
    longitude_slopes(levels, rows, padded, matrix, dlon, elon)

    def store(f, l, r0, tendency):
        rate[f, l, pl.ds(r0, TILE), :] = tendency

    interior(levels, rows, padded, dlon, elon, geo, kap, store)
    for copy in copies:
        copy.wait()


def first_halo_kernel(
    levels, rows, given, padded, polar, left, right, halo1, halo2, geo, kap, rate, low, high, d1, d2, caps
):
    def store(f, l, r0, value, extra):
        tendency = given[f, l, pl.ds(r0, TILE), :] + extra
        rate[f, l, pl.ds(r0, TILE), :] = tendency
        ahead = value + time_step * tendency
        if l < REACH:
            low[pl.ds((f * REACH + l) * rows + r0, TILE), :] = ahead
        if l >= levels - REACH:
            high[pl.ds((f * REACH + l - levels + REACH) * rows + r0, TILE), :] = ahead

    add_halo(levels, rows, padded, polar, left, right, halo1, halo2, geo, kap, d1, d2, caps, store)


def halo_tile(ref, rows, r0):
    out = [
        [ref[pl.ds((f * REACH + REACH - 1 - b) * rows + r0, TILE), :] for b in range(REACH)]
        for f in range(FIELDS)
    ]
    out[3] = [-v for v in out[3]]
    return out


def own_tile(ref, rows, r0):
    return [
        [ref[pl.ds((f * REACH + b) * rows + r0, TILE), :] for b in range(REACH)] for f in range(FIELDS)
    ]


def section_kernel(levels, rows, padded, rate, below, above, kappa, full, ahead, edge, polar):
    def body(t, carry):
        r0 = pl.multiple_of(t * TILE, TILE)
        for halo_ref, at, up in ((below, 0, False), (above, levels - REACH, True)):
            halo = halo_tile(halo_ref, rows, r0)
            center = [
                [padded[f, at + a, pl.ds(r0 + TILE, TILE), :] for a in range(REACH)] for f in range(FIELDS)
            ]
            extra = across_level(center[3], center[4], halo, [kappa[at + a] for a in range(REACH)], up)
            for f in range(FIELDS):
                for a in range(REACH):
                    total = rate[f, at + a, pl.ds(r0, TILE), :] + extra[f][a]
                    full[f, at + a, pl.ds(r0, TILE), :] = total
                    ahead[f, at + a, pl.ds(r0 + TILE, TILE), :] = center[f][a] + time_step * total
        return carry

    lax.fori_loop(0, rows // TILE, body, 0)
    lane = lax.broadcasted_iota(jnp.int32, (TILE, LANES), 1)
    for f in range(FIELDS):
        pack_edges(f, levels, rows, ahead, edge, polar, lane)
        for l in range(levels):
            ahead[f, l, pl.ds(0, TILE), :] = jnp.zeros((TILE, LANES), jnp.float32)
            ahead[f, l, pl.ds(rows + TILE, REACH), :] = padded[f, l, pl.ds(rows + TILE, REACH), :]


def second_kernel(
    levels, rows, padded, matrix, geo, kap, full, start, below, above, both, low, high, dlon, elon
):
    longitude_slopes(levels, rows, padded, matrix, dlon, elon)

    def store(f, l, r0, tendency):
        at = pl.ds(r0, TILE)
        both[f, l, at, :] = (0.5 * time_step) * (full[f, l, at, :] + tendency)

    interior(levels, rows, padded, dlon, elon, geo, kap, store)
    tail = FIELDS * REACH * rows

    def body(t, carry):
        r0 = pl.multiple_of(t * TILE, TILE)
        for halo_ref, out, at, up in ((below, low, 0, True), (above, high, levels - REACH, False)):
            beyond = halo_tile(halo_ref, rows, r0)
            mine = [
                [start[f, at + a, pl.ds(r0 + TILE, TILE), :] for a in range(REACH)] for f in range(FIELDS)
            ]
            kappas = [halo_ref[pl.ds(tail + REACH - 1 - a, 1), :] for a in range(REACH)]
            there = time_step * halo_ref[pl.ds(tail + REACH, 1), :]
            extra = across_level(beyond[3], beyond[4], mine, kappas, up)
            for f in range(FIELDS):
                for a in range(REACH):
                    out[pl.ds((f * REACH + a) * rows + r0, TILE), :] = there * extra[f][a]
        return carry

    lax.fori_loop(0, rows // TILE, body, 0)


def second_halo_kernel(
    levels, rows, given, padded, polar, left, right, halo1, halo2, geo, kap, both, d1, d2, caps
):
    def store(f, l, r0, value, extra):
        at = pl.ds(r0, TILE)
        both[f, l, at, :] = given[f, l, at, :] + (0.5 * time_step) * extra

    add_halo(levels, rows, padded, polar, left, right, halo1, halo2, geo, kap, d1, d2, caps, store)


def last_kernel(at, up, levels, rows, *refs):
    padded, both, sent, more, kap = refs[:5]
    out, staged, sems = refs[-3:]
    odd = lax.axis_index("rad") % 2
    mirror = jnp.where(odd == 1, -1.0, 1.0).astype(jnp.float32)
    real = jnp.where(odd == 1, levels - at - REACH, at)
    copies = []
    for t in range(rows // TILE):
        here = pl.ds(t * TILE, TILE)
        halo = halo_tile(sent, rows, t * TILE)
        there = own_tile(more, rows, t * TILE)
        halo = [[halo[f][b] + there[f][b] for b in range(REACH)] for f in range(FIELDS)]
        wind = [padded[3, at + a, pl.ds((t + 1) * TILE, TILE), :] for a in range(REACH)]
        temper = [padded[4, at + a, pl.ds((t + 1) * TILE, TILE), :] for a in range(REACH)]
        extra = across_level(wind, temper, halo, [kap[at + a] for a in range(REACH)], up)
        for f in range(FIELDS):
            for a in range(REACH):
                new = both[f, at + a, here, :] + (0.5 * time_step) * extra[f][a]
                staged[f, jnp.where(odd == 1, REACH - 1 - a, a), here, :] = mirror * new if f == 3 else new
        target = out.at[:, pl.ds(real, REACH), here]
        copies.append(pltpu.make_async_copy(staged.at[:, :, here], target, sems.at[t]))
        copies[-1].start()
    for copy in copies:
        copy.wait()


def on_device(state, outer_rows, kappa):
    levels, rows, width = state.shape[1:]
    ring, depth = lax.axis_size("lon"), lax.axis_size("rad")
    assert width == LANES and levels >= 2 * REACH and GROUPS % levels == 0
    assert rows % (TILE * (GROUPS // levels)) == 0
    matrices = stencil_matrices(width)
    geo = geometry(rows, width * ring, width)
    halo_rows = FIELDS * REACH * rows
    packs = FIELDS * levels * rows // GROUPS
    pad_shape = (FIELDS, levels, rows + 2 * TILE, width)
    full_shape = (FIELDS, levels, rows, width)

    def call(kernel, out_shape, in_specs, args, scratch=(), aliases=None, cost=1.0, name=None):
        spaces = {id(VMEM): pltpu.VMEM, id(HBM): pltpu.HBM}
        args = [pltpu.with_memory_space_constraint(x, spaces[id(s)]) for s, x in zip(in_specs, args)]
        return pl.pallas_call(
            functools.partial(kernel, levels, rows),
            out_shape=out_shape,
            in_specs=list(in_specs),
            out_specs=jax.tree.map(lambda o: HBM if o.memory_space is pltpu.HBM else VMEM, out_shape),
            scratch_shapes=list(scratch),
            input_output_aliases=aliases or {},
            cost_estimate=pl.CostEstimate(flops=0, bytes_accessed=int(cost * 3.69e6), transcendentals=0),
            compiler_params=pltpu.CompilerParams(vmem_limit_bytes=16 * 2**20),
            name=name,
        )(*args)

    east = [(i, (i + 1) % ring) for i in range(ring)]
    west = [(b, a) for a, b in east]
    half = [(i, (i + ring // 2) % ring) for i in range(ring)]
    swap_high = [p for i in range(0, depth - 1, 2) for p in ((i, i + 1), (i + 1, i))]
    swap_low = [p for i in range(1, depth - 1, 2) for p in ((i, i + 1), (i + 1, i))]

    def around(edge, polar):
        left = lax.ppermute(edge, "lon", east)
        right = lax.ppermute(edge, "lon", west)
        return left, right, lax.ppermute(polar, "lon", half)

    padded, low, high, edge, polar, kap, matrix, geo = call(
        edges_kernel,
        [
            in_vmem(*pad_shape),
            in_vmem(halo_rows + TILE, width),
            in_vmem(halo_rows + TILE, width),
            in_vmem(packs, width),
            in_vmem(FIELDS * levels * REACH, width),
            in_vmem(levels, TILE, width),
            pltpu.VMEM(matrices[0].shape, matrices[0].dtype),
            in_vmem(*geo.shape),
        ],
        (HBM,) * 5,
        (state, outer_rows, kappa, matrices[0], geo),
        scratch=(
            in_vmem(*full_shape),
            in_vmem(*outer_rows.shape),
            pltpu.SMEM(kappa.shape, jnp.float32),
            pltpu.SemaphoreType.DMA((FIELDS + 4,)),
        ),
        name="edges",
    )
    below = lax.ppermute(low, "rad", swap_low)
    above = lax.ppermute(high, "rad", swap_high)
    left, right, beyond = around(edge, polar)
    lon_scratch = (in_vmem(*full_shape), in_vmem(*full_shape[1:]))
    halo_scratch = (
        in_vmem(packs, GROUPS * width),
        in_vmem(packs // FIELDS, GROUPS * width),
        in_vmem(FIELDS, levels, 2 * TILE, width),
    )
    side = in_vmem(halo_rows, width)
    rate, halo1, halo2 = call(
        first_kernel,
        [in_vmem(*full_shape), *(pltpu.VMEM(m.shape, m.dtype) for m in matrices[1:])],
        (VMEM,) * 4 + (HBM,) * 2,
        (padded, matrix, geo, kap, *matrices[1:]),
        scratch=(*lon_scratch, pltpu.SemaphoreType.DMA((2,))),
        cost=2.0,
        name="first",
    )
    rate, low, high = call(
        first_halo_kernel,
        [in_vmem(*full_shape), side, side],
        (VMEM,) * 9,
        (rate, padded, beyond, left, right, halo1, halo2, geo, kap),
        scratch=halo_scratch,
        aliases={0: 0},
        name="first_halo",
    )
    below2 = lax.ppermute(low, "rad", swap_low)
    above2 = lax.ppermute(high, "rad", swap_high)
    full, ahead, edge, polar = call(
        section_kernel,
        [
            in_vmem(*full_shape),
            in_vmem(*pad_shape),
            in_vmem(packs, width),
            in_vmem(FIELDS * levels * REACH, width),
        ],
        (VMEM,) * 5,
        (padded, rate, below, above, kap),
        name="section",
    )
    left, right, beyond = around(edge, polar)
    both, low, high = call(
        second_kernel,
        [in_vmem(*full_shape), side, side],
        (VMEM,) * 8,
        (ahead, matrix, geo, kap, full, padded, below, above),
        scratch=lon_scratch,
        cost=2.5,
        name="second",
    )
    both = call(
        second_halo_kernel,
        in_vmem(*full_shape),
        (VMEM,) * 9,
        (both, ahead, beyond, left, right, halo1, halo2, geo, kap),
        scratch=halo_scratch,
        aliases={0: 0},
        name="second_halo",
    )
    last_scratch = (
        in_vmem(FIELDS, REACH, rows, width),
        pltpu.SemaphoreType.DMA((rows // TILE,)),
    )
    result = pltpu.HBM(full_shape, jnp.float32)
    out = call(
        functools.partial(last_kernel, 0, False),
        result,
        (VMEM,) * 5,
        (ahead, both, below2, low, kap),
        scratch=last_scratch,
        cost=0.5,
        name="last_low",
    )
    return call(
        functools.partial(last_kernel, levels - REACH, True),
        result,
        (VMEM,) * 5 + (HBM,),
        (ahead, both, above2, high, kap, out),
        scratch=last_scratch,
        aliases={5: 0},
        name="last_high",
    )


def solution(mesh):
    placed = (P(None, "rad", None, "lon"), P(None, "rad", None, "lon"), P("rad"))
    return jax.shard_map(
        on_device,
        mesh=mesh,
        in_specs=placed,
        out_specs=P(None, "rad", None, "lon"),
        check_vma=False,
    )
```

```python
import functools
import math

import jax
import jax.numpy as jnp
import numpy as np
from jax import lax
from jax.experimental import pallas as pl
from jax.experimental.pallas import tpu as pltpu
from jax.sharding import PartitionSpec as P

first_coeffs = (0.8, -0.2, 4.0 / 105.0, -1.0 / 280.0)
second_coeffs = (-205.0 / 72.0, 1.6, -0.2, 8.0 / 315.0, -1.0 / 560.0)
time_step = 0.002
gamma_less_one = 0.4
radial_ratio = 3.0
FIELDS = 5
REACH = 4
TILE = 8
LANES = 128
GROUPS = LANES // (2 * REACH)
signs = (1.0, -1.0, -1.0, 1.0, 1.0)
first_whole = (672.0, -168.0, 32.0, -3.0)
second_whole = (8064.0, -1008.0, 128.0, -9.0)

level_first = tuple(radial_ratio * c for c in first_coeffs)
level_second = tuple(radial_ratio * radial_ratio * c for c in second_coeffs)

VMEM = pl.BlockSpec(memory_space=pltpu.VMEM)
HBM = pl.BlockSpec(memory_space=pltpu.HBM)


def in_vmem(*shape):
    return pltpu.VMEM(shape, jnp.float32)


def stencil_matrix(width):
    matrix = np.zeros((width, 2 * width), np.float32)
    for out in range(width):
        for k in range(1, REACH + 1):
            for sign in (1, -1):
                if 0 <= out + sign * k < width:
                    matrix[out + sign * k, out] = sign * first_whole[k - 1]
                    matrix[out + sign * k, width + out] = second_whole[k - 1]
    return jnp.asarray(matrix, jnp.bfloat16)


def geometry(rows, nlon, width):
    theta = (np.arange(rows) + 0.5) * (2.0 * math.pi / nlon)
    metric = 1.0 / np.sin(theta)
    table = np.stack([metric / 840.0, metric * metric / 5040.0, np.cos(theta) * metric])
    return jnp.asarray(np.broadcast_to(table[:, :, None], (3, rows, width)), jnp.float32)


def packed(tiles, lane):
    total = None
    for g, tile in enumerate(tiles):
        moved = pltpu.roll(tile, (REACH + 2 * REACH * g) % LANES, 1)
        if total is None:
            total = moved
        else:
            total = jnp.where(lane >= 2 * REACH * g, moved, total)
    return total


def across_level(center_wind, center_temper, halo, kappa, above):
    out = [[None] * REACH for _ in range(FIELDS)]
    for a in range(REACH):
        slopes = []
        for f in range(FIELDS):
            total = None
            for b in range(REACH):
                k = b + REACH - a if above else a + REACH - b
                if 1 <= k <= REACH:
                    c = level_first[k - 1] if above else -level_first[k - 1]
                    term = c * halo[f][b]
                    total = term if total is None else total + term
            slopes.append(total)
        curve = None
        for b in range(REACH):
            k = b + REACH - a if above else a + REACH - b
            if 1 <= k <= REACH:
                term = level_second[k] * halo[4][b]
                curve = term if curve is None else curve + term
        wind, temper = center_wind[a], center_temper[a]
        out[0][a] = -wind * slopes[0] - slopes[3]
        out[1][a] = -wind * slopes[1]
        out[2][a] = -wind * slopes[2]
        out[3][a] = -wind * slopes[3] - temper * slopes[0] - slopes[4]
        out[4][a] = -wind * slopes[4] - (gamma_less_one * temper) * slopes[3] + kappa[a] * curve
    return out


def edges_kernel(
    levels, rows, state, outer_rows, kappa, matrix_in, geo_in,
    staged, beyond, low, high, inner, outer, polar, kap, matrix, geo,
    kappa_scalars, sems,
):
    block = REACH * rows
    odd, mirror = mirrored()
    reads = [(state.at[f], staged.at[f]) for f in range(FIELDS)]
    reads += [(kappa, kappa_scalars), (outer_rows, beyond), (matrix_in, matrix), (geo_in, geo)]
    copies = [pltpu.make_async_copy(*read, sems.at[i]) for i, read in enumerate(reads)]
    for copy in copies:
        copy.start()
    packs = []
    for f in range(FIELDS):
        copies[f].wait()
        real = [jnp.where(odd == 1, levels - 1 - l, l) for l in range(levels)]
        tiles = []
        for l in range(levels):
            whole = staged[f, real[l]]
            if f == 3:
                whole = mirror * whole
            if l < REACH:
                low[pl.ds(f * block + l * rows, rows), :] = whole
            if l >= levels - REACH:
                high[pl.ds(f * block + (l - levels + REACH) * rows, rows), :] = whole
            tiles.append([whole[t * TILE : (t + 1) * TILE] for t in range(rows // TILE)])
            polar[pl.ds((f * levels + l) * REACH, REACH), :] = whole[:REACH]
        packs += packed(levels, rows, tiles)
    store_packs(packs, inner, outer)
    copies[FIELDS].wait()
    for l in range(levels):
        value = kappa_scalars[jnp.where(odd == 1, levels - 1 - l, l)]
        kap[l] = jnp.full((TILE, LANES), value, jnp.float32)
        if l < REACH:
            low[pl.ds(FIELDS * block + l, 1), :] = jnp.full((1, LANES), value, jnp.float32)
        if l >= levels - REACH:
            high[pl.ds(FIELDS * block + l - levels + REACH, 1), :] = jnp.full((1, LANES), value, jnp.float32)
    low[pl.ds(FIELDS * block + REACH, REACH), :] = jnp.ones((REACH, LANES), jnp.float32)
    high[pl.ds(FIELDS * block + REACH, REACH), :] = jnp.ones((REACH, LANES), jnp.float32)
    for copy in copies[FIELDS + 1 :]:
        copy.wait()


def mirrored():
    odd = lax.axis_index("rad") % 2
    return odd, jnp.where(odd == 1, -1.0, 1.0).astype(jnp.float32)


def lanes():
    return lax.broadcasted_iota(jnp.int32, (TILE, LANES), 1)


def packed(levels, rows, tiles):
    per = GROUPS // levels
    out = []
    for j in range(rows // TILE // per):
        total = None
        for g in range(GROUPS):
            moved = pltpu.roll(tiles[g % levels][j * per + g // levels], (REACH + 2 * REACH * g) % LANES, 1)
            total = moved if total is None else jnp.where(lanes() >= 2 * REACH * g, moved, total)
        out.append(total)
    return out


def store_packs(packs, inner, outer):
    first_half = lanes() % (2 * REACH) < REACH
    odd = lax.axis_index("lon") % 2 == 1
    for i in range(0, len(packs), 2):
        a, b = packs[i], packs[min(i + 1, len(packs) - 1)]
        at = pl.ds(i // 2 * TILE, TILE)
        east = jnp.where(first_half, a, pltpu.roll(b, REACH, 1))
        west = jnp.where(first_half, pltpu.roll(a, LANES - REACH, 1), b)
        inner[at, :] = jnp.where(odd, west, east)
        outer[at, :] = jnp.where(odd, east, west)


def load_packs(count, inner, outer):
    first_half = lanes() % (2 * REACH) < REACH
    odd = lax.axis_index("lon") % 2 == 1
    out = []
    for i in range(0, count, 2):
        at = pl.ds(i // 2 * TILE, TILE)
        before = jnp.where(odd, inner[at, :], outer[at, :])
        after = jnp.where(odd, outer[at, :], inner[at, :])
        out.append(jnp.where(first_half, before, pltpu.roll(after, REACH, 1)))
        out.append(jnp.where(first_half, pltpu.roll(before, LANES - REACH, 1), after))
    return out[:count]


def pieces_of(x):
    out = []
    for piece in range(3):
        out.append(x.astype(jnp.bfloat16))
        if piece < 2:
            x = x - out[-1].astype(jnp.float32)
    return out


def times_whole(pieces, m):
    total = None
    for piece in pieces:
        term = jnp.dot(piece, m, preferred_element_type=jnp.float32)
        total = term if total is None else total + term
    return total


def longitude_slopes(levels, rows, padded, matrix, dlon, elon):
    for f in range(FIELDS):
        x = padded[f, :, pl.ds(TILE, rows), :].reshape(levels * rows, LANES)
        total = times_whole(pieces_of(x), matrix[:, pl.ds(0, 2 * LANES if f == 4 else LANES)])
        dlon[f] = total[:, :LANES].reshape(levels, rows, LANES)
        if f == 4:
            elon[...] = total[:, LANES:].reshape(levels, rows, LANES)


def groups_slope(pack, coeffs, sign):
    place = lanes() % (2 * REACH)
    total = None
    for k in range(1, REACH + 1):
        ahead = pltpu.roll(pack, LANES - k, 1)
        behind = pltpu.roll(pack, k, 1)
        from_after = (place < REACH) & (place >= REACH - k)
        from_before = (place >= REACH) & (place < REACH + k)
        term = jnp.where(from_after, coeffs[k - 1] * ahead, 0.0)
        term = jnp.where(from_before, (sign * coeffs[k - 1]) * behind, term)
        total = term if total is None else total + term
    return total


def add_halo(levels, rows, padded, polar, inner, outer, geo, kap, store):
    per = GROUPS // levels
    count = rows // TILE // per
    packs = load_packs(FIELDS * count, inner, outer)
    slopes = [groups_slope(pack, first_whole, -1.0) for pack in packs]
    bends = [groups_slope(pack, second_whole, 1.0) for pack in packs[4 * count :]]
    lane = lanes()
    at_side = (lane < REACH) | (lane >= LANES - REACH)
    row = lax.broadcasted_iota(jnp.int32, (TILE, LANES), 0)

    def by_row(coeffs, m):
        total = jnp.zeros((TILE, LANES), jnp.float32)
        for k in range(m + 1, REACH + 1):
            total = jnp.where(row == k - m - 1, coeffs[k - 1], total)
        return total

    first_rows = [by_row([-c for c in first_coeffs], m) for m in range(REACH)]
    second_rows = [by_row(second_coeffs[1:], m) for m in range(REACH)]
    for t in range(rows // TILE):
        j, u = divmod(t, per)
        here = pl.ds(t * TILE, TILE)
        metric = jnp.where(at_side, geo[0, here, :], 0.0)
        metric2 = jnp.where(at_side, geo[1, here, :], 0.0)
        for l in range(levels):
            shift = (LANES - REACH - 2 * REACH * (u * levels + l)) % LANES
            center = [padded[f, l, pl.ds((t + 1) * TILE, TILE), :] for f in range(FIELDS)]
            wlon, wrow, temper = center[1], center[2], center[4]
            slon = [metric * pltpu.roll(slopes[f * count + j], shift, 1) for f in range(FIELDS)]
            laplace = metric2 * pltpu.roll(bends[j], shift, 1)
            extra = [-wlon * slope for slope in slon]
            extra[1] = extra[1] - temper * slon[0] - slon[4]
            spread = slon[1]
            if t == 0:
                srow = []
                for f in range(FIELDS):
                    total = None
                    for m in range(REACH):
                        across = signs[f] * polar[pl.ds((f * levels + l) * REACH + m, 1), :]
                        term = first_rows[m] * across
                        total = term if total is None else total + term
                        if f == 4:
                            laplace = laplace + second_rows[m] * across
                    srow.append(total)
                extra = [e - wrow * slope for e, slope in zip(extra, srow)]
                extra[2] = extra[2] - temper * srow[0] - srow[4]
                spread = spread + srow[2]
            extra[0] = extra[0] - spread
            extra[4] = extra[4] - (gamma_less_one * temper) * spread + kap[l] * laplace
            for f in range(FIELDS):
                store(f, l, t * TILE, center[f], extra[f])


def interior(levels, rows, padded, dlon, elon, geo, kappa, store):
    def body(t, carry):
        r0 = pl.multiple_of(t * TILE, TILE)
        here = pl.ds(r0, TILE)
        metric = geo[0, here, :]
        metric2 = geo[1, here, :]
        curvature = geo[2, here, :]
        center = [[padded[f, l, pl.ds(r0 + TILE, TILE), :] for l in range(levels)] for f in range(FIELDS)]
        out = [[None] * levels for _ in range(FIELDS)]
        for l in range(levels):
            wlon, wrow, wlev, temper = (center[f][l] for f in (1, 2, 3, 4))
            slon, srow, slev = [], [], []
            for f in range(FIELDS):
                slon.append(metric * dlon[f, l, here, :])
                total = None
                for k in range(1, REACH + 1):
                    ahead = padded[f, l, pl.ds(r0 + TILE + k, TILE), :]
                    behind = padded[f, l, pl.ds(r0 + TILE - k, TILE), :]
                    term = first_coeffs[k - 1] * (ahead - behind)
                    total = term if total is None else total + term
                    if f == 4:
                        curve = second_coeffs[k] * (ahead + behind)
                        bend = curve if k == 1 else bend + curve
                srow.append(total)
                total = None
                for k in range(1, REACH + 1):
                    up = center[f][l + k] if l + k < levels else None
                    down = center[f][l - k] if l - k >= 0 else None
                    if up is not None and down is not None:
                        term = level_first[k - 1] * (up - down)
                    elif up is not None:
                        term = level_first[k - 1] * up
                    elif down is not None:
                        term = -level_first[k - 1] * down
                    else:
                        continue
                    total = term if total is None else total + term
                slev.append(total)
            lift = None
            for k in range(1, REACH + 1):
                near = [center[4][l + s * k] for s in (1, -1) if 0 <= l + s * k < levels]
                if near:
                    term = level_second[k] * (near[0] + near[1] if len(near) == 2 else near[0])
                    lift = term if lift is None else lift + term
            middle = second_coeffs[0]
            laplace = metric2 * (elon[l, here, :] + (5040.0 * middle) * temper) + bend
            laplace = laplace + (middle + level_second[0]) * temper + lift
            carried = [wlon * slon[f] + wrow * srow[f] + wlev * slev[f] for f in range(FIELDS)]
            spread = slon[1] + srow[2] + slev[3] + curvature * wrow
            out[0][l] = -carried[0] - spread
            out[1][l] = -carried[1] - temper * slon[0] - slon[4]
            out[2][l] = -carried[2] - temper * srow[0] - srow[4]
            out[3][l] = -carried[3] - temper * slev[0] - slev[4]
            out[4][l] = -carried[4] - (gamma_less_one * temper) * spread + kappa[l] * laplace
            for f in range(FIELDS):
                store(f, l, r0, out[f][l])
        return carry

    lax.fori_loop(0, rows // TILE, body, 0)


def first_kernel(levels, rows, staged, beyond, matrix, geo, kap, padded, rate, dlon, elon):
    odd, mirror = mirrored()
    for f in range(FIELDS):
        for l in range(levels):
            real = jnp.where(odd == 1, levels - 1 - l, l)
            whole, after = staged[f, real], beyond[f, real]
            if f == 3:
                whole, after = mirror * whole, mirror * after
            padded[f, l, pl.ds(0, TILE), :] = jnp.zeros((TILE, LANES), jnp.float32)
            padded[f, l, pl.ds(TILE, rows), :] = whole
            padded[f, l, pl.ds(TILE + rows, REACH), :] = after
    longitude_slopes(levels, rows, padded, matrix, dlon, elon)

    def store(f, l, r0, tendency):
        rate[f, l, pl.ds(r0, TILE), :] = tendency

    interior(levels, rows, padded, dlon, elon, geo, kap, store)


def first_halo_kernel(
    levels, rows, given, padded, polar, inner, outer, geo, kap, rate, low, high
):
    def store(f, l, r0, value, extra):
        tendency = given[f, l, pl.ds(r0, TILE), :] + extra
        rate[f, l, pl.ds(r0, TILE), :] = tendency
        ahead = value + time_step * tendency
        if l < REACH:
            low[pl.ds((f * REACH + l) * rows + r0, TILE), :] = ahead
        if l >= levels - REACH:
            high[pl.ds((f * REACH + l - levels + REACH) * rows + r0, TILE), :] = ahead

    add_halo(levels, rows, padded, polar, inner, outer, geo, kap, store)


def halo_tile(ref, rows, r0):
    out = [
        [ref[pl.ds((f * REACH + REACH - 1 - b) * rows + r0, TILE), :] for b in range(REACH)]
        for f in range(FIELDS)
    ]
    out[3] = [-v for v in out[3]]
    return out


def own_tile(ref, rows, r0):
    return [
        [ref[pl.ds((f * REACH + b) * rows + r0, TILE), :] for b in range(REACH)] for f in range(FIELDS)
    ]


def section_kernel(levels, rows, padded, rate, below, above, kappa, full, ahead, inner, outer, polar):
    def body(t, carry):
        r0 = pl.multiple_of(t * TILE, TILE)
        for halo_ref, at, up in ((below, 0, False), (above, levels - REACH, True)):
            halo = halo_tile(halo_ref, rows, r0)
            center = [
                [padded[f, at + a, pl.ds(r0 + TILE, TILE), :] for a in range(REACH)] for f in range(FIELDS)
            ]
            extra = across_level(center[3], center[4], halo, [kappa[at + a] for a in range(REACH)], up)
            for f in range(FIELDS):
                for a in range(REACH):
                    total = rate[f, at + a, pl.ds(r0, TILE), :] + extra[f][a]
                    full[f, at + a, pl.ds(r0, TILE), :] = total
                    ahead[f, at + a, pl.ds(r0 + TILE, TILE), :] = center[f][a] + time_step * total
        return carry

    lax.fori_loop(0, rows // TILE, body, 0)
    packs = []
    for f in range(FIELDS):
        tiles = [[ahead[f, l, pl.ds((t + 1) * TILE, TILE), :] for t in range(rows // TILE)] for l in range(levels)]
        packs += packed(levels, rows, tiles)
        for l in range(levels):
            polar[pl.ds((f * levels + l) * REACH, REACH), :] = ahead[f, l, pl.ds(TILE, REACH), :]
            ahead[f, l, pl.ds(0, TILE), :] = jnp.zeros((TILE, LANES), jnp.float32)
            ahead[f, l, pl.ds(rows + TILE, REACH), :] = padded[f, l, pl.ds(rows + TILE, REACH), :]
    store_packs(packs, inner, outer)


def second_kernel(
    levels, rows, padded, matrix, geo, kap, full, start, below, above, both, low, high, dlon, elon
):
    longitude_slopes(levels, rows, padded, matrix, dlon, elon)

    def store(f, l, r0, tendency):
        at = pl.ds(r0, TILE)
        both[f, l, at, :] = (0.5 * time_step) * (full[f, l, at, :] + tendency)

    interior(levels, rows, padded, dlon, elon, geo, kap, store)
    tail = FIELDS * REACH * rows

    def body(t, carry):
        r0 = pl.multiple_of(t * TILE, TILE)
        for halo_ref, out, at, up in ((below, low, 0, True), (above, high, levels - REACH, False)):
            beyond = halo_tile(halo_ref, rows, r0)
            mine = [
                [start[f, at + a, pl.ds(r0 + TILE, TILE), :] for a in range(REACH)] for f in range(FIELDS)
            ]
            kappas = [halo_ref[pl.ds(tail + REACH - 1 - a, 1), :] for a in range(REACH)]
            there = time_step * halo_ref[pl.ds(tail + REACH, 1), :]
            extra = across_level(beyond[3], beyond[4], mine, kappas, up)
            for f in range(FIELDS):
                for a in range(REACH):
                    out[pl.ds((f * REACH + a) * rows + r0, TILE), :] = there * extra[f][a]
        return carry

    lax.fori_loop(0, rows // TILE, body, 0)


def second_halo_kernel(
    levels, rows, given, padded, polar, inner, outer, geo, kap, both
):
    def store(f, l, r0, value, extra):
        at = pl.ds(r0, TILE)
        both[f, l, at, :] = given[f, l, at, :] + (0.5 * time_step) * extra

    add_halo(levels, rows, padded, polar, inner, outer, geo, kap, store)


def last_kernel(at, up, levels, rows, *refs):
    padded, both, sent, more, kap = refs[:5]
    out, staged, sems = refs[-3:]
    odd, mirror = mirrored()
    real = jnp.where(odd == 1, levels - at - REACH, at)
    copies = []
    for t in range(rows // TILE):
        here = pl.ds(t * TILE, TILE)
        halo = halo_tile(sent, rows, t * TILE)
        there = own_tile(more, rows, t * TILE)
        halo = [[halo[f][b] + there[f][b] for b in range(REACH)] for f in range(FIELDS)]
        wind = [padded[3, at + a, pl.ds((t + 1) * TILE, TILE), :] for a in range(REACH)]
        temper = [padded[4, at + a, pl.ds((t + 1) * TILE, TILE), :] for a in range(REACH)]
        extra = across_level(wind, temper, halo, [kap[at + a] for a in range(REACH)], up)
        for f in range(FIELDS):
            for a in range(REACH):
                new = both[f, at + a, here, :] + (0.5 * time_step) * extra[f][a]
                staged[f, jnp.where(odd == 1, REACH - 1 - a, a), here, :] = mirror * new if f == 3 else new
        target = out.at[:, pl.ds(real, REACH), here]
        copies.append(pltpu.make_async_copy(staged.at[:, :, here], target, sems.at[t]))
        copies[-1].start()
    for copy in copies:
        copy.wait()


def on_device(state, outer_rows, kappa):
    levels, rows, width = state.shape[1:]
    ring, depth = lax.axis_size("lon"), lax.axis_size("rad")
    assert ring % 4 == 0 and width == LANES and levels >= 2 * REACH and GROUPS % levels == 0
    assert rows % (TILE * (GROUPS // levels)) == 0
    matrix = stencil_matrix(width)
    geo = geometry(rows, width * ring, width)
    halo_rows = FIELDS * REACH * rows
    packs = -(-(FIELDS * levels * rows // TILE // GROUPS) // 2) * TILE
    pad_shape = (FIELDS, levels, rows + 2 * TILE, width)
    full_shape = (FIELDS, levels, rows, width)

    def call(kernel, out_shape, in_specs, args, scratch=(), aliases=None, cost=1.0, name=None):
        spaces = {id(VMEM): pltpu.VMEM, id(HBM): pltpu.HBM}
        args = [pltpu.with_memory_space_constraint(x, spaces[id(s)]) for s, x in zip(in_specs, args)]
        return pl.pallas_call(
            functools.partial(kernel, levels, rows),
            out_shape=out_shape,
            in_specs=list(in_specs),
            out_specs=jax.tree.map(lambda o: HBM if o.memory_space is pltpu.HBM else VMEM, out_shape),
            scratch_shapes=list(scratch),
            input_output_aliases=aliases or {},
            cost_estimate=pl.CostEstimate(flops=0, bytes_accessed=int(cost * 3.69e6), transcendentals=0),
            compiler_params=pltpu.CompilerParams(vmem_limit_bytes=16 * 2**20),
            name=name,
        )(*args)

    pairs = [(i, i + 1) for i in range(0, ring, 2)]
    swap_inner = pairs + [(b, a) for a, b in pairs]
    pairs = [(i, (i + 1) % ring) for i in range(1, ring, 2)]
    swap_outer = pairs + [(b, a) for a, b in pairs]
    half = [(i, (i + ring // 2) % ring) for i in range(ring)]
    swap_high = [p for i in range(0, depth - 1, 2) for p in ((i, i + 1), (i + 1, i))]
    swap_low = [p for i in range(1, depth - 1, 2) for p in ((i, i + 1), (i + 1, i))]

    def around(inner, outer, polar):
        inner = lax.ppermute(inner, "lon", swap_inner)
        outer = lax.ppermute(outer, "lon", swap_outer)
        return inner, outer, lax.ppermute(polar, "lon", half)

    edge_shapes = [in_vmem(packs, width), in_vmem(packs, width), in_vmem(FIELDS * levels * REACH, width)]
    staged, after, low, high, *edges, kap, matrix, geo = call(
        edges_kernel,
        [
            in_vmem(*full_shape),
            in_vmem(*outer_rows.shape),
            in_vmem(halo_rows + TILE, width),
            in_vmem(halo_rows + TILE, width),
            *edge_shapes,
            in_vmem(levels, TILE, width),
            pltpu.VMEM(matrix.shape, matrix.dtype),
            in_vmem(*geo.shape),
        ],
        (HBM,) * 5,
        (state, outer_rows, kappa, matrix, geo),
        scratch=(pltpu.SMEM(kappa.shape, jnp.float32), pltpu.SemaphoreType.DMA((FIELDS + 4,))),
        name="edges",
    )
    below = lax.ppermute(low, "rad", swap_low)
    above = lax.ppermute(high, "rad", swap_high)
    inner, outer, beyond = around(*edges)
    lon_scratch = (in_vmem(*full_shape), in_vmem(*full_shape[1:]))
    side = in_vmem(halo_rows, width)
    padded, rate = call(
        first_kernel,
        [in_vmem(*pad_shape), in_vmem(*full_shape)],
        (VMEM,) * 5,
        (staged, after, matrix, geo, kap),
        scratch=lon_scratch,
        cost=2.0,
        name="first",
    )
    rate, low, high = call(
        first_halo_kernel,
        [in_vmem(*full_shape), side, side],
        (VMEM,) * 7,
        (rate, padded, beyond, inner, outer, geo, kap),
        aliases={0: 0},
        name="first_halo",
    )
    below2 = lax.ppermute(low, "rad", swap_low)
    above2 = lax.ppermute(high, "rad", swap_high)
    full, ahead, *edges = call(
        section_kernel,
        [
            in_vmem(*full_shape),
            in_vmem(*pad_shape),
            *edge_shapes,
        ],
        (VMEM,) * 5,
        (padded, rate, below, above, kap),
        name="section",
    )
    inner, outer, beyond = around(*edges)
    both, low, high = call(
        second_kernel,
        [in_vmem(*full_shape), side, side],
        (VMEM,) * 8,
        (ahead, matrix, geo, kap, full, padded, below, above),
        scratch=lon_scratch,
        cost=2.5,
        name="second",
    )
    both = call(
        second_halo_kernel,
        in_vmem(*full_shape),
        (VMEM,) * 7,
        (both, ahead, beyond, inner, outer, geo, kap),
        aliases={0: 0},
        name="second_halo",
    )
    last_scratch = (
        in_vmem(FIELDS, REACH, rows, width),
        pltpu.SemaphoreType.DMA((rows // TILE,)),
    )
    result = pltpu.HBM(full_shape, jnp.float32)
    out = call(
        functools.partial(last_kernel, 0, False),
        result,
        (VMEM,) * 5,
        (ahead, both, below2, low, kap),
        scratch=last_scratch,
        cost=0.5,
        name="last_low",
    )
    return call(
        functools.partial(last_kernel, levels - REACH, True),
        result,
        (VMEM,) * 5 + (HBM,),
        (ahead, both, above2, high, kap, out),
        scratch=last_scratch,
        aliases={5: 0},
        name="last_high",
    )


def solution(mesh):
    placed = (P(None, "rad", None, "lon"), P(None, "rad", None, "lon"), P("rad"))
    return jax.shard_map(
        on_device,
        mesh=mesh,
        in_specs=placed,
        out_specs=P(None, "rad", None, "lon"),
        check_vma=False,
    )
```

```python
import functools
import math

import jax
import jax.numpy as jnp
import numpy as np
from jax import lax
from jax.experimental import pallas as pl
from jax.experimental.pallas import tpu as pltpu
from jax.sharding import PartitionSpec as P

first_coeffs = (0.8, -0.2, 4.0 / 105.0, -1.0 / 280.0)
second_coeffs = (-205.0 / 72.0, 1.6, -0.2, 8.0 / 315.0, -1.0 / 560.0)
time_step = 0.002
gamma_less_one = 0.4
radial_ratio = 3.0
FIELDS = 5
REACH = 4
TILE = 8
LANES = 128
GROUPS = LANES // (2 * REACH)
signs = (1.0, -1.0, -1.0, 1.0, 1.0)
first_whole = (672.0, -168.0, 32.0, -3.0)
second_whole = (8064.0, -1008.0, 128.0, -9.0)

level_first = tuple(radial_ratio * c for c in first_coeffs)
level_second = tuple(radial_ratio * radial_ratio * c for c in second_coeffs)

VMEM = pl.BlockSpec(memory_space=pltpu.VMEM)
HBM = pl.BlockSpec(memory_space=pltpu.HBM)


def in_vmem(*shape):
    return pltpu.VMEM(shape, jnp.float32)


def stencil_matrix(width):
    matrix = np.zeros((width, 2 * width), np.float32)
    for out in range(width):
        for k in range(1, REACH + 1):
            for sign in (1, -1):
                if 0 <= out + sign * k < width:
                    matrix[out + sign * k, out] = sign * first_whole[k - 1]
                    matrix[out + sign * k, width + out] = second_whole[k - 1]
    return jnp.asarray(matrix, jnp.bfloat16)


def geometry(rows, nlon, width):
    theta = (np.arange(rows) + 0.5) * (2.0 * math.pi / nlon)
    metric = 1.0 / np.sin(theta)
    table = np.stack([metric / 840.0, metric * metric / 5040.0, np.cos(theta) * metric])
    return jnp.asarray(np.broadcast_to(table[:, :, None], (3, rows, width)), jnp.float32)


def packed(tiles, lane):
    total = None
    for g, tile in enumerate(tiles):
        moved = pltpu.roll(tile, (REACH + 2 * REACH * g) % LANES, 1)
        if total is None:
            total = moved
        else:
            total = jnp.where(lane >= 2 * REACH * g, moved, total)
    return total


def across_level(center_wind, center_temper, halo, kappa, above):
    out = [[None] * REACH for _ in range(FIELDS)]
    for a in range(REACH):
        slopes = []
        for f in range(FIELDS):
            total = None
            for b in range(REACH):
                k = b + REACH - a if above else a + REACH - b
                if 1 <= k <= REACH:
                    c = level_first[k - 1] if above else -level_first[k - 1]
                    term = c * halo[f][b]
                    total = term if total is None else total + term
            slopes.append(total)
        curve = None
        for b in range(REACH):
            k = b + REACH - a if above else a + REACH - b
            if 1 <= k <= REACH:
                term = level_second[k] * halo[4][b]
                curve = term if curve is None else curve + term
        wind, temper = center_wind[a], center_temper[a]
        out[0][a] = -wind * slopes[0] - slopes[3]
        out[1][a] = -wind * slopes[1]
        out[2][a] = -wind * slopes[2]
        out[3][a] = -wind * slopes[3] - temper * slopes[0] - slopes[4]
        out[4][a] = -wind * slopes[4] - (gamma_less_one * temper) * slopes[3] + kappa[a] * curve
    return out


def levels_kernel(
    levels, rows, state, outer_rows, kappa, matrix_in, geo_in,
    high, low, beyond, kap, matrix, geo, kappa_scalars, sems,
):
    block = REACH * rows
    odd, _ = mirrored()
    starts = (jnp.where(odd == 1, 0, REACH), jnp.where(odd == 1, REACH, 0))
    reads = [
        (state.at[pl.ds(pl.multiple_of((f * levels + start) * rows, TILE), block)], side.at[pl.ds(f * block, block)])
        for start, side in zip(starts, (high, low))
        for f in range(FIELDS)
    ]
    reads += [(kappa, kappa_scalars), (outer_rows, beyond), (matrix_in, matrix), (geo_in, geo)]
    copies = [pltpu.make_async_copy(*read, sems.at[i]) for i, read in enumerate(reads)]
    for copy in copies:
        copy.start()
    copies[2 * FIELDS].wait()
    for start, side in zip(starts, (high, low)):
        for i in range(REACH):
            value = jnp.full((1, LANES), kappa_scalars[start + i], jnp.float32)
            side[pl.ds(FIELDS * block + i, 1), :] = value
    for l in range(levels):
        value = kappa_scalars[jnp.where(odd == 1, levels - 1 - l, l)]
        kap[l] = jnp.full((TILE, LANES), value, jnp.float32)
    for i, copy in enumerate(copies):
        if i != 2 * FIELDS:
            copy.wait()


def own_level(high, low, rows, f, l, odd):
    i = l % REACH
    at = (f * REACH + jnp.where(odd == 1, REACH - 1 - i, i)) * rows
    return (low if l < REACH else high), pl.multiple_of(at, TILE)


def edges_kernel(levels, rows, given, high, low, inner, outer, polar):
    odd, mirror = mirrored()
    packs = []
    for f in range(FIELDS):
        tiles = []
        for l in range(levels):
            side, at = own_level(high, low, rows, f, l, odd)
            tiles.append([side[pl.ds(at + t * TILE, TILE), :] for t in range(rows // TILE)])
            cap = side[pl.ds(at, REACH), :]
            polar[pl.ds((f * levels + l) * REACH, REACH), :] = mirror * cap if f == 3 else cap
        packs += [mirror * pack if f == 3 else pack for pack in packed(levels, rows, tiles)]
    store_packs(packs, inner, outer)


def mirrored():
    odd = lax.axis_index("rad") % 2
    return odd, jnp.where(odd == 1, -1.0, 1.0).astype(jnp.float32)


def bordered(at):
    here, depth = lax.axis_index("rad"), lax.axis_size("rad")
    inside = jnp.where((here > 0) & (here < depth - 1), 1.0, 0.0)
    return inside.astype(jnp.float32) if at == 0 else jnp.float32(1.0)


def lanes():
    return lax.broadcasted_iota(jnp.int32, (TILE, LANES), 1)


def packed(levels, rows, tiles):
    per = GROUPS // levels
    out = []
    for j in range(rows // TILE // per):
        total = None
        for g in range(GROUPS):
            moved = pltpu.roll(tiles[g % levels][j * per + g // levels], (REACH + 2 * REACH * g) % LANES, 1)
            total = moved if total is None else jnp.where(lanes() >= 2 * REACH * g, moved, total)
        out.append(total)
    return out


def store_packs(packs, inner, outer):
    first_half = lanes() % (2 * REACH) < REACH
    odd = lax.axis_index("lon") % 2 == 1
    for i in range(0, len(packs), 2):
        a, b = packs[i], packs[min(i + 1, len(packs) - 1)]
        at = pl.ds(i // 2 * TILE, TILE)
        east = jnp.where(first_half, a, pltpu.roll(b, REACH, 1))
        west = jnp.where(first_half, pltpu.roll(a, LANES - REACH, 1), b)
        inner[at, :] = jnp.where(odd, west, east)
        outer[at, :] = jnp.where(odd, east, west)


def load_packs(count, inner, outer):
    first_half = lanes() % (2 * REACH) < REACH
    odd = lax.axis_index("lon") % 2 == 1
    out = []
    for i in range(0, count, 2):
        at = pl.ds(i // 2 * TILE, TILE)
        before = jnp.where(odd, inner[at, :], outer[at, :])
        after = jnp.where(odd, outer[at, :], inner[at, :])
        out.append(jnp.where(first_half, before, pltpu.roll(after, REACH, 1)))
        out.append(jnp.where(first_half, pltpu.roll(before, LANES - REACH, 1), after))
    return out[:count]


def pieces_of(x):
    out = []
    for piece in range(3):
        out.append(x.astype(jnp.bfloat16))
        if piece < 2:
            x = x - out[-1].astype(jnp.float32)
    return out


def times_whole(pieces, m):
    total = None
    for piece in pieces:
        term = jnp.dot(piece, m, preferred_element_type=jnp.float32)
        total = term if total is None else total + term
    return total


def longitude_slopes(levels, rows, padded, matrix, dlon, elon):
    for f in range(FIELDS):
        x = padded[f, :, pl.ds(TILE, rows), :].reshape(levels * rows, LANES)
        total = times_whole(pieces_of(x), matrix[:, pl.ds(0, 2 * LANES if f == 4 else LANES)])
        dlon[f] = total[:, :LANES].reshape(levels, rows, LANES)
        if f == 4:
            elon[...] = total[:, LANES:].reshape(levels, rows, LANES)


def groups_slope(pack, coeffs, sign):
    place = lanes() % (2 * REACH)
    total = None
    for k in range(1, REACH + 1):
        ahead = pltpu.roll(pack, LANES - k, 1)
        behind = pltpu.roll(pack, k, 1)
        from_after = (place < REACH) & (place >= REACH - k)
        from_before = (place >= REACH) & (place < REACH + k)
        term = jnp.where(from_after, coeffs[k - 1] * ahead, 0.0)
        term = jnp.where(from_before, (sign * coeffs[k - 1]) * behind, term)
        total = term if total is None else total + term
    return total


def add_halo(levels, rows, own, padded, polar, inner, outer, geo, kap, store):
    per = GROUPS // levels
    count = rows // TILE // per
    packs = load_packs(FIELDS * count, inner, outer)
    slopes = [groups_slope(pack, first_whole, -1.0) for pack in packs]
    bends = [groups_slope(pack, second_whole, 1.0) for pack in packs[4 * count :]]
    lane = lanes()
    at_side = (lane < REACH) | (lane >= LANES - REACH)
    row = lax.broadcasted_iota(jnp.int32, (TILE, LANES), 0)

    def by_row(coeffs, m):
        total = jnp.zeros((TILE, LANES), jnp.float32)
        for k in range(m + 1, REACH + 1):
            total = jnp.where(row == k - m - 1, coeffs[k - 1], total)
        return total

    first_rows = [by_row([-c for c in first_coeffs], m) for m in range(REACH)]
    second_rows = [by_row(second_coeffs[1:], m) for m in range(REACH)]
    for t in range(rows // TILE):
        j, u = divmod(t, per)
        here = pl.ds(t * TILE, TILE)
        metric = jnp.where(at_side, geo[0, here, :], 0.0)
        metric2 = jnp.where(at_side, geo[1, here, :], 0.0)
        for l in own:
            shift = (LANES - REACH - 2 * REACH * (u * levels + l)) % LANES
            center = [padded[f, l, pl.ds((t + 1) * TILE, TILE), :] for f in range(FIELDS)]
            wlon, wrow, temper = center[1], center[2], center[4]
            slon = [metric * pltpu.roll(slopes[f * count + j], shift, 1) for f in range(FIELDS)]
            laplace = metric2 * pltpu.roll(bends[j], shift, 1)
            extra = [-wlon * slope for slope in slon]
            extra[1] = extra[1] - temper * slon[0] - slon[4]
            spread = slon[1]
            if t == 0:
                srow = []
                for f in range(FIELDS):
                    total = None
                    for m in range(REACH):
                        across = signs[f] * polar[pl.ds((f * levels + l) * REACH + m, 1), :]
                        term = first_rows[m] * across
                        total = term if total is None else total + term
                        if f == 4:
                            laplace = laplace + second_rows[m] * across
                    srow.append(total)
                extra = [e - wrow * slope for e, slope in zip(extra, srow)]
                extra[2] = extra[2] - temper * srow[0] - srow[4]
                spread = spread + srow[2]
            extra[0] = extra[0] - spread
            extra[4] = extra[4] - (gamma_less_one * temper) * spread + kap[l] * laplace
            for f in range(FIELDS):
                store(f, l, t * TILE, center[f], extra[f])


def interior(levels, rows, padded, dlon, elon, geo, kappa, store):
    def body(t, carry):
        r0 = pl.multiple_of(t * TILE, TILE)
        here = pl.ds(r0, TILE)
        metric = geo[0, here, :]
        metric2 = geo[1, here, :]
        curvature = geo[2, here, :]
        center = [[padded[f, l, pl.ds(r0 + TILE, TILE), :] for l in range(levels)] for f in range(FIELDS)]
        out = [[None] * levels for _ in range(FIELDS)]
        for l in range(levels):
            wlon, wrow, wlev, temper = (center[f][l] for f in (1, 2, 3, 4))
            slon, srow, slev = [], [], []
            for f in range(FIELDS):
                slon.append(metric * dlon[f, l, here, :])
                total = None
                for k in range(1, REACH + 1):
                    ahead = padded[f, l, pl.ds(r0 + TILE + k, TILE), :]
                    behind = padded[f, l, pl.ds(r0 + TILE - k, TILE), :]
                    term = first_coeffs[k - 1] * (ahead - behind)
                    total = term if total is None else total + term
                    if f == 4:
                        curve = second_coeffs[k] * (ahead + behind)
                        bend = curve if k == 1 else bend + curve
                srow.append(total)
                total = None
                for k in range(1, REACH + 1):
                    up = center[f][l + k] if l + k < levels else None
                    down = center[f][l - k] if l - k >= 0 else None
                    if up is not None and down is not None:
                        term = level_first[k - 1] * (up - down)
                    elif up is not None:
                        term = level_first[k - 1] * up
                    elif down is not None:
                        term = -level_first[k - 1] * down
                    else:
                        continue
                    total = term if total is None else total + term
                slev.append(total)
            lift = None
            for k in range(1, REACH + 1):
                near = [center[4][l + s * k] for s in (1, -1) if 0 <= l + s * k < levels]
                if near:
                    term = level_second[k] * (near[0] + near[1] if len(near) == 2 else near[0])
                    lift = term if lift is None else lift + term
            middle = second_coeffs[0]
            laplace = metric2 * (elon[l, here, :] + (5040.0 * middle) * temper) + bend
            laplace = laplace + (middle + level_second[0]) * temper + lift
            carried = [wlon * slon[f] + wrow * srow[f] + wlev * slev[f] for f in range(FIELDS)]
            spread = slon[1] + srow[2] + slev[3] + curvature * wrow
            out[0][l] = -carried[0] - spread
            out[1][l] = -carried[1] - temper * slon[0] - slon[4]
            out[2][l] = -carried[2] - temper * srow[0] - srow[4]
            out[3][l] = -carried[3] - temper * slev[0] - slev[4]
            out[4][l] = -carried[4] - (gamma_less_one * temper) * spread + kappa[l] * laplace
            for f in range(FIELDS):
                store(f, l, r0, out[f][l])
        return carry

    lax.fori_loop(0, rows // TILE, body, 0)


def first_kernel(levels, rows, high, low, beyond, matrix, geo, kap, padded, rate, dlon, elon):
    odd, mirror = mirrored()
    for f in range(FIELDS):
        for l in range(levels):
            side, at = own_level(high, low, rows, f, l, odd)
            whole = side[pl.ds(at, rows), :]
            after = beyond[f, jnp.where(odd == 1, levels - 1 - l, l)]
            if f == 3:
                whole, after = mirror * whole, mirror * after
            padded[f, l, pl.ds(0, TILE), :] = jnp.zeros((TILE, LANES), jnp.float32)
            padded[f, l, pl.ds(TILE, rows), :] = whole
            padded[f, l, pl.ds(TILE + rows, REACH), :] = after
    longitude_slopes(levels, rows, padded, matrix, dlon, elon)

    def store(f, l, r0, tendency):
        rate[f, l, pl.ds(r0, TILE), :] = tendency

    interior(levels, rows, padded, dlon, elon, geo, kap, store)


def first_halo_kernel(at, levels, rows, given, padded, polar, inner, outer, geo, kap, rate, side):
    def store(f, l, r0, value, extra):
        tendency = given[f, l, pl.ds(r0, TILE), :] + extra
        rate[f, l, pl.ds(r0, TILE), :] = tendency
        side[pl.ds((f * REACH + l - at) * rows + r0, TILE), :] = value + time_step * tendency

    own = range(at, at + REACH)
    add_halo(levels, rows, own, padded, polar, inner, outer, geo, kap, store)


def raw_tile(ref, rows, r0, odd, mirror):
    out = []
    for f in range(FIELDS):
        ats = [(f * REACH + jnp.where(odd == 1, REACH - 1 - b, b)) * rows + r0 for b in range(REACH)]
        out.append([ref[pl.ds(pl.multiple_of(at, TILE), TILE), :] for at in ats])
    out[3] = [mirror * v for v in out[3]]
    return out


def halo_tile(ref, rows, r0):
    out = [
        [ref[pl.ds((f * REACH + REACH - 1 - b) * rows + r0, TILE), :] for b in range(REACH)]
        for f in range(FIELDS)
    ]
    out[3] = [-v for v in out[3]]
    return out


def own_tile(ref, rows, r0):
    return [
        [ref[pl.ds((f * REACH + b) * rows + r0, TILE), :] for b in range(REACH)] for f in range(FIELDS)
    ]


def section_side(at, up, levels, rows, padded, rate, sent, kappa, full, ahead):
    odd, mirror = mirrored()
    there = bordered(at)

    def body(t, carry):
        r0 = pl.multiple_of(t * TILE, TILE)
        here, inside = pl.ds(r0, TILE), pl.ds(r0 + TILE, TILE)
        halo = raw_tile(sent, rows, r0, odd, mirror)
        center = [[padded[f, at + a, inside, :] for a in range(REACH)] for f in range(FIELDS)]
        extra = across_level(center[3], center[4], halo, [kappa[at + a] for a in range(REACH)], up)
        for f in range(FIELDS):
            for a in range(REACH):
                more = extra[f][a] if at else there * extra[f][a]
                total = rate[f, at + a, here, :] + more
                full[f, at + a, here, :] = total
                ahead[f, at + a, inside, :] = center[f][a] + time_step * total
        return carry

    lax.fori_loop(0, rows // TILE, body, 0)
    for f in range(FIELDS):
        for l in range(at, at + REACH):
            ahead[f, l, pl.ds(0, TILE), :] = jnp.zeros((TILE, LANES), jnp.float32)
            ahead[f, l, pl.ds(rows + TILE, REACH), :] = padded[f, l, pl.ds(rows + TILE, REACH), :]


def section_high_kernel(levels, rows, padded, rate, above, kappa, full, ahead):
    section_side(levels - REACH, True, levels, rows, padded, rate, above, kappa, full, ahead)


def section_low_kernel(
    levels, rows, padded, rate, below, kappa, given1, given2, full, ahead, inner, outer, polar
):
    section_side(0, False, levels, rows, padded, rate, below, kappa, full, ahead)
    packs = []
    for f in range(FIELDS):
        tiles = [[ahead[f, l, pl.ds((t + 1) * TILE, TILE), :] for t in range(rows // TILE)] for l in range(levels)]
        packs += packed(levels, rows, tiles)
        for l in range(levels):
            polar[pl.ds((f * levels + l) * REACH, REACH), :] = ahead[f, l, pl.ds(TILE, REACH), :]
    store_packs(packs, inner, outer)


def second_kernel(
    levels, rows, padded, matrix, geo, kap, full, start, below, above, both, low, high, dlon, elon
):
    longitude_slopes(levels, rows, padded, matrix, dlon, elon)

    def store(f, l, r0, tendency):
        at = pl.ds(r0, TILE)
        both[f, l, at, :] = (0.5 * time_step) * (full[f, l, at, :] + tendency)

    interior(levels, rows, padded, dlon, elon, geo, kap, store)
    tail = FIELDS * REACH * rows
    odd, mirror = mirrored()

    def body(t, carry):
        r0 = pl.multiple_of(t * TILE, TILE)
        for halo_ref, out, at, up in ((below, low, 0, True), (above, high, levels - REACH, False)):
            beyond = raw_tile(halo_ref, rows, r0, odd, mirror)
            mine = [
                [start[f, at + a, pl.ds(r0 + TILE, TILE), :] for a in range(REACH)] for f in range(FIELDS)
            ]
            kappas = [
                halo_ref[pl.ds(tail + jnp.where(odd == 1, REACH - 1 - a, a), 1), :] for a in range(REACH)
            ]
            there = time_step * bordered(at)
            extra = across_level(beyond[3], beyond[4], mine, kappas, up)
            for f in range(FIELDS):
                for a in range(REACH):
                    out[pl.ds((f * REACH + a) * rows + r0, TILE), :] = there * extra[f][a]
        return carry

    lax.fori_loop(0, rows // TILE, body, 0)


def second_halo_kernel(
    levels, rows, given, padded, polar, inner, outer, geo, kap, both
):
    def store(f, l, r0, value, extra):
        at = pl.ds(r0, TILE)
        both[f, l, at, :] = given[f, l, at, :] + (0.5 * time_step) * extra

    add_halo(levels, rows, range(levels), padded, polar, inner, outer, geo, kap, store)


def last_kernel(at, up, levels, rows, *refs):
    padded, both, sent, more, kap = refs[:5]
    out, staged, sems = refs[-3:]
    odd, mirror = mirrored()
    scale = (0.5 * time_step) * bordered(at)
    real = jnp.where(odd == 1, levels - at - REACH, at)
    copies = []
    for t in range(rows // TILE):
        here = pl.ds(t * TILE, TILE)
        halo = halo_tile(sent, rows, t * TILE)
        there = own_tile(more, rows, t * TILE)
        halo = [[halo[f][b] + there[f][b] for b in range(REACH)] for f in range(FIELDS)]
        wind = [padded[3, at + a, pl.ds((t + 1) * TILE, TILE), :] for a in range(REACH)]
        temper = [padded[4, at + a, pl.ds((t + 1) * TILE, TILE), :] for a in range(REACH)]
        extra = across_level(wind, temper, halo, [kap[at + a] for a in range(REACH)], up)
        for f in range(FIELDS):
            for a in range(REACH):
                new = both[f, at + a, here, :] + scale * extra[f][a]
                staged[f, jnp.where(odd == 1, REACH - 1 - a, a), here, :] = mirror * new if f == 3 else new
        target = out.at[:, pl.ds(real, REACH), here]
        copies.append(pltpu.make_async_copy(staged.at[:, :, here], target, sems.at[t]))
        copies[-1].start()
    for copy in copies:
        copy.wait()


def on_device(state, outer_rows, kappa):
    levels, rows, width = state.shape[1:]
    ring, depth = lax.axis_size("lon"), lax.axis_size("rad")
    assert ring % 4 == 0 and depth % 2 == 0 and width == LANES and levels == 2 * REACH and GROUPS % levels == 0
    assert rows % (TILE * (GROUPS // levels)) == 0
    matrix = stencil_matrix(width)
    geo = geometry(rows, width * ring, width)
    halo_rows = FIELDS * REACH * rows
    packs = -(-(FIELDS * levels * rows // TILE // GROUPS) // 2) * TILE
    pad_shape = (FIELDS, levels, rows + 2 * TILE, width)
    full_shape = (FIELDS, levels, rows, width)

    def call(kernel, out_shape, in_specs, args, scratch=(), aliases=None, cost=1.0, name=None):
        spaces = {id(VMEM): pltpu.VMEM, id(HBM): pltpu.HBM}
        args = [pltpu.with_memory_space_constraint(x, spaces[id(s)]) for s, x in zip(in_specs, args)]
        return pl.pallas_call(
            functools.partial(kernel, levels, rows),
            out_shape=out_shape,
            in_specs=list(in_specs),
            out_specs=jax.tree.map(lambda o: HBM if o.memory_space is pltpu.HBM else VMEM, out_shape),
            scratch_shapes=list(scratch),
            input_output_aliases=aliases or {},
            cost_estimate=pl.CostEstimate(flops=0, bytes_accessed=int(cost * 3.69e6), transcendentals=0),
            compiler_params=pltpu.CompilerParams(vmem_limit_bytes=16 * 2**20),
            name=name,
        )(*args)

    pairs = [(i, i + 1) for i in range(0, ring, 2)]
    swap_inner = pairs + [(b, a) for a, b in pairs]
    pairs = [(i, (i + 1) % ring) for i in range(1, ring, 2)]
    swap_outer = pairs + [(b, a) for a, b in pairs]
    half = [(i, (i + ring // 2) % ring) for i in range(ring)]
    pairs = [(i, i + 1) for i in range(0, depth, 2)]
    swap_high = pairs + [(b, a) for a, b in pairs]
    pairs = [(lon * depth + i, lon * depth + i + 1) for lon in range(ring) for i in range(1, depth - 1, 2)]
    pairs += [(lon * depth + i, (lon + 1) * depth + i) for lon in range(0, ring, 2) for i in (0, depth - 1)]
    swap_low = pairs + [(b, a) for a, b in pairs]

    def around(inner, outer, polar):
        inner = lax.ppermute(inner, "lon", swap_inner)
        outer = lax.ppermute(outer, "lon", swap_outer)
        return inner, outer, lax.ppermute(polar, "lon", half)

    edge_shapes = [in_vmem(packs, width), in_vmem(packs, width), in_vmem(FIELDS * levels * REACH, width)]
    payload = in_vmem(halo_rows + TILE, width)
    high, low, after, kap, matrix, geo = call(
        levels_kernel,
        [
            payload,
            payload,
            in_vmem(*outer_rows.shape),
            in_vmem(levels, TILE, width),
            pltpu.VMEM(matrix.shape, matrix.dtype),
            in_vmem(*geo.shape),
        ],
        (HBM,) * 5,
        (state.reshape(-1, width), outer_rows, kappa, matrix, geo),
        scratch=(pltpu.SMEM(kappa.shape, jnp.float32), pltpu.SemaphoreType.DMA((2 * FIELDS + 4,))),
        name="levels",
    )
    above = lax.ppermute(high, "rad", swap_high)
    low, *edges = call(
        edges_kernel,
        [payload, *edge_shapes],
        (VMEM,) * 2,
        (low, high),
        aliases={0: 0},
        name="edges",
    )
    below = lax.ppermute(low, ("lon", "rad"), swap_low)
    inner, outer, beyond = around(*edges)
    lon_scratch = (in_vmem(*full_shape), in_vmem(*full_shape[1:]))
    side = in_vmem(halo_rows, width)
    padded, rate = call(
        first_kernel,
        [in_vmem(*pad_shape), in_vmem(*full_shape)],
        (VMEM,) * 6,
        (high, low, after, matrix, geo, kap),
        scratch=lon_scratch,
        cost=2.0,
        name="first",
    )

    def first_halo(rate, at):
        return call(
            functools.partial(first_halo_kernel, at),
            [in_vmem(*full_shape), side],
            (VMEM,) * 7,
            (rate, padded, beyond, inner, outer, geo, kap),
            aliases={0: 0},
            cost=0.6,
            name="first_halo",
        )

    rate, high = first_halo(rate, levels - REACH)
    above2 = lax.ppermute(high, "rad", swap_high)
    rate, low = first_halo(rate, 0)
    below2 = lax.ppermute(low, ("lon", "rad"), swap_low)
    full, ahead = call(
        section_high_kernel,
        [in_vmem(*full_shape), in_vmem(*pad_shape)],
        (VMEM,) * 4,
        (padded, rate, above, kap),
        cost=0.4,
        name="section_high",
    )
    full, ahead, *edges = call(
        section_low_kernel,
        [in_vmem(*full_shape), in_vmem(*pad_shape), *edge_shapes],
        (VMEM,) * 6,
        (padded, rate, below, kap, full, ahead),
        aliases={4: 0, 5: 1},
        cost=0.5,
        name="section_low",
    )
    inner, outer, beyond = around(*edges)
    both, low, high = call(
        second_kernel,
        [in_vmem(*full_shape), side, side],
        (VMEM,) * 8,
        (ahead, matrix, geo, kap, full, padded, below, above),
        scratch=lon_scratch,
        cost=2.5,
        name="second",
    )
    both = call(
        second_halo_kernel,
        in_vmem(*full_shape),
        (VMEM,) * 7,
        (both, ahead, beyond, inner, outer, geo, kap),
        aliases={0: 0},
        name="second_halo",
    )
    last_scratch = (
        in_vmem(FIELDS, REACH, rows, width),
        pltpu.SemaphoreType.DMA((rows // TILE,)),
    )
    result = pltpu.HBM(full_shape, jnp.float32)
    out = call(
        functools.partial(last_kernel, levels - REACH, True),
        result,
        (VMEM,) * 5,
        (ahead, both, above2, high, kap),
        scratch=last_scratch,
        cost=0.5,
        name="last_high",
    )
    return call(
        functools.partial(last_kernel, 0, False),
        result,
        (VMEM,) * 5 + (HBM,),
        (ahead, both, below2, low, kap, out),
        scratch=last_scratch,
        aliases={5: 0},
        name="last_low",
    )


def solution(mesh):
    placed = (P(None, "rad", None, "lon"), P(None, "rad", None, "lon"), P("rad"))
    return jax.shard_map(
        on_device,
        mesh=mesh,
        in_specs=placed,
        out_specs=P(None, "rad", None, "lon"),
        check_vma=False,
    )
```

```python
import functools
import math

import jax
import jax.numpy as jnp
import numpy as np
from jax import lax
from jax.experimental import pallas as pl
from jax.experimental.pallas import tpu as pltpu
from jax.sharding import PartitionSpec as P

first_coeffs = (0.8, -0.2, 4.0 / 105.0, -1.0 / 280.0)
second_coeffs = (-205.0 / 72.0, 1.6, -0.2, 8.0 / 315.0, -1.0 / 560.0)
time_step = 0.002
gamma_less_one = 0.4
radial_ratio = 3.0
FIELDS = 5
REACH = 4
TILE = 8
LANES = 128
GROUPS = LANES // (2 * REACH)
signs = (1.0, -1.0, -1.0, 1.0, 1.0)
first_whole = (672.0, -168.0, 32.0, -3.0)
second_whole = (8064.0, -1008.0, 128.0, -9.0)

level_first = tuple(radial_ratio * c for c in first_coeffs)
level_second = tuple(radial_ratio * radial_ratio * c for c in second_coeffs)

VMEM = pl.BlockSpec(memory_space=pltpu.VMEM)
HBM = pl.BlockSpec(memory_space=pltpu.HBM)


def in_vmem(*shape):
    return pltpu.VMEM(shape, jnp.float32)


def stencil_matrix(width):
    matrix = np.zeros((width, 2 * width), np.float32)
    for out in range(width):
        for k in range(1, REACH + 1):
            for sign in (1, -1):
                if 0 <= out + sign * k < width:
                    matrix[out + sign * k, out] = sign * first_whole[k - 1]
                    matrix[out + sign * k, width + out] = second_whole[k - 1]
    return jnp.asarray(matrix)


def geometry(rows, nlon, width):
    theta = (np.arange(rows) + 0.5) * (2.0 * math.pi / nlon)
    metric = 1.0 / np.sin(theta)
    table = np.stack([metric / 840.0, metric * metric / 5040.0, np.cos(theta) * metric])
    return jnp.asarray(np.broadcast_to(table[:, :, None], (3, rows, width)), jnp.float32)


def packed(tiles, lane):
    total = None
    for g, tile in enumerate(tiles):
        moved = pltpu.roll(tile, (REACH + 2 * REACH * g) % LANES, 1)
        if total is None:
            total = moved
        else:
            total = jnp.where(lane >= 2 * REACH * g, moved, total)
    return total


def across_level(center_wind, center_temper, halo, kappa, above):
    out = [[None] * REACH for _ in range(FIELDS)]
    for a in range(REACH):
        slopes = []
        for f in range(FIELDS):
            total = None
            for b in range(REACH):
                k = b + REACH - a if above else a + REACH - b
                if 1 <= k <= REACH:
                    c = level_first[k - 1] if above else -level_first[k - 1]
                    term = c * halo[f][b]
                    total = term if total is None else total + term
            slopes.append(total)
        curve = None
        for b in range(REACH):
            k = b + REACH - a if above else a + REACH - b
            if 1 <= k <= REACH:
                term = level_second[k] * halo[4][b]
                curve = term if curve is None else curve + term
        wind, temper = center_wind[a], center_temper[a]
        out[0][a] = -wind * slopes[0] - slopes[3]
        out[1][a] = -wind * slopes[1]
        out[2][a] = -wind * slopes[2]
        out[3][a] = -wind * slopes[3] - temper * slopes[0] - slopes[4]
        out[4][a] = -wind * slopes[4] - (gamma_less_one * temper) * slopes[3] + kappa[a] * curve
    return out


def high_kernel(
    levels, rows, state, kappa, high, kap, raw_kap, kappa_scalars, sems
):
    block = REACH * rows
    odd, _ = mirrored()
    start = jnp.where(odd == 1, 0, REACH)
    reads = [
        (state.at[pl.ds(pl.multiple_of((f * levels + start) * rows, TILE), block)], high.at[pl.ds(f * block, block)])
        for f in range(FIELDS)
    ]
    reads.append((kappa, kappa_scalars))
    copies = [pltpu.make_async_copy(*read, sems.at[i]) for i, read in enumerate(reads)]
    for copy in copies:
        copy.start()
    copies[FIELDS].wait()
    for i in range(REACH):
        row = pl.ds(FIELDS * block + i, 1)
        high[row, :] = jnp.full((1, LANES), kappa_scalars[start + i], jnp.float32)
        raw_kap[pl.ds(i, 1), :] = jnp.full((1, LANES), kappa_scalars[REACH - start + i], jnp.float32)
    for l in range(levels):
        value = kappa_scalars[jnp.where(odd == 1, levels - 1 - l, l)]
        kap[l] = jnp.full((TILE, LANES), value, jnp.float32)
    for copy in copies[:FIELDS]:
        copy.wait()


def low_kernel(levels, rows, state, raw_kap, low):
    block = REACH * rows
    odd, _ = mirrored()
    start = jnp.where(odd == 1, REACH, 0)
    for f in range(FIELDS):
        at = pl.multiple_of((f * levels + start) * rows, TILE)
        low[pl.ds(f * block, block), :] = state[pl.ds(at, block), :]
    low[pl.ds(FIELDS * block, REACH), :] = raw_kap[pl.ds(0, REACH), :]


def own_level(high, low, rows, f, l, odd):
    i = l % REACH
    at = (f * REACH + jnp.where(odd == 1, REACH - 1 - i, i)) * rows
    return (low if l < REACH else high), pl.multiple_of(at, TILE)


def edges_kernel(levels, rows, high, low, inner, outer, polar):
    odd, mirror = mirrored()
    packs = []
    for f in range(FIELDS):
        tiles = []
        for l in range(levels):
            side, at = own_level(high, low, rows, f, l, odd)
            tiles.append([side[pl.ds(at + t * TILE, TILE), :] for t in range(rows // TILE)])
            cap = side[pl.ds(at, REACH), :]
            polar[pl.ds((f * levels + l) * REACH, REACH), :] = mirror * cap if f == 3 else cap
        packs += [mirror * pack if f == 3 else pack for pack in packed(levels, rows, tiles)]
    store_packs(packs, inner, outer)


def mirrored():
    odd = lax.axis_index("rad") % 2
    return odd, jnp.where(odd == 1, -1.0, 1.0).astype(jnp.float32)


def bordered(at):
    here, depth = lax.axis_index("rad"), lax.axis_size("rad")
    inside = jnp.where((here > 0) & (here < depth - 1), 1.0, 0.0)
    return inside.astype(jnp.float32) if at == 0 else jnp.float32(1.0)


def lanes():
    return lax.broadcasted_iota(jnp.int32, (TILE, LANES), 1)


def packed(levels, rows, tiles):
    per = GROUPS // levels
    out = []
    for j in range(rows // TILE // per):
        total = None
        for g in range(GROUPS):
            moved = pltpu.roll(tiles[g % levels][j * per + g // levels], (REACH + 2 * REACH * g) % LANES, 1)
            total = moved if total is None else jnp.where(lanes() >= 2 * REACH * g, moved, total)
        out.append(total)
    return out


def store_packs(packs, inner, outer):
    first_half = lanes() % (2 * REACH) < REACH
    odd = lax.axis_index("lon") % 2 == 1
    for i in range(0, len(packs), 2):
        a, b = packs[i], packs[min(i + 1, len(packs) - 1)]
        at = pl.ds(i // 2 * TILE, TILE)
        east = jnp.where(first_half, a, pltpu.roll(b, REACH, 1))
        west = jnp.where(first_half, pltpu.roll(a, LANES - REACH, 1), b)
        inner[at, :] = jnp.where(odd, west, east)
        outer[at, :] = jnp.where(odd, east, west)


def load_packs(count, inner, outer):
    first_half = lanes() % (2 * REACH) < REACH
    odd = lax.axis_index("lon") % 2 == 1
    out = []
    for i in range(0, count, 2):
        at = pl.ds(i // 2 * TILE, TILE)
        before = jnp.where(odd, inner[at, :], outer[at, :])
        after = jnp.where(odd, outer[at, :], inner[at, :])
        out.append(jnp.where(first_half, before, pltpu.roll(after, REACH, 1)))
        out.append(jnp.where(first_half, pltpu.roll(before, LANES - REACH, 1), after))
    return out[:count]


def pieces_of(x):
    out = []
    for piece in range(3):
        out.append(x.astype(jnp.bfloat16))
        if piece < 2:
            x = x - out[-1].astype(jnp.float32)
    return out


def times_whole(pieces, m):
    total = None
    for piece in pieces:
        term = jnp.dot(piece, m, preferred_element_type=jnp.float32)
        total = term if total is None else total + term
    return total


def longitude_slopes(levels, rows, padded, matrix, dlon, elon):
    for f in range(FIELDS):
        x = padded[f, :, pl.ds(TILE, rows), :].reshape(levels * rows, LANES)
        whole = matrix[:, pl.ds(0, 2 * LANES if f == 4 else LANES)].astype(jnp.bfloat16)
        total = times_whole(pieces_of(x), whole)
        dlon[f] = total[:, :LANES].reshape(levels, rows, LANES)
        if f == 4:
            elon[...] = total[:, LANES:].reshape(levels, rows, LANES)


def groups_slope(pack, coeffs, sign):
    place = lanes() % (2 * REACH)
    total = None
    for k in range(1, REACH + 1):
        ahead = pltpu.roll(pack, LANES - k, 1)
        behind = pltpu.roll(pack, k, 1)
        from_after = (place < REACH) & (place >= REACH - k)
        from_before = (place >= REACH) & (place < REACH + k)
        term = jnp.where(from_after, coeffs[k - 1] * ahead, 0.0)
        term = jnp.where(from_before, (sign * coeffs[k - 1]) * behind, term)
        total = term if total is None else total + term
    return total


def add_halo(levels, rows, own, padded, polar, inner, outer, geo, kap, store):
    per = GROUPS // levels
    count = rows // TILE // per
    packs = load_packs(FIELDS * count, inner, outer)
    slopes = [groups_slope(pack, first_whole, -1.0) for pack in packs]
    bends = [groups_slope(pack, second_whole, 1.0) for pack in packs[4 * count :]]
    lane = lanes()
    at_side = (lane < REACH) | (lane >= LANES - REACH)
    row = lax.broadcasted_iota(jnp.int32, (TILE, LANES), 0)

    def by_row(coeffs, m):
        total = jnp.zeros((TILE, LANES), jnp.float32)
        for k in range(m + 1, REACH + 1):
            total = jnp.where(row == k - m - 1, coeffs[k - 1], total)
        return total

    first_rows = [by_row([-c for c in first_coeffs], m) for m in range(REACH)]
    second_rows = [by_row(second_coeffs[1:], m) for m in range(REACH)]
    for t in range(rows // TILE):
        j, u = divmod(t, per)
        here = pl.ds(t * TILE, TILE)
        metric = jnp.where(at_side, geo[0, here, :], 0.0)
        metric2 = jnp.where(at_side, geo[1, here, :], 0.0)
        for l in own:
            shift = (LANES - REACH - 2 * REACH * (u * levels + l)) % LANES
            center = [padded[f, l, pl.ds((t + 1) * TILE, TILE), :] for f in range(FIELDS)]
            wlon, wrow, temper = center[1], center[2], center[4]
            slon = [metric * pltpu.roll(slopes[f * count + j], shift, 1) for f in range(FIELDS)]
            laplace = metric2 * pltpu.roll(bends[j], shift, 1)
            extra = [-wlon * slope for slope in slon]
            extra[1] = extra[1] - temper * slon[0] - slon[4]
            spread = slon[1]
            if t == 0:
                srow = []
                for f in range(FIELDS):
                    total = None
                    for m in range(REACH):
                        across = signs[f] * polar[pl.ds((f * levels + l) * REACH + m, 1), :]
                        term = first_rows[m] * across
                        total = term if total is None else total + term
                        if f == 4:
                            laplace = laplace + second_rows[m] * across
                    srow.append(total)
                extra = [e - wrow * slope for e, slope in zip(extra, srow)]
                extra[2] = extra[2] - temper * srow[0] - srow[4]
                spread = spread + srow[2]
            extra[0] = extra[0] - spread
            extra[4] = extra[4] - (gamma_less_one * temper) * spread + kap[l] * laplace
            for f in range(FIELDS):
                store(f, l, t * TILE, center[f], extra[f])


def interior(levels, rows, padded, dlon, elon, geo, kappa, store):
    def body(t, carry):
        r0 = pl.multiple_of(t * TILE, TILE)
        here = pl.ds(r0, TILE)
        metric = geo[0, here, :]
        metric2 = geo[1, here, :]
        curvature = geo[2, here, :]
        center = [[padded[f, l, pl.ds(r0 + TILE, TILE), :] for l in range(levels)] for f in range(FIELDS)]
        out = [[None] * levels for _ in range(FIELDS)]
        for l in range(levels):
            wlon, wrow, wlev, temper = (center[f][l] for f in (1, 2, 3, 4))
            slon, srow, slev = [], [], []
            for f in range(FIELDS):
                slon.append(metric * dlon[f, l, here, :])
                total = None
                for k in range(1, REACH + 1):
                    ahead = padded[f, l, pl.ds(r0 + TILE + k, TILE), :]
                    behind = padded[f, l, pl.ds(r0 + TILE - k, TILE), :]
                    term = first_coeffs[k - 1] * (ahead - behind)
                    total = term if total is None else total + term
                    if f == 4:
                        curve = second_coeffs[k] * (ahead + behind)
                        bend = curve if k == 1 else bend + curve
                srow.append(total)
                total = None
                for k in range(1, REACH + 1):
                    up = center[f][l + k] if l + k < levels else None
                    down = center[f][l - k] if l - k >= 0 else None
                    if up is not None and down is not None:
                        term = level_first[k - 1] * (up - down)
                    elif up is not None:
                        term = level_first[k - 1] * up
                    elif down is not None:
                        term = -level_first[k - 1] * down
                    else:
                        continue
                    total = term if total is None else total + term
                slev.append(total)
            lift = None
            for k in range(1, REACH + 1):
                near = [center[4][l + s * k] for s in (1, -1) if 0 <= l + s * k < levels]
                if near:
                    term = level_second[k] * (near[0] + near[1] if len(near) == 2 else near[0])
                    lift = term if lift is None else lift + term
            middle = second_coeffs[0]
            laplace = metric2 * (elon[l, here, :] + (5040.0 * middle) * temper) + bend
            laplace = laplace + (middle + level_second[0]) * temper + lift
            carried = [wlon * slon[f] + wrow * srow[f] + wlev * slev[f] for f in range(FIELDS)]
            spread = slon[1] + srow[2] + slev[3] + curvature * wrow
            out[0][l] = -carried[0] - spread
            out[1][l] = -carried[1] - temper * slon[0] - slon[4]
            out[2][l] = -carried[2] - temper * srow[0] - srow[4]
            out[3][l] = -carried[3] - temper * slev[0] - slev[4]
            out[4][l] = -carried[4] - (gamma_less_one * temper) * spread + kappa[l] * laplace
            for f in range(FIELDS):
                store(f, l, r0, out[f][l])
        return carry

    lax.fori_loop(0, rows // TILE, body, 0)


def first_kernel(levels, rows, high, low, beyond, matrix, geo, kap, padded, rate, dlon, elon):
    odd, mirror = mirrored()
    for f in range(FIELDS):
        for l in range(levels):
            side, at = own_level(high, low, rows, f, l, odd)
            whole = side[pl.ds(at, rows), :]
            after = beyond[f, jnp.where(odd == 1, levels - 1 - l, l)]
            if f == 3:
                whole, after = mirror * whole, mirror * after
            padded[f, l, pl.ds(0, TILE), :] = jnp.zeros((TILE, LANES), jnp.float32)
            padded[f, l, pl.ds(TILE, rows), :] = whole
            padded[f, l, pl.ds(TILE + rows, REACH), :] = after
    longitude_slopes(levels, rows, padded, matrix, dlon, elon)

    def store(f, l, r0, tendency):
        rate[f, l, pl.ds(r0, TILE), :] = tendency

    interior(levels, rows, padded, dlon, elon, geo, kap, store)


def first_halo_kernel(at, levels, rows, given, padded, polar, inner, outer, geo, kap, rate, side):
    def store(f, l, r0, value, extra):
        tendency = given[f, l, pl.ds(r0, TILE), :] + extra
        rate[f, l, pl.ds(r0, TILE), :] = tendency
        side[pl.ds((f * REACH + l - at) * rows + r0, TILE), :] = value + time_step * tendency

    own = range(at, at + REACH)
    add_halo(levels, rows, own, padded, polar, inner, outer, geo, kap, store)


def raw_tile(ref, rows, r0, odd, mirror):
    out = []
    for f in range(FIELDS):
        ats = [(f * REACH + jnp.where(odd == 1, REACH - 1 - b, b)) * rows + r0 for b in range(REACH)]
        out.append([ref[pl.ds(pl.multiple_of(at, TILE), TILE), :] for at in ats])
    out[3] = [mirror * v for v in out[3]]
    return out


def halo_tile(ref, rows, r0):
    out = [
        [ref[pl.ds((f * REACH + REACH - 1 - b) * rows + r0, TILE), :] for b in range(REACH)]
        for f in range(FIELDS)
    ]
    out[3] = [-v for v in out[3]]
    return out


def own_tile(ref, rows, r0):
    return [
        [ref[pl.ds((f * REACH + b) * rows + r0, TILE), :] for b in range(REACH)] for f in range(FIELDS)
    ]


def section_side(at, up, levels, rows, padded, rate, sent, kappa, full, ahead):
    odd, mirror = mirrored()
    there = bordered(at)

    def body(t, carry):
        r0 = pl.multiple_of(t * TILE, TILE)
        here, inside = pl.ds(r0, TILE), pl.ds(r0 + TILE, TILE)
        halo = raw_tile(sent, rows, r0, odd, mirror)
        center = [[padded[f, at + a, inside, :] for a in range(REACH)] for f in range(FIELDS)]
        extra = across_level(center[3], center[4], halo, [kappa[at + a] for a in range(REACH)], up)
        for f in range(FIELDS):
            for a in range(REACH):
                more = extra[f][a] if at else there * extra[f][a]
                total = rate[f, at + a, here, :] + more
                full[f, at + a, here, :] = total
                ahead[f, at + a, inside, :] = center[f][a] + time_step * total
        return carry

    lax.fori_loop(0, rows // TILE, body, 0)
    for f in range(FIELDS):
        for l in range(at, at + REACH):
            ahead[f, l, pl.ds(0, TILE), :] = jnp.zeros((TILE, LANES), jnp.float32)
            ahead[f, l, pl.ds(rows + TILE, REACH), :] = padded[f, l, pl.ds(rows + TILE, REACH), :]


def section_high_kernel(levels, rows, padded, rate, above, kappa, full, ahead):
    section_side(levels - REACH, True, levels, rows, padded, rate, above, kappa, full, ahead)


def section_low_kernel(
    levels, rows, padded, rate, below, kappa, given1, given2, full, ahead, inner, outer, polar
):
    section_side(0, False, levels, rows, padded, rate, below, kappa, full, ahead)
    packs = []
    for f in range(FIELDS):
        tiles = [[ahead[f, l, pl.ds((t + 1) * TILE, TILE), :] for t in range(rows // TILE)] for l in range(levels)]
        packs += packed(levels, rows, tiles)
        for l in range(levels):
            polar[pl.ds((f * levels + l) * REACH, REACH), :] = ahead[f, l, pl.ds(TILE, REACH), :]
    store_packs(packs, inner, outer)


def second_kernel(
    levels, rows, padded, matrix, geo, kap, full, start, below, above, both, low, high, dlon, elon
):
    longitude_slopes(levels, rows, padded, matrix, dlon, elon)

    def store(f, l, r0, tendency):
        at = pl.ds(r0, TILE)
        both[f, l, at, :] = (0.5 * time_step) * (full[f, l, at, :] + tendency)

    interior(levels, rows, padded, dlon, elon, geo, kap, store)
    tail = FIELDS * REACH * rows
    odd, mirror = mirrored()

    def body(t, carry):
        r0 = pl.multiple_of(t * TILE, TILE)
        for halo_ref, out, at, up in ((below, low, 0, True), (above, high, levels - REACH, False)):
            beyond = raw_tile(halo_ref, rows, r0, odd, mirror)
            mine = [
                [start[f, at + a, pl.ds(r0 + TILE, TILE), :] for a in range(REACH)] for f in range(FIELDS)
            ]
            kappas = [
                halo_ref[pl.ds(tail + jnp.where(odd == 1, REACH - 1 - a, a), 1), :] for a in range(REACH)
            ]
            there = time_step * bordered(at)
            extra = across_level(beyond[3], beyond[4], mine, kappas, up)
            for f in range(FIELDS):
                for a in range(REACH):
                    out[pl.ds((f * REACH + a) * rows + r0, TILE), :] = there * extra[f][a]
        return carry

    lax.fori_loop(0, rows // TILE, body, 0)


def second_halo_kernel(
    levels, rows, given, padded, polar, inner, outer, geo, kap, both
):
    def store(f, l, r0, value, extra):
        at = pl.ds(r0, TILE)
        both[f, l, at, :] = given[f, l, at, :] + (0.5 * time_step) * extra

    add_halo(levels, rows, range(levels), padded, polar, inner, outer, geo, kap, store)


def write_side(at, more, levels, rows, padded, both, kap, out, staged, sems):
    odd, mirror = mirrored()
    for t in range(rows // TILE):
        here, inside = pl.ds(t * TILE, TILE), pl.ds((t + 1) * TILE, TILE)
        extra = None
        if more is not None:
            wind = [padded[3, at + a, inside, :] for a in range(REACH)]
            temper = [padded[4, at + a, inside, :] for a in range(REACH)]
            extra = more(t * TILE, wind, temper, [kap[at + a] for a in range(REACH)])
        for f in range(FIELDS):
            for a in range(REACH):
                new = both[f, at + a, here, :]
                if extra is not None:
                    new = new + (0.5 * time_step) * extra[f][a]
                staged[f, jnp.where(odd == 1, REACH - 1 - a, a), here, :] = mirror * new if f == 3 else new
        side_copy(at, t, levels, odd, out, staged, sems).start()


def side_copy(at, t, levels, odd, out, staged, sems):
    real, here = jnp.where(odd == 1, levels - at - REACH, at), pl.ds(t * TILE, TILE)
    return pltpu.make_async_copy(staged.at[:, :, here], out.at[:, pl.ds(real, REACH), here], sems.at[t])


def wait_side(at, levels, rows, out, staged, sems):
    odd, _ = mirrored()
    for t in range(rows // TILE):
        side_copy(at, t, levels, odd, out, staged, sems).wait()


def second_share(sent, more, up, rows):
    def share(r0, wind, temper, kappa):
        halo, there = halo_tile(sent, rows, r0), own_tile(more, rows, r0)
        halo = [[halo[f][b] + there[f][b] for b in range(REACH)] for f in range(FIELDS)]
        return across_level(wind, temper, halo, kappa, up)

    return share


def at_end():
    here, depth = lax.axis_index("rad"), lax.axis_size("rad")
    return (here == 0) | (here == depth - 1)


def last_high_kernel(
    levels, rows, padded, both, sent, more, kap, out, staged, sems, low_staged, low_sems
):
    @pl.when(at_end())
    def _():
        write_side(0, None, levels, rows, padded, both, kap, out, low_staged, low_sems)

    share = second_share(sent, more, True, rows)
    write_side(levels - REACH, share, levels, rows, padded, both, kap, out, staged, sems)
    wait_side(levels - REACH, levels, rows, out, staged, sems)

    @pl.when(at_end())
    def _():
        wait_side(0, levels, rows, out, low_staged, low_sems)


def last_low_kernel(levels, rows, padded, both, sent, more, kap, given, out, staged, sems):
    @pl.when(jnp.logical_not(at_end()))
    def _():
        share = second_share(sent, more, False, rows)
        write_side(0, share, levels, rows, padded, both, kap, out, staged, sems)
        wait_side(0, levels, rows, out, staged, sems)


def on_device(state, outer_rows, kappa):
    levels, rows, width = state.shape[1:]
    ring, depth = lax.axis_size("lon"), lax.axis_size("rad")
    assert ring % 4 == 0 and depth % 2 == 0 and width == LANES and levels == 2 * REACH and GROUPS % levels == 0
    assert rows % (TILE * (GROUPS // levels)) == 0
    matrix = stencil_matrix(width)
    geo = geometry(rows, width * ring, width)
    halo_rows = FIELDS * REACH * rows
    packs = -(-(FIELDS * levels * rows // TILE // GROUPS) // 2) * TILE
    pad_shape = (FIELDS, levels, rows + 2 * TILE, width)
    full_shape = (FIELDS, levels, rows, width)

    def call(kernel, out_shape, in_specs, args, scratch=(), aliases=None, cost=1.0, name=None):
        spaces = {id(VMEM): pltpu.VMEM, id(HBM): pltpu.HBM}
        args = [pltpu.with_memory_space_constraint(x, spaces[id(s)]) for s, x in zip(in_specs, args)]
        return pl.pallas_call(
            functools.partial(kernel, levels, rows),
            out_shape=out_shape,
            in_specs=list(in_specs),
            out_specs=jax.tree.map(lambda o: HBM if o.memory_space is pltpu.HBM else VMEM, out_shape),
            scratch_shapes=list(scratch),
            input_output_aliases=aliases or {},
            cost_estimate=pl.CostEstimate(flops=0, bytes_accessed=int(cost * 3.69e6), transcendentals=0),
            compiler_params=pltpu.CompilerParams(vmem_limit_bytes=16 * 2**20),
            name=name,
        )(*args)

    pairs = [(i, i + 1) for i in range(0, ring, 2)]
    swap_inner = pairs + [(b, a) for a, b in pairs]
    pairs = [(i, (i + 1) % ring) for i in range(1, ring, 2)]
    swap_outer = pairs + [(b, a) for a, b in pairs]
    half = [(i, (i + ring // 2) % ring) for i in range(ring)]
    pairs = [(i, i + 1) for i in range(0, depth, 2)]
    swap_high = pairs + [(b, a) for a, b in pairs]
    pairs = [(lon * depth + i, lon * depth + i + 1) for lon in range(ring) for i in range(1, depth - 1, 2)]
    pairs += [(lon * depth + i, (lon + 1) * depth + i) for lon in range(0, ring, 2) for i in (0, depth - 1)]
    swap_low = pairs + [(b, a) for a, b in pairs]

    def around(inner, outer, polar):
        inner = lax.ppermute(inner, "lon", swap_inner)
        outer = lax.ppermute(outer, "lon", swap_outer)
        return inner, outer, lax.ppermute(polar, "lon", half)

    edge_shapes = [in_vmem(packs, width), in_vmem(packs, width), in_vmem(FIELDS * levels * REACH, width)]
    payload = in_vmem(halo_rows + TILE, width)
    flat = state.reshape(-1, width)
    high, kap, raw_kap = call(
        high_kernel,
        [payload, in_vmem(levels, TILE, width), in_vmem(TILE, width)],
        (HBM,) * 2,
        (flat, kappa),
        scratch=(pltpu.SMEM(kappa.shape, jnp.float32), pltpu.SemaphoreType.DMA((FIELDS + 1,))),
        name="high",
    )
    above = lax.ppermute(high, "rad", swap_high)
    low = call(low_kernel, payload, (VMEM,) * 2, (flat, raw_kap), cost=0.2, name="low")
    below = lax.ppermute(low, ("lon", "rad"), swap_low)
    edges = call(edges_kernel, edge_shapes, (VMEM,) * 2, (high, low), cost=0.4, name="edges")
    inner, outer, beyond = around(*edges)
    lon_scratch = (in_vmem(*full_shape), in_vmem(*full_shape[1:]))
    side = in_vmem(halo_rows, width)
    padded, rate = call(
        first_kernel,
        [in_vmem(*pad_shape), in_vmem(*full_shape)],
        (VMEM,) * 6,
        (high, low, outer_rows, matrix, geo, kap),
        scratch=lon_scratch,
        cost=2.0,
        name="first",
    )

    def first_halo(rate, at):
        return call(
            functools.partial(first_halo_kernel, at),
            [in_vmem(*full_shape), side],
            (VMEM,) * 7,
            (rate, padded, beyond, inner, outer, geo, kap),
            aliases={0: 0},
            cost=0.6,
            name="first_halo",
        )

    rate, high = first_halo(rate, levels - REACH)
    above2 = lax.ppermute(high, "rad", swap_high)
    rate, low = first_halo(rate, 0)
    below2 = lax.ppermute(low, ("lon", "rad"), swap_low)
    full, ahead = call(
        section_high_kernel,
        [in_vmem(*full_shape), in_vmem(*pad_shape)],
        (VMEM,) * 4,
        (padded, rate, above, kap),
        cost=0.4,
        name="section_high",
    )
    full, ahead, *edges = call(
        section_low_kernel,
        [in_vmem(*full_shape), in_vmem(*pad_shape), *edge_shapes],
        (VMEM,) * 6,
        (padded, rate, below, kap, full, ahead),
        aliases={4: 0, 5: 1},
        cost=0.5,
        name="section_low",
    )
    inner, outer, beyond = around(*edges)
    both, low, high = call(
        second_kernel,
        [in_vmem(*full_shape), side, side],
        (VMEM,) * 8,
        (ahead, matrix, geo, kap, full, padded, below, above),
        scratch=lon_scratch,
        cost=2.5,
        name="second",
    )
    both = call(
        second_halo_kernel,
        in_vmem(*full_shape),
        (VMEM,) * 7,
        (both, ahead, beyond, inner, outer, geo, kap),
        aliases={0: 0},
        name="second_halo",
    )
    last_scratch = (
        in_vmem(FIELDS, REACH, rows, width),
        pltpu.SemaphoreType.DMA((rows // TILE,)),
    )
    result = pltpu.HBM(full_shape, jnp.float32)
    out = call(
        last_high_kernel,
        result,
        (VMEM,) * 5,
        (ahead, both, above2, high, kap),
        scratch=last_scratch * 2,
        cost=0.5,
        name="last_high",
    )
    return call(
        last_low_kernel,
        result,
        (VMEM,) * 5 + (HBM,),
        (ahead, both, below2, low, kap, out),
        scratch=last_scratch,
        aliases={5: 0},
        name="last_low",
    )


def solution(mesh):
    placed = (P(None, "rad", None, "lon"), P(None, "rad", None, "lon"), P("rad"))
    return jax.shard_map(
        on_device,
        mesh=mesh,
        in_specs=placed,
        out_specs=P(None, "rad", None, "lon"),
        check_vma=False,
    )
```

```python
import functools
import math

import jax
import jax.numpy as jnp
import numpy as np
from jax import lax
from jax.experimental import pallas as pl
from jax.experimental.pallas import tpu as pltpu
from jax.sharding import PartitionSpec as P

first_coeffs = (0.8, -0.2, 4.0 / 105.0, -1.0 / 280.0)
second_coeffs = (-205.0 / 72.0, 1.6, -0.2, 8.0 / 315.0, -1.0 / 560.0)
time_step = 0.002
gamma_less_one = 0.4
radial_ratio = 3.0
FIELDS = 5
REACH = 4
TILE = 8
LANES = 128
GROUPS = LANES // (2 * REACH)
signs = (1.0, -1.0, -1.0, 1.0, 1.0)
first_whole = (672.0, -168.0, 32.0, -3.0)
second_whole = (8064.0, -1008.0, 128.0, -9.0)

level_first = tuple(radial_ratio * c for c in first_coeffs)
level_second = tuple(radial_ratio * radial_ratio * c for c in second_coeffs)

VMEM = pl.BlockSpec(memory_space=pltpu.VMEM)
HBM = pl.BlockSpec(memory_space=pltpu.HBM)


def in_vmem(*shape):
    return pltpu.VMEM(shape, jnp.float32)


def stencil_matrix(width):
    matrix = np.zeros((width, 2 * width), np.float32)
    for out in range(width):
        for k in range(1, REACH + 1):
            for sign in (1, -1):
                if 0 <= out + sign * k < width:
                    matrix[out + sign * k, out] = sign * first_whole[k - 1]
                    matrix[out + sign * k, width + out] = second_whole[k - 1]
    return jnp.asarray(matrix)


def geometry(rows, nlon, width):
    theta = (np.arange(rows) + 0.5) * (2.0 * math.pi / nlon)
    metric = 1.0 / np.sin(theta)
    table = np.stack([metric / 840.0, metric * metric / 5040.0, np.cos(theta) * metric])
    return jnp.asarray(np.broadcast_to(table[:, :, None], (3, rows, width)), jnp.float32)


def packed(tiles, lane):
    total = None
    for g, tile in enumerate(tiles):
        moved = pltpu.roll(tile, (REACH + 2 * REACH * g) % LANES, 1)
        if total is None:
            total = moved
        else:
            total = jnp.where(lane >= 2 * REACH * g, moved, total)
    return total


def across_level(center_wind, center_temper, halo, kappa, above):
    out = [[None] * REACH for _ in range(FIELDS)]
    for a in range(REACH):
        slopes = []
        for f in range(FIELDS):
            total = None
            for b in range(REACH):
                k = b + REACH - a if above else a + REACH - b
                if 1 <= k <= REACH:
                    c = level_first[k - 1] if above else -level_first[k - 1]
                    term = c * halo[f][b]
                    total = term if total is None else total + term
            slopes.append(total)
        curve = None
        for b in range(REACH):
            k = b + REACH - a if above else a + REACH - b
            if 1 <= k <= REACH:
                term = level_second[k] * halo[4][b]
                curve = term if curve is None else curve + term
        wind, temper = center_wind[a], center_temper[a]
        out[0][a] = -wind * slopes[0] - slopes[3]
        out[1][a] = -wind * slopes[1]
        out[2][a] = -wind * slopes[2]
        out[3][a] = -wind * slopes[3] - temper * slopes[0] - slopes[4]
        out[4][a] = -wind * slopes[4] - (gamma_less_one * temper) * slopes[3] + kappa[a] * curve
    return out


def high_kernel(
    levels, rows, state, kappa, high, kap, raw_kap, kappa_scalars, sems
):
    block = REACH * rows
    odd, _ = mirrored()
    start = jnp.where(odd == 1, 0, REACH)
    half, reads = block // 2, [(kappa, kappa_scalars)]
    for f in range(FIELDS):
        for part in range(2):
            at = pl.multiple_of((f * levels + start) * rows + part * half, TILE)
            reads.append((state.at[pl.ds(at, half)], high.at[pl.ds(f * block + part * half, half)]))
    copies = [pltpu.make_async_copy(*read, sems.at[i]) for i, read in enumerate(reads)]
    for copy in copies:
        copy.start()
    copies[0].wait()
    for i in range(REACH):
        row = pl.ds(FIELDS * block + i, 1)
        high[row, :] = jnp.full((1, LANES), kappa_scalars[start + i], jnp.float32)
        raw_kap[pl.ds(i, 1), :] = jnp.full((1, LANES), kappa_scalars[REACH - start + i], jnp.float32)
    for l in range(levels):
        value = kappa_scalars[jnp.where(odd == 1, levels - 1 - l, l)]
        kap[l] = jnp.full((TILE, LANES), value, jnp.float32)
    for copy in copies[1:]:
        copy.wait()


def low_kernel(levels, rows, state, raw_kap, low):
    block = REACH * rows
    odd, _ = mirrored()
    start = jnp.where(odd == 1, REACH, 0)
    for f in range(FIELDS):
        at = pl.multiple_of((f * levels + start) * rows, TILE)
        low[pl.ds(f * block, block), :] = state[pl.ds(at, block), :]
    low[pl.ds(FIELDS * block, REACH), :] = raw_kap[pl.ds(0, REACH), :]


def own_level(high, low, rows, f, l, odd):
    i = l % REACH
    at = (f * REACH + jnp.where(odd == 1, REACH - 1 - i, i)) * rows
    return (low if l < REACH else high), pl.multiple_of(at, TILE)


def edges_kernel(levels, rows, high, low, inner, outer, polar):
    odd, mirror = mirrored()
    packs = []
    for f in range(FIELDS):
        tiles = []
        for l in range(levels):
            side, at = own_level(high, low, rows, f, l, odd)
            tiles.append([side[pl.ds(at + t * TILE, TILE), :] for t in range(rows // TILE)])
            cap = side[pl.ds(at, REACH), :]
            polar[pl.ds((f * levels + l) * REACH, REACH), :] = mirror * cap if f == 3 else cap
        packs += [mirror * pack if f == 3 else pack for pack in packed(levels, rows, tiles)]
    store_packs(packs, inner, outer)


def mirrored():
    odd = lax.axis_index("rad") % 2
    return odd, jnp.where(odd == 1, -1.0, 1.0).astype(jnp.float32)


def bordered(at):
    here, depth = lax.axis_index("rad"), lax.axis_size("rad")
    inside = jnp.where((here > 0) & (here < depth - 1), 1.0, 0.0)
    return inside.astype(jnp.float32) if at == 0 else jnp.float32(1.0)


def lanes():
    return lax.broadcasted_iota(jnp.int32, (TILE, LANES), 1)


def packed(levels, rows, tiles):
    per = GROUPS // levels
    out = []
    for j in range(rows // TILE // per):
        total = None
        for g in range(GROUPS):
            moved = pltpu.roll(tiles[g % levels][j * per + g // levels], (REACH + 2 * REACH * g) % LANES, 1)
            total = moved if total is None else jnp.where(lanes() >= 2 * REACH * g, moved, total)
        out.append(total)
    return out


def store_packs(packs, inner, outer):
    first_half = lanes() % (2 * REACH) < REACH
    odd = lax.axis_index("lon") % 2 == 1
    for i in range(0, len(packs), 2):
        a, b = packs[i], packs[min(i + 1, len(packs) - 1)]
        at = pl.ds(i // 2 * TILE, TILE)
        east = jnp.where(first_half, a, pltpu.roll(b, REACH, 1))
        west = jnp.where(first_half, pltpu.roll(a, LANES - REACH, 1), b)
        inner[at, :] = jnp.where(odd, west, east)
        outer[at, :] = jnp.where(odd, east, west)


def load_packs(count, inner, outer):
    first_half = lanes() % (2 * REACH) < REACH
    odd = lax.axis_index("lon") % 2 == 1
    out = []
    for i in range(0, count, 2):
        at = pl.ds(i // 2 * TILE, TILE)
        before = jnp.where(odd, inner[at, :], outer[at, :])
        after = jnp.where(odd, outer[at, :], inner[at, :])
        out.append(jnp.where(first_half, before, pltpu.roll(after, REACH, 1)))
        out.append(jnp.where(first_half, pltpu.roll(before, LANES - REACH, 1), after))
    return out[:count]


def pieces_of(x):
    out = []
    for piece in range(3):
        out.append(x.astype(jnp.bfloat16))
        if piece < 2:
            x = x - out[-1].astype(jnp.float32)
    return out


def times_whole(pieces, m):
    total = None
    for piece in pieces:
        term = jnp.dot(piece, m, preferred_element_type=jnp.float32)
        total = term if total is None else total + term
    return total


def longitude_slopes(levels, rows, padded, matrix, dlon, elon):
    for f in range(FIELDS):
        x = padded[f, :, pl.ds(TILE, rows), :].reshape(levels * rows, LANES)
        whole = matrix[:, pl.ds(0, 2 * LANES if f == 4 else LANES)].astype(jnp.bfloat16)
        total = times_whole(pieces_of(x), whole)
        dlon[f] = total[:, :LANES].reshape(levels, rows, LANES)
        if f == 4:
            elon[...] = total[:, LANES:].reshape(levels, rows, LANES)


def groups_slope(pack, coeffs, sign):
    place = lanes() % (2 * REACH)
    total = None
    for k in range(1, REACH + 1):
        ahead = pltpu.roll(pack, LANES - k, 1)
        behind = pltpu.roll(pack, k, 1)
        from_after = (place < REACH) & (place >= REACH - k)
        from_before = (place >= REACH) & (place < REACH + k)
        term = jnp.where(from_after, coeffs[k - 1] * ahead, 0.0)
        term = jnp.where(from_before, (sign * coeffs[k - 1]) * behind, term)
        total = term if total is None else total + term
    return total


def add_halo(levels, rows, own, padded, polar, inner, outer, geo, kap, store):
    per = GROUPS // levels
    count = rows // TILE // per
    packs = load_packs(FIELDS * count, inner, outer)
    slopes = [groups_slope(pack, first_whole, -1.0) for pack in packs]
    bends = [groups_slope(pack, second_whole, 1.0) for pack in packs[4 * count :]]
    lane = lanes()
    at_side = (lane < REACH) | (lane >= LANES - REACH)
    row = lax.broadcasted_iota(jnp.int32, (TILE, LANES), 0)

    def by_row(coeffs, m):
        total = jnp.zeros((TILE, LANES), jnp.float32)
        for k in range(m + 1, REACH + 1):
            total = jnp.where(row == k - m - 1, coeffs[k - 1], total)
        return total

    first_rows = [by_row([-c for c in first_coeffs], m) for m in range(REACH)]
    second_rows = [by_row(second_coeffs[1:], m) for m in range(REACH)]
    for t in range(rows // TILE):
        j, u = divmod(t, per)
        here = pl.ds(t * TILE, TILE)
        metric = jnp.where(at_side, geo[0, here, :], 0.0)
        metric2 = jnp.where(at_side, geo[1, here, :], 0.0)
        for l in own:
            shift = (LANES - REACH - 2 * REACH * (u * levels + l)) % LANES
            center = [padded[f, l, pl.ds((t + 1) * TILE, TILE), :] for f in range(FIELDS)]
            wlon, wrow, temper = center[1], center[2], center[4]
            slon = [metric * pltpu.roll(slopes[f * count + j], shift, 1) for f in range(FIELDS)]
            laplace = metric2 * pltpu.roll(bends[j], shift, 1)
            extra = [-wlon * slope for slope in slon]
            extra[1] = extra[1] - temper * slon[0] - slon[4]
            spread = slon[1]
            if t == 0:
                srow = []
                for f in range(FIELDS):
                    total = None
                    for m in range(REACH):
                        across = signs[f] * polar[pl.ds((f * levels + l) * REACH + m, 1), :]
                        term = first_rows[m] * across
                        total = term if total is None else total + term
                        if f == 4:
                            laplace = laplace + second_rows[m] * across
                    srow.append(total)
                extra = [e - wrow * slope for e, slope in zip(extra, srow)]
                extra[2] = extra[2] - temper * srow[0] - srow[4]
                spread = spread + srow[2]
            extra[0] = extra[0] - spread
            extra[4] = extra[4] - (gamma_less_one * temper) * spread + kap[l] * laplace
            for f in range(FIELDS):
                store(f, l, t * TILE, center[f], extra[f])


def interior(levels, rows, padded, dlon, elon, geo, kappa, store):
    def body(t, carry):
        r0 = pl.multiple_of(t * TILE, TILE)
        here = pl.ds(r0, TILE)
        metric = geo[0, here, :]
        metric2 = geo[1, here, :]
        curvature = geo[2, here, :]
        center = [[padded[f, l, pl.ds(r0 + TILE, TILE), :] for l in range(levels)] for f in range(FIELDS)]
        out = [[None] * levels for _ in range(FIELDS)]
        for l in range(levels):
            wlon, wrow, wlev, temper = (center[f][l] for f in (1, 2, 3, 4))
            slon, srow, slev = [], [], []
            for f in range(FIELDS):
                slon.append(metric * dlon[f, l, here, :])
                total = None
                for k in range(1, REACH + 1):
                    ahead = padded[f, l, pl.ds(r0 + TILE + k, TILE), :]
                    behind = padded[f, l, pl.ds(r0 + TILE - k, TILE), :]
                    term = first_coeffs[k - 1] * (ahead - behind)
                    total = term if total is None else total + term
                    if f == 4:
                        curve = second_coeffs[k] * (ahead + behind)
                        bend = curve if k == 1 else bend + curve
                srow.append(total)
                total = None
                for k in range(1, REACH + 1):
                    up = center[f][l + k] if l + k < levels else None
                    down = center[f][l - k] if l - k >= 0 else None
                    if up is not None and down is not None:
                        term = level_first[k - 1] * (up - down)
                    elif up is not None:
                        term = level_first[k - 1] * up
                    elif down is not None:
                        term = -level_first[k - 1] * down
                    else:
                        continue
                    total = term if total is None else total + term
                slev.append(total)
            lift = None
            for k in range(1, REACH + 1):
                near = [center[4][l + s * k] for s in (1, -1) if 0 <= l + s * k < levels]
                if near:
                    term = level_second[k] * (near[0] + near[1] if len(near) == 2 else near[0])
                    lift = term if lift is None else lift + term
            middle = second_coeffs[0]
            laplace = metric2 * (elon[l, here, :] + (5040.0 * middle) * temper) + bend
            laplace = laplace + (middle + level_second[0]) * temper + lift
            carried = [wlon * slon[f] + wrow * srow[f] + wlev * slev[f] for f in range(FIELDS)]
            spread = slon[1] + srow[2] + slev[3] + curvature * wrow
            out[0][l] = -carried[0] - spread
            out[1][l] = -carried[1] - temper * slon[0] - slon[4]
            out[2][l] = -carried[2] - temper * srow[0] - srow[4]
            out[3][l] = -carried[3] - temper * slev[0] - slev[4]
            out[4][l] = -carried[4] - (gamma_less_one * temper) * spread + kappa[l] * laplace
            for f in range(FIELDS):
                store(f, l, r0, out[f][l])
        return carry

    lax.fori_loop(0, rows // TILE, body, 0)


def first_kernel(levels, rows, high, low, beyond, matrix, geo, kap, padded, rate, dlon, elon):
    odd, mirror = mirrored()
    for f in range(FIELDS):
        for l in range(levels):
            side, at = own_level(high, low, rows, f, l, odd)
            whole = side[pl.ds(at, rows), :]
            after = beyond[f, jnp.where(odd == 1, levels - 1 - l, l)]
            if f == 3:
                whole, after = mirror * whole, mirror * after
            padded[f, l, pl.ds(0, TILE), :] = jnp.zeros((TILE, LANES), jnp.float32)
            padded[f, l, pl.ds(TILE, rows), :] = whole
            padded[f, l, pl.ds(TILE + rows, REACH), :] = after
    longitude_slopes(levels, rows, padded, matrix, dlon, elon)

    def store(f, l, r0, tendency):
        rate[f, l, pl.ds(r0, TILE), :] = tendency

    interior(levels, rows, padded, dlon, elon, geo, kap, store)


def first_halo_kernel(at, levels, rows, given, padded, polar, inner, outer, geo, kap, rate, side):
    def store(f, l, r0, value, extra):
        tendency = given[f, l, pl.ds(r0, TILE), :] + extra
        rate[f, l, pl.ds(r0, TILE), :] = tendency
        side[pl.ds((f * REACH + l - at) * rows + r0, TILE), :] = value + time_step * tendency

    own = range(at, at + REACH)
    add_halo(levels, rows, own, padded, polar, inner, outer, geo, kap, store)


def raw_tile(ref, rows, r0, odd, mirror):
    out = []
    for f in range(FIELDS):
        ats = [(f * REACH + jnp.where(odd == 1, REACH - 1 - b, b)) * rows + r0 for b in range(REACH)]
        out.append([ref[pl.ds(pl.multiple_of(at, TILE), TILE), :] for at in ats])
    out[3] = [mirror * v for v in out[3]]
    return out


def halo_tile(ref, rows, r0):
    out = [
        [ref[pl.ds((f * REACH + REACH - 1 - b) * rows + r0, TILE), :] for b in range(REACH)]
        for f in range(FIELDS)
    ]
    out[3] = [-v for v in out[3]]
    return out


def own_tile(ref, rows, r0):
    return [
        [ref[pl.ds((f * REACH + b) * rows + r0, TILE), :] for b in range(REACH)] for f in range(FIELDS)
    ]


def section_side(at, up, levels, rows, padded, rate, sent, kappa, full, ahead):
    odd, mirror = mirrored()
    there = bordered(at)

    def body(t, carry):
        r0 = pl.multiple_of(t * TILE, TILE)
        here, inside = pl.ds(r0, TILE), pl.ds(r0 + TILE, TILE)
        halo = raw_tile(sent, rows, r0, odd, mirror)
        center = [[padded[f, at + a, inside, :] for a in range(REACH)] for f in range(FIELDS)]
        extra = across_level(center[3], center[4], halo, [kappa[at + a] for a in range(REACH)], up)
        for f in range(FIELDS):
            for a in range(REACH):
                more = extra[f][a] if at else there * extra[f][a]
                total = rate[f, at + a, here, :] + more
                full[f, at + a, here, :] = total
                ahead[f, at + a, inside, :] = center[f][a] + time_step * total
        return carry

    lax.fori_loop(0, rows // TILE, body, 0)
    for f in range(FIELDS):
        for l in range(at, at + REACH):
            ahead[f, l, pl.ds(0, TILE), :] = jnp.zeros((TILE, LANES), jnp.float32)
            ahead[f, l, pl.ds(rows + TILE, REACH), :] = padded[f, l, pl.ds(rows + TILE, REACH), :]


def section_high_kernel(levels, rows, padded, rate, above, kappa, full, ahead):
    section_side(levels - REACH, True, levels, rows, padded, rate, above, kappa, full, ahead)


def section_low_kernel(
    levels, rows, padded, rate, below, kappa, given1, given2, full, ahead, inner, outer, polar
):
    section_side(0, False, levels, rows, padded, rate, below, kappa, full, ahead)
    packs = []
    for f in range(FIELDS):
        tiles = [[ahead[f, l, pl.ds((t + 1) * TILE, TILE), :] for t in range(rows // TILE)] for l in range(levels)]
        packs += packed(levels, rows, tiles)
        for l in range(levels):
            polar[pl.ds((f * levels + l) * REACH, REACH), :] = ahead[f, l, pl.ds(TILE, REACH), :]
    store_packs(packs, inner, outer)


def second_kernel(
    levels, rows, padded, matrix, geo, kap, full, start, below, above, both, low, high, dlon, elon
):
    longitude_slopes(levels, rows, padded, matrix, dlon, elon)

    def store(f, l, r0, tendency):
        at = pl.ds(r0, TILE)
        both[f, l, at, :] = (0.5 * time_step) * (full[f, l, at, :] + tendency)

    interior(levels, rows, padded, dlon, elon, geo, kap, store)
    tail = FIELDS * REACH * rows
    odd, mirror = mirrored()

    def body(t, carry):
        r0 = pl.multiple_of(t * TILE, TILE)
        for halo_ref, out, at, up in ((below, low, 0, True), (above, high, levels - REACH, False)):
            beyond = raw_tile(halo_ref, rows, r0, odd, mirror)
            mine = [
                [start[f, at + a, pl.ds(r0 + TILE, TILE), :] for a in range(REACH)] for f in range(FIELDS)
            ]
            kappas = [
                halo_ref[pl.ds(tail + jnp.where(odd == 1, REACH - 1 - a, a), 1), :] for a in range(REACH)
            ]
            there = time_step * bordered(at)
            extra = across_level(beyond[3], beyond[4], mine, kappas, up)
            for f in range(FIELDS):
                for a in range(REACH):
                    out[pl.ds((f * REACH + a) * rows + r0, TILE), :] = there * extra[f][a]
        return carry

    lax.fori_loop(0, rows // TILE, body, 0)


def second_halo_kernel(
    levels, rows, given, padded, polar, inner, outer, geo, kap, both
):
    def store(f, l, r0, value, extra):
        at = pl.ds(r0, TILE)
        both[f, l, at, :] = given[f, l, at, :] + (0.5 * time_step) * extra

    add_halo(levels, rows, range(levels), padded, polar, inner, outer, geo, kap, store)


def write_side(at, more, levels, rows, padded, both, kap, out, staged, sems):
    odd, mirror = mirrored()
    for t in range(rows // TILE):
        here, inside = pl.ds(t * TILE, TILE), pl.ds((t + 1) * TILE, TILE)
        extra = None
        if more is not None:
            wind = [padded[3, at + a, inside, :] for a in range(REACH)]
            temper = [padded[4, at + a, inside, :] for a in range(REACH)]
            extra = more(t * TILE, wind, temper, [kap[at + a] for a in range(REACH)])
        for f in range(FIELDS):
            for a in range(REACH):
                new = both[f, at + a, here, :]
                if extra is not None:
                    new = new + (0.5 * time_step) * extra[f][a]
                staged[f, jnp.where(odd == 1, REACH - 1 - a, a), here, :] = mirror * new if f == 3 else new
        side_copy(at, t, levels, odd, out, staged, sems).start()


def side_copy(at, t, levels, odd, out, staged, sems):
    real, here = jnp.where(odd == 1, levels - at - REACH, at), pl.ds(t * TILE, TILE)
    return pltpu.make_async_copy(staged.at[:, :, here], out.at[:, pl.ds(real, REACH), here], sems.at[t])


def wait_side(at, levels, rows, out, staged, sems):
    odd, _ = mirrored()
    for t in range(rows // TILE):
        side_copy(at, t, levels, odd, out, staged, sems).wait()


def second_share(sent, more, up, rows):
    def share(r0, wind, temper, kappa):
        halo, there = halo_tile(sent, rows, r0), own_tile(more, rows, r0)
        halo = [[halo[f][b] + there[f][b] for b in range(REACH)] for f in range(FIELDS)]
        return across_level(wind, temper, halo, kappa, up)

    return share


def at_end():
    here, depth = lax.axis_index("rad"), lax.axis_size("rad")
    return (here == 0) | (here == depth - 1)


def end_low_kernel(levels, rows, padded, both, kap, out, staged, sems):
    @pl.when(at_end())
    def _():
        write_side(0, None, levels, rows, padded, both, kap, out, staged, sems)
        wait_side(0, levels, rows, out, staged, sems)


def last_high_kernel(levels, rows, padded, both, sent, more, kap, given, out, staged, sems):
    share = second_share(sent, more, True, rows)
    write_side(levels - REACH, share, levels, rows, padded, both, kap, out, staged, sems)
    wait_side(levels - REACH, levels, rows, out, staged, sems)


def last_low_kernel(levels, rows, padded, both, sent, more, kap, given, out, staged, sems):
    @pl.when(jnp.logical_not(at_end()))
    def _():
        share = second_share(sent, more, False, rows)
        write_side(0, share, levels, rows, padded, both, kap, out, staged, sems)
        wait_side(0, levels, rows, out, staged, sems)


def on_device(state, outer_rows, kappa):
    levels, rows, width = state.shape[1:]
    ring, depth = lax.axis_size("lon"), lax.axis_size("rad")
    assert ring % 4 == 0 and depth % 2 == 0 and width == LANES and levels == 2 * REACH and GROUPS % levels == 0
    assert rows % (TILE * (GROUPS // levels)) == 0
    matrix = stencil_matrix(width)
    geo = geometry(rows, width * ring, width)
    halo_rows = FIELDS * REACH * rows
    packs = -(-(FIELDS * levels * rows // TILE // GROUPS) // 2) * TILE
    pad_shape = (FIELDS, levels, rows + 2 * TILE, width)
    full_shape = (FIELDS, levels, rows, width)

    def call(kernel, out_shape, in_specs, args, scratch=(), aliases=None, cost=1.0, name=None):
        spaces = {id(VMEM): pltpu.VMEM, id(HBM): pltpu.HBM}
        args = [pltpu.with_memory_space_constraint(x, spaces[id(s)]) for s, x in zip(in_specs, args)]
        return pl.pallas_call(
            functools.partial(kernel, levels, rows),
            out_shape=out_shape,
            in_specs=list(in_specs),
            out_specs=jax.tree.map(lambda o: HBM if o.memory_space is pltpu.HBM else VMEM, out_shape),
            scratch_shapes=list(scratch),
            input_output_aliases=aliases or {},
            cost_estimate=pl.CostEstimate(flops=0, bytes_accessed=int(cost * 3.69e6), transcendentals=0),
            compiler_params=pltpu.CompilerParams(vmem_limit_bytes=16 * 2**20),
            name=name,
        )(*args)

    pairs = [(i, i + 1) for i in range(0, ring, 2)]
    swap_inner = pairs + [(b, a) for a, b in pairs]
    pairs = [(i, (i + 1) % ring) for i in range(1, ring, 2)]
    swap_outer = pairs + [(b, a) for a, b in pairs]
    half = [(i, (i + ring // 2) % ring) for i in range(ring)]
    pairs = [(i, i + 1) for i in range(0, depth, 2)]
    swap_high = pairs + [(b, a) for a, b in pairs]
    pairs = [(lon * depth + i, lon * depth + i + 1) for lon in range(ring) for i in range(1, depth - 1, 2)]
    pairs += [(lon * depth + i, (lon + 1) * depth + i) for lon in range(0, ring, 2) for i in (0, depth - 1)]
    swap_low = pairs + [(b, a) for a, b in pairs]

    def around(inner, outer, polar):
        inner = lax.ppermute(inner, "lon", swap_inner)
        outer = lax.ppermute(outer, "lon", swap_outer)
        return inner, outer, lax.ppermute(polar, "lon", half)

    edge_shapes = [in_vmem(packs, width), in_vmem(packs, width), in_vmem(FIELDS * levels * REACH, width)]
    payload = in_vmem(halo_rows + TILE, width)
    flat = state.reshape(-1, width)
    high, kap, raw_kap = call(
        high_kernel,
        [payload, in_vmem(levels, TILE, width), in_vmem(TILE, width)],
        (HBM,) * 2,
        (flat, kappa),
        scratch=(pltpu.SMEM(kappa.shape, jnp.float32), pltpu.SemaphoreType.DMA((2 * FIELDS + 1,))),
        name="high",
    )
    above = lax.ppermute(high, "rad", swap_high)
    low = call(low_kernel, payload, (VMEM,) * 2, (flat, raw_kap), cost=0.2, name="low")
    below = lax.ppermute(low, ("lon", "rad"), swap_low)
    edges = call(edges_kernel, edge_shapes, (VMEM,) * 2, (high, low), cost=0.4, name="edges")
    inner, outer, beyond = around(*edges)
    lon_scratch = (in_vmem(*full_shape), in_vmem(*full_shape[1:]))
    side = in_vmem(halo_rows, width)
    padded, rate = call(
        first_kernel,
        [in_vmem(*pad_shape), in_vmem(*full_shape)],
        (VMEM,) * 6,
        (high, low, outer_rows, matrix, geo, kap),
        scratch=lon_scratch,
        cost=2.0,
        name="first",
    )

    def first_halo(rate, at):
        return call(
            functools.partial(first_halo_kernel, at),
            [in_vmem(*full_shape), side],
            (VMEM,) * 7,
            (rate, padded, beyond, inner, outer, geo, kap),
            aliases={0: 0},
            cost=0.6,
            name="first_halo",
        )

    rate, high = first_halo(rate, levels - REACH)
    above2 = lax.ppermute(high, "rad", swap_high)
    rate, low = first_halo(rate, 0)
    below2 = lax.ppermute(low, ("lon", "rad"), swap_low)
    full, ahead = call(
        section_high_kernel,
        [in_vmem(*full_shape), in_vmem(*pad_shape)],
        (VMEM,) * 4,
        (padded, rate, above, kap),
        cost=0.4,
        name="section_high",
    )
    full, ahead, *edges = call(
        section_low_kernel,
        [in_vmem(*full_shape), in_vmem(*pad_shape), *edge_shapes],
        (VMEM,) * 6,
        (padded, rate, below, kap, full, ahead),
        aliases={4: 0, 5: 1},
        cost=0.5,
        name="section_low",
    )
    inner, outer, beyond = around(*edges)
    both, low, high = call(
        second_kernel,
        [in_vmem(*full_shape), side, side],
        (VMEM,) * 8,
        (ahead, matrix, geo, kap, full, padded, below, above),
        scratch=lon_scratch,
        cost=2.5,
        name="second",
    )
    both = call(
        second_halo_kernel,
        in_vmem(*full_shape),
        (VMEM,) * 7,
        (both, ahead, beyond, inner, outer, geo, kap),
        aliases={0: 0},
        name="second_halo",
    )
    last_scratch = (
        in_vmem(FIELDS, REACH, rows, width),
        pltpu.SemaphoreType.DMA((rows // TILE,)),
    )
    result = pltpu.HBM(full_shape, jnp.float32)
    out = call(
        end_low_kernel,
        result,
        (VMEM,) * 3,
        (ahead, both, kap),
        scratch=last_scratch,
        cost=0.5,
        name="end_low",
    )
    out = call(
        last_high_kernel,
        result,
        (VMEM,) * 5 + (HBM,),
        (ahead, both, above2, high, kap, out),
        scratch=last_scratch,
        aliases={5: 0},
        cost=0.5,
        name="last_high",
    )
    return call(
        last_low_kernel,
        result,
        (VMEM,) * 5 + (HBM,),
        (ahead, both, below2, low, kap, out),
        scratch=last_scratch,
        aliases={5: 0},
        name="last_low",
    )


def solution(mesh):
    placed = (P(None, "rad", None, "lon"), P(None, "rad", None, "lon"), P("rad"))
    return jax.shard_map(
        on_device,
        mesh=mesh,
        in_specs=placed,
        out_specs=P(None, "rad", None, "lon"),
        check_vma=False,
    )
```

```python
import functools
import math

import jax
import jax.numpy as jnp
import numpy as np
from jax import lax
from jax.experimental import pallas as pl
from jax.experimental.pallas import tpu as pltpu
from jax.sharding import PartitionSpec as P

first_coeffs = (0.8, -0.2, 4.0 / 105.0, -1.0 / 280.0)
second_coeffs = (-205.0 / 72.0, 1.6, -0.2, 8.0 / 315.0, -1.0 / 560.0)
time_step = 0.002
gamma_less_one = 0.4
radial_ratio = 3.0
FIELDS = 5
REACH = 4
TILE = 8
LANES = 128
GROUPS = LANES // (2 * REACH)
signs = (1.0, -1.0, -1.0, 1.0, 1.0)
first_whole = (672.0, -168.0, 32.0, -3.0)
second_whole = (8064.0, -1008.0, 128.0, -9.0)

level_first = tuple(radial_ratio * c for c in first_coeffs)
level_second = tuple(radial_ratio * radial_ratio * c for c in second_coeffs)

VMEM = pl.BlockSpec(memory_space=pltpu.VMEM)
HBM = pl.BlockSpec(memory_space=pltpu.HBM)


def in_vmem(*shape):
    return pltpu.VMEM(shape, jnp.float32)


def stencil_matrix(width):
    matrix = np.zeros((width, 2 * width), np.float32)
    for out in range(width):
        for k in range(1, REACH + 1):
            for sign in (1, -1):
                if 0 <= out + sign * k < width:
                    matrix[out + sign * k, out] = sign * first_whole[k - 1]
                    matrix[out + sign * k, width + out] = second_whole[k - 1]
    return jnp.asarray(matrix)


def geometry(rows, nlon, width):
    theta = (np.arange(rows) + 0.5) * (2.0 * math.pi / nlon)
    metric = 1.0 / np.sin(theta)
    table = np.stack([metric / 840.0, metric * metric / 5040.0, np.cos(theta) * metric])
    return jnp.asarray(np.broadcast_to(table[:, :, None], (3, rows, width)), jnp.float32)


def packed(tiles, lane):
    total = None
    for g, tile in enumerate(tiles):
        moved = pltpu.roll(tile, (REACH + 2 * REACH * g) % LANES, 1)
        if total is None:
            total = moved
        else:
            total = jnp.where(lane >= 2 * REACH * g, moved, total)
    return total


def across_level(center_wind, center_temper, halo, kappa, above):
    out = [[None] * REACH for _ in range(FIELDS)]
    for a in range(REACH):
        slopes = []
        for f in range(FIELDS):
            total = None
            for b in range(REACH):
                k = b + REACH - a if above else a + REACH - b
                if 1 <= k <= REACH:
                    c = level_first[k - 1] if above else -level_first[k - 1]
                    term = c * halo[f][b]
                    total = term if total is None else total + term
            slopes.append(total)
        curve = None
        for b in range(REACH):
            k = b + REACH - a if above else a + REACH - b
            if 1 <= k <= REACH:
                term = level_second[k] * halo[4][b]
                curve = term if curve is None else curve + term
        wind, temper = center_wind[a], center_temper[a]
        out[0][a] = -wind * slopes[0] - slopes[3]
        out[1][a] = -wind * slopes[1]
        out[2][a] = -wind * slopes[2]
        out[3][a] = -wind * slopes[3] - temper * slopes[0] - slopes[4]
        out[4][a] = -wind * slopes[4] - (gamma_less_one * temper) * slopes[3] + kappa[a] * curve
    return out


def high_kernel(
    levels, rows, state, kappa, high, kap, raw_kap, kappa_scalars, sems
):
    block = REACH * rows
    odd, _ = mirrored()
    start = jnp.where(odd == 1, 0, REACH)
    half, reads = block // 2, [(kappa, kappa_scalars)]
    for f in range(FIELDS):
        for part in range(2):
            at = pl.multiple_of((f * levels + start) * rows + part * half, TILE)
            reads.append((state.at[pl.ds(at, half)], high.at[pl.ds(f * block + part * half, half)]))
    copies = [pltpu.make_async_copy(*read, sems.at[i]) for i, read in enumerate(reads)]
    for copy in copies:
        copy.start()
    copies[0].wait()
    for i in range(REACH):
        row = pl.ds(FIELDS * block + i, 1)
        high[row, :] = jnp.full((1, LANES), kappa_scalars[start + i], jnp.float32)
        raw_kap[pl.ds(i, 1), :] = jnp.full((1, LANES), kappa_scalars[REACH - start + i], jnp.float32)
    for l in range(levels):
        value = kappa_scalars[jnp.where(odd == 1, levels - 1 - l, l)]
        kap[l] = jnp.full((TILE, LANES), value, jnp.float32)
    for copy in copies[1:]:
        copy.wait()


def low_kernel(levels, rows, state, raw_kap, low):
    block = REACH * rows
    odd, _ = mirrored()
    start = jnp.where(odd == 1, REACH, 0)
    for f in range(FIELDS):
        at = pl.multiple_of((f * levels + start) * rows, TILE)
        low[pl.ds(f * block, block), :] = state[pl.ds(at, block), :]
    low[pl.ds(FIELDS * block, REACH), :] = raw_kap[pl.ds(0, REACH), :]


def own_level(high, low, rows, f, l, odd):
    i = l % REACH
    at = (f * REACH + jnp.where(odd == 1, REACH - 1 - i, i)) * rows
    return (low if l < REACH else high), pl.multiple_of(at, TILE)


def edges_kernel(levels, rows, high, low, inner, outer, polar):
    odd, mirror = mirrored()
    packs = []
    for f in range(FIELDS):
        tiles = []
        for l in range(levels):
            side, at = own_level(high, low, rows, f, l, odd)
            tiles.append([side[pl.ds(at + t * TILE, TILE), :] for t in range(rows // TILE)])
            cap = side[pl.ds(at, REACH), :]
            polar[pl.ds((f * levels + l) * REACH, REACH), :] = mirror * cap if f == 3 else cap
        packs += [mirror * pack if f == 3 else pack for pack in packed(levels, rows, tiles)]
    store_packs(packs, inner, outer)


def mirrored():
    odd = lax.axis_index("lon") % 2
    return odd, jnp.where(odd == 1, -1.0, 1.0).astype(jnp.float32)


def bordered(at):
    last = lax.axis_size("rad") - 1
    here = lax.axis_index("rad")
    odd, _ = mirrored()
    from_first = jnp.where(odd == 1, last - here, here)
    return from_first > 0 if at == 0 else from_first < last


def share_of(at, factor):
    return jnp.where(bordered(at), factor, 0.0).astype(jnp.float32)


def lanes():
    return lax.broadcasted_iota(jnp.int32, (TILE, LANES), 1)


def packed(levels, rows, tiles):
    per = GROUPS // levels
    out = []
    for j in range(rows // TILE // per):
        total = None
        for g in range(GROUPS):
            moved = pltpu.roll(tiles[g % levels][j * per + g // levels], (REACH + 2 * REACH * g) % LANES, 1)
            total = moved if total is None else jnp.where(lanes() >= 2 * REACH * g, moved, total)
        out.append(total)
    return out


def store_packs(packs, inner, outer):
    first_half = lanes() % (2 * REACH) < REACH
    odd = lax.axis_index("lon") % 2 == 1
    for i in range(0, len(packs), 2):
        a, b = packs[i], packs[min(i + 1, len(packs) - 1)]
        at = pl.ds(i // 2 * TILE, TILE)
        east = jnp.where(first_half, a, pltpu.roll(b, REACH, 1))
        west = jnp.where(first_half, pltpu.roll(a, LANES - REACH, 1), b)
        inner[at, :] = jnp.where(odd, west, east)
        outer[at, :] = jnp.where(odd, east, west)


def load_packs(count, inner, outer):
    first_half = lanes() % (2 * REACH) < REACH
    odd = lax.axis_index("lon") % 2 == 1
    out = []
    for i in range(0, count, 2):
        at = pl.ds(i // 2 * TILE, TILE)
        before = jnp.where(odd, inner[at, :], outer[at, :])
        after = jnp.where(odd, outer[at, :], inner[at, :])
        out.append(jnp.where(first_half, before, pltpu.roll(after, REACH, 1)))
        out.append(jnp.where(first_half, pltpu.roll(before, LANES - REACH, 1), after))
    return out[:count]


def pieces_of(x):
    out = []
    for piece in range(3):
        out.append(x.astype(jnp.bfloat16))
        if piece < 2:
            x = x - out[-1].astype(jnp.float32)
    return out


def times_whole(pieces, m):
    total = None
    for piece in pieces:
        term = jnp.dot(piece, m, preferred_element_type=jnp.float32)
        total = term if total is None else total + term
    return total


def longitude_slopes(levels, rows, padded, matrix, dlon, elon):
    for f in range(FIELDS):
        x = padded[f, :, pl.ds(TILE, rows), :].reshape(levels * rows, LANES)
        whole = matrix[:, pl.ds(0, 2 * LANES if f == 4 else LANES)].astype(jnp.bfloat16)
        total = times_whole(pieces_of(x), whole)
        dlon[f] = total[:, :LANES].reshape(levels, rows, LANES)
        if f == 4:
            elon[...] = total[:, LANES:].reshape(levels, rows, LANES)


def groups_slope(pack, coeffs, sign):
    place = lanes() % (2 * REACH)
    total = None
    for k in range(1, REACH + 1):
        ahead = pltpu.roll(pack, LANES - k, 1)
        behind = pltpu.roll(pack, k, 1)
        from_after = (place < REACH) & (place >= REACH - k)
        from_before = (place >= REACH) & (place < REACH + k)
        term = jnp.where(from_after, coeffs[k - 1] * ahead, 0.0)
        term = jnp.where(from_before, (sign * coeffs[k - 1]) * behind, term)
        total = term if total is None else total + term
    return total


def add_halo(levels, rows, own, padded, polar, inner, outer, geo, kap, store):
    per = GROUPS // levels
    count = rows // TILE // per
    packs = load_packs(FIELDS * count, inner, outer)
    slopes = [groups_slope(pack, first_whole, -1.0) for pack in packs]
    bends = [groups_slope(pack, second_whole, 1.0) for pack in packs[4 * count :]]
    lane = lanes()
    at_side = (lane < REACH) | (lane >= LANES - REACH)
    row = lax.broadcasted_iota(jnp.int32, (TILE, LANES), 0)

    def by_row(coeffs, m):
        total = jnp.zeros((TILE, LANES), jnp.float32)
        for k in range(m + 1, REACH + 1):
            total = jnp.where(row == k - m - 1, coeffs[k - 1], total)
        return total

    first_rows = [by_row([-c for c in first_coeffs], m) for m in range(REACH)]
    second_rows = [by_row(second_coeffs[1:], m) for m in range(REACH)]
    for t in range(rows // TILE):
        j, u = divmod(t, per)
        here = pl.ds(t * TILE, TILE)
        metric = jnp.where(at_side, geo[0, here, :], 0.0)
        metric2 = jnp.where(at_side, geo[1, here, :], 0.0)
        for l in own:
            shift = (LANES - REACH - 2 * REACH * (u * levels + levels - 1 - l)) % LANES
            center = [padded[f, l, pl.ds((t + 1) * TILE, TILE), :] for f in range(FIELDS)]
            wlon, wrow, temper = center[1], center[2], center[4]
            slon = [metric * pltpu.roll(slopes[f * count + j], shift, 1) for f in range(FIELDS)]
            slon[3] = -slon[3]
            laplace = metric2 * pltpu.roll(bends[j], shift, 1)
            extra = [-wlon * slope for slope in slon]
            extra[1] = extra[1] - temper * slon[0] - slon[4]
            spread = slon[1]
            if t == 0:
                srow = []
                for f in range(FIELDS):
                    total = None
                    for m in range(REACH):
                        across = signs[f] * polar[pl.ds((f * levels + l) * REACH + m, 1), :]
                        term = first_rows[m] * across
                        total = term if total is None else total + term
                        if f == 4:
                            laplace = laplace + second_rows[m] * across
                    srow.append(total)
                extra = [e - wrow * slope for e, slope in zip(extra, srow)]
                extra[2] = extra[2] - temper * srow[0] - srow[4]
                spread = spread + srow[2]
            extra[0] = extra[0] - spread
            extra[4] = extra[4] - (gamma_less_one * temper) * spread + kap[l] * laplace
            for f in range(FIELDS):
                store(f, l, t * TILE, center[f], extra[f])


def interior(levels, rows, padded, dlon, elon, geo, kappa, store):
    def body(t, carry):
        r0 = pl.multiple_of(t * TILE, TILE)
        here = pl.ds(r0, TILE)
        metric = geo[0, here, :]
        metric2 = geo[1, here, :]
        curvature = geo[2, here, :]
        center = [[padded[f, l, pl.ds(r0 + TILE, TILE), :] for l in range(levels)] for f in range(FIELDS)]
        out = [[None] * levels for _ in range(FIELDS)]
        for l in range(levels):
            wlon, wrow, wlev, temper = (center[f][l] for f in (1, 2, 3, 4))
            slon, srow, slev = [], [], []
            for f in range(FIELDS):
                slon.append(metric * dlon[f, l, here, :])
                total = None
                for k in range(1, REACH + 1):
                    ahead = padded[f, l, pl.ds(r0 + TILE + k, TILE), :]
                    behind = padded[f, l, pl.ds(r0 + TILE - k, TILE), :]
                    term = first_coeffs[k - 1] * (ahead - behind)
                    total = term if total is None else total + term
                    if f == 4:
                        curve = second_coeffs[k] * (ahead + behind)
                        bend = curve if k == 1 else bend + curve
                srow.append(total)
                total = None
                for k in range(1, REACH + 1):
                    up = center[f][l + k] if l + k < levels else None
                    down = center[f][l - k] if l - k >= 0 else None
                    if up is not None and down is not None:
                        term = level_first[k - 1] * (up - down)
                    elif up is not None:
                        term = level_first[k - 1] * up
                    elif down is not None:
                        term = -level_first[k - 1] * down
                    else:
                        continue
                    total = term if total is None else total + term
                slev.append(total)
            lift = None
            for k in range(1, REACH + 1):
                near = [center[4][l + s * k] for s in (1, -1) if 0 <= l + s * k < levels]
                if near:
                    term = level_second[k] * (near[0] + near[1] if len(near) == 2 else near[0])
                    lift = term if lift is None else lift + term
            middle = second_coeffs[0]
            laplace = metric2 * (elon[l, here, :] + (5040.0 * middle) * temper) + bend
            laplace = laplace + (middle + level_second[0]) * temper + lift
            carried = [wlon * slon[f] + wrow * srow[f] + wlev * slev[f] for f in range(FIELDS)]
            spread = slon[1] + srow[2] + slev[3] + curvature * wrow
            out[0][l] = -carried[0] - spread
            out[1][l] = -carried[1] - temper * slon[0] - slon[4]
            out[2][l] = -carried[2] - temper * srow[0] - srow[4]
            out[3][l] = -carried[3] - temper * slev[0] - slev[4]
            out[4][l] = -carried[4] - (gamma_less_one * temper) * spread + kappa[l] * laplace
            for f in range(FIELDS):
                store(f, l, r0, out[f][l])
        return carry

    lax.fori_loop(0, rows // TILE, body, 0)


def first_kernel(levels, rows, high, low, beyond, matrix, geo, kap, padded, rate, dlon, elon):
    odd, mirror = mirrored()
    for f in range(FIELDS):
        for l in range(levels):
            side, at = own_level(high, low, rows, f, l, odd)
            whole = side[pl.ds(at, rows), :]
            after = beyond[f, jnp.where(odd == 1, levels - 1 - l, l)]
            if f == 3:
                whole, after = mirror * whole, mirror * after
            padded[f, l, pl.ds(0, TILE), :] = jnp.zeros((TILE, LANES), jnp.float32)
            padded[f, l, pl.ds(TILE, rows), :] = whole
            padded[f, l, pl.ds(TILE + rows, REACH), :] = after
    longitude_slopes(levels, rows, padded, matrix, dlon, elon)

    def store(f, l, r0, tendency):
        rate[f, l, pl.ds(r0, TILE), :] = tendency

    interior(levels, rows, padded, dlon, elon, geo, kap, store)


def first_halo_kernel(at, levels, rows, given, padded, polar, inner, outer, geo, kap, rate, side):
    def store(f, l, r0, value, extra):
        tendency = given[f, l, pl.ds(r0, TILE), :] + extra
        rate[f, l, pl.ds(r0, TILE), :] = tendency
        side[pl.ds((f * REACH + l - at) * rows + r0, TILE), :] = value + time_step * tendency

    own = range(at, at + REACH)
    add_halo(levels, rows, own, padded, polar, inner, outer, geo, kap, store)


def raw_tile(ref, rows, r0, odd, mirror):
    out = []
    for f in range(FIELDS):
        ats = [(f * REACH + jnp.where(odd == 1, REACH - 1 - b, b)) * rows + r0 for b in range(REACH)]
        out.append([ref[pl.ds(pl.multiple_of(at, TILE), TILE), :] for at in ats])
    out[3] = [mirror * v for v in out[3]]
    return out


def own_tile(ref, rows, r0):
    return [
        [ref[pl.ds((f * REACH + b) * rows + r0, TILE), :] for b in range(REACH)] for f in range(FIELDS)
    ]


def section_side(at, up, levels, rows, padded, rate, sent, kappa, full, ahead):
    odd, mirror = mirrored()
    there = share_of(at, 1.0)

    def body(t, carry):
        r0 = pl.multiple_of(t * TILE, TILE)
        here, inside = pl.ds(r0, TILE), pl.ds(r0 + TILE, TILE)
        halo = raw_tile(sent, rows, r0, odd, mirror)
        center = [[padded[f, at + a, inside, :] for a in range(REACH)] for f in range(FIELDS)]
        extra = across_level(center[3], center[4], halo, [kappa[at + a] for a in range(REACH)], up)
        for f in range(FIELDS):
            for a in range(REACH):
                total = rate[f, at + a, here, :] + there * extra[f][a]
                full[f, at + a, here, :] = total
                ahead[f, at + a, inside, :] = center[f][a] + time_step * total
        return carry

    lax.fori_loop(0, rows // TILE, body, 0)
    for f in range(FIELDS):
        for l in range(at, at + REACH):
            ahead[f, l, pl.ds(0, TILE), :] = jnp.zeros((TILE, LANES), jnp.float32)
            ahead[f, l, pl.ds(rows + TILE, REACH), :] = padded[f, l, pl.ds(rows + TILE, REACH), :]


def section_low_kernel(levels, rows, padded, rate, below, kappa, full, ahead):
    section_side(0, False, levels, rows, padded, rate, below, kappa, full, ahead)


def section_high_kernel(
    levels, rows, padded, rate, above, kappa, given1, given2, full, ahead, inner, outer, polar
):
    section_side(levels - REACH, True, levels, rows, padded, rate, above, kappa, full, ahead)
    packs = []
    for f in range(FIELDS):
        tiles = [[ahead[f, l, pl.ds((t + 1) * TILE, TILE), :] for t in range(rows // TILE)] for l in range(levels)]
        packs += packed(levels, rows, tiles)
        for l in range(levels):
            polar[pl.ds((f * levels + l) * REACH, REACH), :] = ahead[f, l, pl.ds(TILE, REACH), :]
    store_packs(packs, inner, outer)


def second_kernel(
    levels, rows, padded, matrix, geo, kap, full, start, below, above, both, low, high, dlon, elon
):
    longitude_slopes(levels, rows, padded, matrix, dlon, elon)

    def store(f, l, r0, tendency):
        at = pl.ds(r0, TILE)
        both[f, l, at, :] = (0.5 * time_step) * (full[f, l, at, :] + tendency)

    interior(levels, rows, padded, dlon, elon, geo, kap, store)
    tail = FIELDS * REACH * rows
    odd, mirror = mirrored()

    def body(t, carry):
        r0 = pl.multiple_of(t * TILE, TILE)
        for halo_ref, out, at, up in ((below, low, 0, True), (above, high, levels - REACH, False)):
            beyond = raw_tile(halo_ref, rows, r0, odd, mirror)
            mine = [
                [start[f, at + a, pl.ds(r0 + TILE, TILE), :] for a in range(REACH)] for f in range(FIELDS)
            ]
            kappas = [
                halo_ref[pl.ds(tail + jnp.where(odd == 1, REACH - 1 - a, a), 1), :] for a in range(REACH)
            ]
            there = share_of(at, time_step)
            extra = across_level(beyond[3], beyond[4], mine, kappas, up)
            for f in range(FIELDS):
                for a in range(REACH):
                    out[pl.ds((f * REACH + a) * rows + r0, TILE), :] = there * extra[f][a]
        return carry

    lax.fori_loop(0, rows // TILE, body, 0)


def second_halo_kernel(
    levels, rows, given, padded, polar, inner, outer, geo, kap, both
):
    def store(f, l, r0, value, extra):
        at = pl.ds(r0, TILE)
        both[f, l, at, :] = given[f, l, at, :] + (0.5 * time_step) * extra

    add_halo(levels, rows, range(levels), padded, polar, inner, outer, geo, kap, store)


def last_kernel(levels, rows, padded, both, below, above, more_low, more_high, kap, out, staged, sems):
    odd, mirror = mirrored()
    copies = []
    for t in range(rows // TILE):
        here, inside = pl.ds(t * TILE, TILE), pl.ds((t + 1) * TILE, TILE)
        for sent, more, at, up in ((below, more_low, 0, False), (above, more_high, levels - REACH, True)):
            halo, there = own_tile(sent, rows, t * TILE), own_tile(more, rows, t * TILE)
            halo = [[halo[f][b] + there[f][b] for b in range(REACH)] for f in range(FIELDS)]
            wind = [padded[3, at + a, inside, :] for a in range(REACH)]
            temper = [padded[4, at + a, inside, :] for a in range(REACH)]
            extra = across_level(wind, temper, halo, [kap[at + a] for a in range(REACH)], up)
            scale = share_of(at, 0.5 * time_step)
            for f in range(FIELDS):
                for a in range(REACH):
                    new = both[f, at + a, here, :] + scale * extra[f][a]
                    real = jnp.where(odd == 1, levels - 1 - at - a, at + a)
                    staged[f, real, here, :] = mirror * new if f == 3 else new
        copies.append(pltpu.make_async_copy(staged.at[:, :, here], out.at[:, :, here], sems.at[t]))
        copies[-1].start()
    for copy in copies:
        copy.wait()


def on_device(state, outer_rows, kappa):
    levels, rows, width = state.shape[1:]
    ring, depth = lax.axis_size("lon"), lax.axis_size("rad")
    assert ring % 4 == 0 and width == LANES and levels == 2 * REACH and GROUPS % levels == 0
    assert rows % (TILE * (GROUPS // levels)) == 0
    matrix = stencil_matrix(width)
    geo = geometry(rows, width * ring, width)
    halo_rows = FIELDS * REACH * rows
    packs = -(-(FIELDS * levels * rows // TILE // GROUPS) // 2) * TILE
    pad_shape = (FIELDS, levels, rows + 2 * TILE, width)
    full_shape = (FIELDS, levels, rows, width)

    def call(kernel, out_shape, in_specs, args, scratch=(), aliases=None, cost=1.0, name=None):
        spaces = {id(VMEM): pltpu.VMEM, id(HBM): pltpu.HBM}
        args = [pltpu.with_memory_space_constraint(x, spaces[id(s)]) for s, x in zip(in_specs, args)]
        return pl.pallas_call(
            functools.partial(kernel, levels, rows),
            out_shape=out_shape,
            in_specs=list(in_specs),
            out_specs=jax.tree.map(lambda o: HBM if o.memory_space is pltpu.HBM else VMEM, out_shape),
            scratch_shapes=list(scratch),
            input_output_aliases=aliases or {},
            cost_estimate=pl.CostEstimate(flops=0, bytes_accessed=int(cost * 3.69e6), transcendentals=0),
            compiler_params=pltpu.CompilerParams(vmem_limit_bytes=16 * 2**20),
            name=name,
        )(*args)

    pairs = [(i, i + 1) for i in range(0, ring, 2)]
    swap_inner = pairs + [(b, a) for a, b in pairs]
    pairs = [(i, (i + 1) % ring) for i in range(1, ring, 2)]
    swap_outer = pairs + [(b, a) for a, b in pairs]
    half = [(i, (i + ring // 2) % ring) for i in range(ring)]
    onward = []
    for lon in range(0, ring, 2):
        even, odd = lon * depth, (lon + 1) * depth
        onward += [(even + i, even + i + 1) for i in range(depth - 1)] + [(even + depth - 1, odd + depth - 1)]
        onward += [(odd + i + 1, odd + i) for i in range(depth - 1)] + [(odd, even)]
    back = [(b, a) for a, b in onward]
    axes = ("lon", "rad")

    def around(inner, outer, polar):
        inner = lax.ppermute(inner, "lon", swap_inner)
        outer = lax.ppermute(outer, "lon", swap_outer)
        return inner, outer, lax.ppermute(polar, "lon", half)

    edge_shapes = [in_vmem(packs, width), in_vmem(packs, width), in_vmem(FIELDS * levels * REACH, width)]
    payload = in_vmem(halo_rows + TILE, width)
    flat = state.reshape(-1, width)
    high, kap, raw_kap = call(
        high_kernel,
        [payload, in_vmem(levels, TILE, width), in_vmem(TILE, width)],
        (HBM,) * 2,
        (flat, kappa),
        scratch=(pltpu.SMEM(kappa.shape, jnp.float32), pltpu.SemaphoreType.DMA((2 * FIELDS + 1,))),
        name="high",
    )
    below = lax.ppermute(high, axes, onward)
    low = call(low_kernel, payload, (VMEM,) * 2, (flat, raw_kap), cost=0.2, name="low")
    above = lax.ppermute(low, axes, back)
    edges = call(edges_kernel, edge_shapes, (VMEM,) * 2, (high, low), cost=0.4, name="edges")
    inner, outer, beyond = around(*edges)
    lon_scratch = (in_vmem(*full_shape), in_vmem(*full_shape[1:]))
    side = in_vmem(halo_rows, width)
    padded, rate = call(
        first_kernel,
        [in_vmem(*pad_shape), in_vmem(*full_shape)],
        (VMEM,) * 6,
        (high, low, outer_rows, matrix, geo, kap),
        scratch=lon_scratch,
        cost=2.0,
        name="first",
    )

    def first_halo(rate, at):
        return call(
            functools.partial(first_halo_kernel, at),
            [in_vmem(*full_shape), side],
            (VMEM,) * 7,
            (rate, padded, beyond, inner, outer, geo, kap),
            aliases={0: 0},
            cost=0.6,
            name="first_halo",
        )

    rate, high = first_halo(rate, levels - REACH)
    below2 = lax.ppermute(high, axes, onward)
    rate, low = first_halo(rate, 0)
    above2 = lax.ppermute(low, axes, back)
    section_shapes = [in_vmem(*full_shape), in_vmem(*pad_shape)]
    full, ahead = call(
        section_low_kernel,
        section_shapes,
        (VMEM,) * 4,
        (padded, rate, below, kap),
        cost=0.4,
        name="section_low",
    )
    full, ahead, *edges = call(
        section_high_kernel,
        [*section_shapes, *edge_shapes],
        (VMEM,) * 6,
        (padded, rate, above, kap, full, ahead),
        aliases={4: 0, 5: 1},
        cost=0.5,
        name="section_high",
    )
    inner, outer, beyond = around(*edges)
    both, low, high = call(
        second_kernel,
        [in_vmem(*full_shape), side, side],
        (VMEM,) * 8,
        (ahead, matrix, geo, kap, full, padded, below, above),
        scratch=lon_scratch,
        cost=2.5,
        name="second",
    )
    both = call(
        second_halo_kernel,
        in_vmem(*full_shape),
        (VMEM,) * 7,
        (both, ahead, beyond, inner, outer, geo, kap),
        aliases={0: 0},
        name="second_halo",
    )
    return call(
        last_kernel,
        pltpu.HBM(full_shape, jnp.float32),
        (VMEM,) * 7,
        (ahead, both, below2, above2, low, high, kap),
        scratch=(in_vmem(*full_shape), pltpu.SemaphoreType.DMA((rows // TILE,))),
        name="last",
    )


def solution(mesh):
    placed = (P(None, "rad", None, "lon"), P(None, "rad", None, "lon"), P("rad"))
    return jax.shard_map(
        on_device,
        mesh=mesh,
        in_specs=placed,
        out_specs=P(None, "rad", None, "lon"),
        check_vma=False,
    )
```

```python
import functools
import math

import jax
import jax.numpy as jnp
import numpy as np
from jax import lax
from jax.experimental import pallas as pl
from jax.experimental.pallas import tpu as pltpu
from jax.sharding import PartitionSpec as P

first_coeffs = (0.8, -0.2, 4.0 / 105.0, -1.0 / 280.0)
second_coeffs = (-205.0 / 72.0, 1.6, -0.2, 8.0 / 315.0, -1.0 / 560.0)
time_step = 0.002
gamma_less_one = 0.4
radial_ratio = 3.0
FIELDS = 5
REACH = 4
TILE = 8
LANES = 128
GROUPS = LANES // (2 * REACH)
signs = (1.0, -1.0, -1.0, 1.0, 1.0)
first_whole = (672.0, -168.0, 32.0, -3.0)
second_whole = (8064.0, -1008.0, 128.0, -9.0)

level_first = tuple(radial_ratio * c for c in first_coeffs)
level_second = tuple(radial_ratio * radial_ratio * c for c in second_coeffs)

VMEM = pl.BlockSpec(memory_space=pltpu.VMEM)
HBM = pl.BlockSpec(memory_space=pltpu.HBM)


def in_vmem(*shape):
    return pltpu.VMEM(shape, jnp.float32)


def stencil_matrix(width):
    matrix = np.zeros((width, 2 * width), np.float32)
    for out in range(width):
        for k in range(1, REACH + 1):
            for sign in (1, -1):
                if 0 <= out + sign * k < width:
                    matrix[out + sign * k, out] = sign * first_whole[k - 1]
                    matrix[out + sign * k, width + out] = second_whole[k - 1]
    return jnp.asarray(matrix)


def geometry(rows, nlon, width):
    theta = (np.arange(rows) + 0.5) * (2.0 * math.pi / nlon)
    metric = 1.0 / np.sin(theta)
    table = np.stack([metric / 840.0, metric * metric / 5040.0, np.cos(theta) * metric])
    return jnp.asarray(np.broadcast_to(table[:, :, None], (3, rows, width)), jnp.float32)


def packed(tiles, lane):
    total = None
    for g, tile in enumerate(tiles):
        moved = pltpu.roll(tile, (REACH + 2 * REACH * g) % LANES, 1)
        if total is None:
            total = moved
        else:
            total = jnp.where(lane >= 2 * REACH * g, moved, total)
    return total


def across_level(center_wind, center_temper, halo, kappa, above):
    out = [[None] * REACH for _ in range(FIELDS)]
    for a in range(REACH):
        slopes = []
        for f in range(FIELDS):
            total = None
            for b in range(REACH):
                k = b + REACH - a if above else a + REACH - b
                if 1 <= k <= REACH:
                    c = level_first[k - 1] if above else -level_first[k - 1]
                    term = c * halo[f][b]
                    total = term if total is None else total + term
            slopes.append(total)
        curve = None
        for b in range(REACH):
            k = b + REACH - a if above else a + REACH - b
            if 1 <= k <= REACH:
                term = level_second[k] * halo[4][b]
                curve = term if curve is None else curve + term
        wind, temper = center_wind[a], center_temper[a]
        out[0][a] = -wind * slopes[0] - slopes[3]
        out[1][a] = -wind * slopes[1]
        out[2][a] = -wind * slopes[2]
        out[3][a] = -wind * slopes[3] - temper * slopes[0] - slopes[4]
        out[4][a] = -wind * slopes[4] - (gamma_less_one * temper) * slopes[3] + kappa[a] * curve
    return out


def high_kernel(
    levels, rows, state, kappa, high, kap, raw_kap, kappa_scalars, sems
):
    block = REACH * rows
    odd, _ = mirrored()
    start = jnp.where(odd == 1, 0, REACH)
    half, reads = block // 2, [(kappa, kappa_scalars)]
    for f in range(FIELDS):
        for part in range(2):
            at = pl.multiple_of((f * levels + start) * rows + part * half, TILE)
            reads.append((state.at[pl.ds(at, half)], high.at[pl.ds(f * block + part * half, half)]))
    copies = [pltpu.make_async_copy(*read, sems.at[i]) for i, read in enumerate(reads)]
    for copy in copies:
        copy.start()
    copies[0].wait()
    for i in range(REACH):
        row = pl.ds(FIELDS * block + i, 1)
        high[row, :] = jnp.full((1, LANES), kappa_scalars[start + i], jnp.float32)
        raw_kap[pl.ds(i, 1), :] = jnp.full((1, LANES), kappa_scalars[REACH - start + i], jnp.float32)
    for l in range(levels):
        value = kappa_scalars[jnp.where(odd == 1, levels - 1 - l, l)]
        kap[l] = jnp.full((TILE, LANES), value, jnp.float32)
    for copy in copies[1:]:
        copy.wait()


def low_kernel(levels, rows, state, raw_kap, low):
    block = REACH * rows
    odd, _ = mirrored()
    start = jnp.where(odd == 1, REACH, 0)
    for f in range(FIELDS):
        at = pl.multiple_of((f * levels + start) * rows, TILE)
        low[pl.ds(f * block, block), :] = state[pl.ds(at, block), :]
    low[pl.ds(FIELDS * block, REACH), :] = raw_kap[pl.ds(0, REACH), :]


def own_level(high, low, rows, f, l, odd):
    i = l % REACH
    at = (f * REACH + jnp.where(odd == 1, REACH - 1 - i, i)) * rows
    return (low if l < REACH else high), pl.multiple_of(at, TILE)


def edges_kernel(levels, rows, high, low, inner, outer, polar):
    odd, mirror = mirrored()
    packs = []
    for f in range(FIELDS):
        tiles = []
        for l in range(levels):
            side, at = own_level(high, low, rows, f, l, odd)
            tiles.append([side[pl.ds(at + t * TILE, TILE), :] for t in range(rows // TILE)])
            cap = side[pl.ds(at, REACH), :]
            polar[pl.ds((f * levels + l) * REACH, REACH), :] = mirror * cap if f == 3 else cap
        packs += [mirror * pack if f == 3 else pack for pack in packed(levels, rows, tiles)]
    store_packs(packs, inner, outer)


def mirrored():
    odd = lax.axis_index("lon") % 2
    return odd, jnp.where(odd == 1, -1.0, 1.0).astype(jnp.float32)


def bordered(at):
    last = lax.axis_size("rad") - 1
    here = lax.axis_index("rad")
    odd, _ = mirrored()
    from_first = jnp.where(odd == 1, last - here, here)
    return from_first > 0 if at == 0 else from_first < last


def share_of(at, factor):
    return jnp.where(bordered(at), factor, 0.0).astype(jnp.float32)


def lanes():
    return lax.broadcasted_iota(jnp.int32, (TILE, LANES), 1)


def packed(levels, rows, tiles):
    per = GROUPS // levels
    out = []
    for j in range(rows // TILE // per):
        total = None
        for g in range(GROUPS):
            moved = pltpu.roll(tiles[g % levels][j * per + g // levels], (REACH + 2 * REACH * g) % LANES, 1)
            total = moved if total is None else jnp.where(lanes() >= 2 * REACH * g, moved, total)
        out.append(total)
    return out


def store_packs(packs, inner, outer):
    first_half = lanes() % (2 * REACH) < REACH
    odd = lax.axis_index("lon") % 2 == 1
    for i in range(0, len(packs), 2):
        a, b = packs[i], packs[min(i + 1, len(packs) - 1)]
        at = pl.ds(i // 2 * TILE, TILE)
        east = jnp.where(first_half, a, pltpu.roll(b, REACH, 1))
        west = jnp.where(first_half, pltpu.roll(a, LANES - REACH, 1), b)
        inner[at, :] = jnp.where(odd, west, east)
        outer[at, :] = jnp.where(odd, east, west)


def load_packs(count, inner, outer):
    first_half = lanes() % (2 * REACH) < REACH
    odd = lax.axis_index("lon") % 2 == 1
    out = []
    for i in range(0, count, 2):
        at = pl.ds(i // 2 * TILE, TILE)
        before = jnp.where(odd, inner[at, :], outer[at, :])
        after = jnp.where(odd, outer[at, :], inner[at, :])
        out.append(jnp.where(first_half, before, pltpu.roll(after, REACH, 1)))
        out.append(jnp.where(first_half, pltpu.roll(before, LANES - REACH, 1), after))
    return out[:count]


def pieces_of(x):
    out = []
    for piece in range(3):
        out.append(x.astype(jnp.bfloat16))
        if piece < 2:
            x = x - out[-1].astype(jnp.float32)
    return out


def times_whole(pieces, m):
    total = None
    for piece in pieces:
        term = jnp.dot(piece, m, preferred_element_type=jnp.float32)
        total = term if total is None else total + term
    return total


def longitude_slopes(levels, rows, padded, matrix, dlon, elon):
    for f in range(FIELDS):
        x = padded[f, :, pl.ds(TILE, rows), :].reshape(levels * rows, LANES)
        whole = matrix[:, pl.ds(0, 2 * LANES if f == 4 else LANES)].astype(jnp.bfloat16)
        total = times_whole(pieces_of(x), whole)
        dlon[f] = total[:, :LANES].reshape(levels, rows, LANES)
        if f == 4:
            elon[...] = total[:, LANES:].reshape(levels, rows, LANES)


def groups_slope(pack, coeffs, sign):
    place = lanes() % (2 * REACH)
    total = None
    for k in range(1, REACH + 1):
        ahead = pltpu.roll(pack, LANES - k, 1)
        behind = pltpu.roll(pack, k, 1)
        from_after = (place < REACH) & (place >= REACH - k)
        from_before = (place >= REACH) & (place < REACH + k)
        term = jnp.where(from_after, coeffs[k - 1] * ahead, 0.0)
        term = jnp.where(from_before, (sign * coeffs[k - 1]) * behind, term)
        total = term if total is None else total + term
    return total


def add_halo(levels, rows, own, padded, polar, inner, outer, geo, kap, store):
    per = GROUPS // levels
    count = rows // TILE // per
    packs = load_packs(FIELDS * count, inner, outer)
    slopes = [groups_slope(pack, first_whole, -1.0) for pack in packs]
    bends = [groups_slope(pack, second_whole, 1.0) for pack in packs[4 * count :]]
    lane = lanes()
    at_side = (lane < REACH) | (lane >= LANES - REACH)
    row = lax.broadcasted_iota(jnp.int32, (TILE, LANES), 0)

    def by_row(coeffs, m):
        total = jnp.zeros((TILE, LANES), jnp.float32)
        for k in range(m + 1, REACH + 1):
            total = jnp.where(row == k - m - 1, coeffs[k - 1], total)
        return total

    first_rows = [by_row([-c for c in first_coeffs], m) for m in range(REACH)]
    second_rows = [by_row(second_coeffs[1:], m) for m in range(REACH)]
    for t in range(rows // TILE):
        j, u = divmod(t, per)
        here = pl.ds(t * TILE, TILE)
        metric = jnp.where(at_side, geo[0, here, :], 0.0)
        metric2 = jnp.where(at_side, geo[1, here, :], 0.0)
        for l in own:
            shift = (LANES - REACH - 2 * REACH * (u * levels + levels - 1 - l)) % LANES
            center = [padded[f, l, pl.ds((t + 1) * TILE, TILE), :] for f in range(FIELDS)]
            wlon, wrow, temper = center[1], center[2], center[4]
            slon = [metric * pltpu.roll(slopes[f * count + j], shift, 1) for f in range(FIELDS)]
            slon[3] = -slon[3]
            laplace = metric2 * pltpu.roll(bends[j], shift, 1)
            extra = [-wlon * slope for slope in slon]
            extra[1] = extra[1] - temper * slon[0] - slon[4]
            spread = slon[1]
            if t == 0:
                srow = []
                for f in range(FIELDS):
                    total = None
                    for m in range(REACH):
                        across = signs[f] * polar[pl.ds((f * levels + l) * REACH + m, 1), :]
                        term = first_rows[m] * across
                        total = term if total is None else total + term
                        if f == 4:
                            laplace = laplace + second_rows[m] * across
                    srow.append(total)
                extra = [e - wrow * slope for e, slope in zip(extra, srow)]
                extra[2] = extra[2] - temper * srow[0] - srow[4]
                spread = spread + srow[2]
            extra[0] = extra[0] - spread
            extra[4] = extra[4] - (gamma_less_one * temper) * spread + kap[l] * laplace
            for f in range(FIELDS):
                store(f, l, t * TILE, center[f], extra[f])


def interior(levels, rows, padded, dlon, elon, geo, kappa, store):
    def body(t, carry):
        r0 = pl.multiple_of(t * TILE, TILE)
        here = pl.ds(r0, TILE)
        metric = geo[0, here, :]
        metric2 = geo[1, here, :]
        curvature = geo[2, here, :]
        center = [[padded[f, l, pl.ds(r0 + TILE, TILE), :] for l in range(levels)] for f in range(FIELDS)]
        out = [[None] * levels for _ in range(FIELDS)]
        for l in range(levels):
            wlon, wrow, wlev, temper = (center[f][l] for f in (1, 2, 3, 4))
            slon, srow, slev = [], [], []
            for f in range(FIELDS):
                slon.append(metric * dlon[f, l, here, :])
                total = None
                for k in range(1, REACH + 1):
                    ahead = padded[f, l, pl.ds(r0 + TILE + k, TILE), :]
                    behind = padded[f, l, pl.ds(r0 + TILE - k, TILE), :]
                    term = first_coeffs[k - 1] * (ahead - behind)
                    total = term if total is None else total + term
                    if f == 4:
                        curve = second_coeffs[k] * (ahead + behind)
                        bend = curve if k == 1 else bend + curve
                srow.append(total)
                total = None
                for k in range(1, REACH + 1):
                    up = center[f][l + k] if l + k < levels else None
                    down = center[f][l - k] if l - k >= 0 else None
                    if up is not None and down is not None:
                        term = level_first[k - 1] * (up - down)
                    elif up is not None:
                        term = level_first[k - 1] * up
                    elif down is not None:
                        term = -level_first[k - 1] * down
                    else:
                        continue
                    total = term if total is None else total + term
                slev.append(total)
            lift = None
            for k in range(1, REACH + 1):
                near = [center[4][l + s * k] for s in (1, -1) if 0 <= l + s * k < levels]
                if near:
                    term = level_second[k] * (near[0] + near[1] if len(near) == 2 else near[0])
                    lift = term if lift is None else lift + term
            middle = second_coeffs[0]
            laplace = metric2 * (elon[l, here, :] + (5040.0 * middle) * temper) + bend
            laplace = laplace + (middle + level_second[0]) * temper + lift
            carried = [wlon * slon[f] + wrow * srow[f] + wlev * slev[f] for f in range(FIELDS)]
            spread = slon[1] + srow[2] + slev[3] + curvature * wrow
            out[0][l] = -carried[0] - spread
            out[1][l] = -carried[1] - temper * slon[0] - slon[4]
            out[2][l] = -carried[2] - temper * srow[0] - srow[4]
            out[3][l] = -carried[3] - temper * slev[0] - slev[4]
            out[4][l] = -carried[4] - (gamma_less_one * temper) * spread + kappa[l] * laplace
            for f in range(FIELDS):
                store(f, l, r0, out[f][l])
        return carry

    lax.fori_loop(0, rows // TILE, body, 0)


def first_kernel(levels, rows, high, low, beyond, matrix, geo, kap, padded, rate, dlon, elon):
    odd, mirror = mirrored()
    for f in range(FIELDS):
        for l in range(levels):
            side, at = own_level(high, low, rows, f, l, odd)
            whole = side[pl.ds(at, rows), :]
            after = beyond[f, jnp.where(odd == 1, levels - 1 - l, l)]
            if f == 3:
                whole, after = mirror * whole, mirror * after
            padded[f, l, pl.ds(0, TILE), :] = jnp.zeros((TILE, LANES), jnp.float32)
            padded[f, l, pl.ds(TILE, rows), :] = whole
            padded[f, l, pl.ds(TILE + rows, REACH), :] = after
    longitude_slopes(levels, rows, padded, matrix, dlon, elon)

    def store(f, l, r0, tendency):
        rate[f, l, pl.ds(r0, TILE), :] = tendency

    interior(levels, rows, padded, dlon, elon, geo, kap, store)


def first_halo_kernel(at, levels, rows, given, padded, polar, inner, outer, geo, kap, rate, side):
    def store(f, l, r0, value, extra):
        tendency = given[f, l, pl.ds(r0, TILE), :] + extra
        rate[f, l, pl.ds(r0, TILE), :] = tendency
        side[pl.ds((f * REACH + l - at) * rows + r0, TILE), :] = value + time_step * tendency

    own = range(at, at + REACH)
    add_halo(levels, rows, own, padded, polar, inner, outer, geo, kap, store)


def raw_tile(ref, rows, r0, odd, mirror):
    out = []
    for f in range(FIELDS):
        ats = [(f * REACH + jnp.where(odd == 1, REACH - 1 - b, b)) * rows + r0 for b in range(REACH)]
        out.append([ref[pl.ds(pl.multiple_of(at, TILE), TILE), :] for at in ats])
    out[3] = [mirror * v for v in out[3]]
    return out


def own_tile(ref, rows, r0):
    return [
        [ref[pl.ds((f * REACH + b) * rows + r0, TILE), :] for b in range(REACH)] for f in range(FIELDS)
    ]


def section_side(at, up, levels, rows, padded, rate, sent, kappa, full, ahead):
    odd, mirror = mirrored()
    there = share_of(at, 1.0)

    def body(t, carry):
        r0 = pl.multiple_of(t * TILE, TILE)
        here, inside = pl.ds(r0, TILE), pl.ds(r0 + TILE, TILE)
        halo = raw_tile(sent, rows, r0, odd, mirror)
        center = [[padded[f, at + a, inside, :] for a in range(REACH)] for f in range(FIELDS)]
        extra = across_level(center[3], center[4], halo, [kappa[at + a] for a in range(REACH)], up)
        for f in range(FIELDS):
            for a in range(REACH):
                total = rate[f, at + a, here, :] + there * extra[f][a]
                full[f, at + a, here, :] = total
                ahead[f, at + a, inside, :] = center[f][a] + time_step * total
        return carry

    lax.fori_loop(0, rows // TILE, body, 0)
    for f in range(FIELDS):
        for l in range(at, at + REACH):
            ahead[f, l, pl.ds(0, TILE), :] = jnp.zeros((TILE, LANES), jnp.float32)
            ahead[f, l, pl.ds(rows + TILE, REACH), :] = padded[f, l, pl.ds(rows + TILE, REACH), :]


def section_low_kernel(levels, rows, padded, rate, below, kappa, full, ahead):
    section_side(0, False, levels, rows, padded, rate, below, kappa, full, ahead)


def section_high_kernel(
    levels, rows, padded, rate, above, kappa, given1, given2, full, ahead, inner, outer, polar
):
    section_side(levels - REACH, True, levels, rows, padded, rate, above, kappa, full, ahead)
    packs = []
    for f in range(FIELDS):
        tiles = [[ahead[f, l, pl.ds((t + 1) * TILE, TILE), :] for t in range(rows // TILE)] for l in range(levels)]
        packs += packed(levels, rows, tiles)
        for l in range(levels):
            polar[pl.ds((f * levels + l) * REACH, REACH), :] = ahead[f, l, pl.ds(TILE, REACH), :]
    store_packs(packs, inner, outer)


def second_kernel(
    levels, rows, padded, matrix, geo, kap, full, start, below, above, both, low, high, dlon, elon
):
    longitude_slopes(levels, rows, padded, matrix, dlon, elon)

    def store(f, l, r0, tendency):
        at = pl.ds(r0, TILE)
        both[f, l, at, :] = (0.5 * time_step) * (full[f, l, at, :] + tendency)

    interior(levels, rows, padded, dlon, elon, geo, kap, store)
    tail = FIELDS * REACH * rows
    odd, mirror = mirrored()

    def body(t, carry):
        r0 = pl.multiple_of(t * TILE, TILE)
        for halo_ref, out, at, up in ((below, low, 0, True), (above, high, levels - REACH, False)):
            beyond = raw_tile(halo_ref, rows, r0, odd, mirror)
            mine = [
                [start[f, at + a, pl.ds(r0 + TILE, TILE), :] for a in range(REACH)] for f in range(FIELDS)
            ]
            kappas = [
                halo_ref[pl.ds(tail + jnp.where(odd == 1, REACH - 1 - a, a), 1), :] for a in range(REACH)
            ]
            there = share_of(at, time_step)
            extra = across_level(beyond[3], beyond[4], mine, kappas, up)
            for f in range(FIELDS):
                for a in range(REACH):
                    out[pl.ds((f * REACH + a) * rows + r0, TILE), :] = there * extra[f][a]
        return carry

    lax.fori_loop(0, rows // TILE, body, 0)


def second_halo_kernel(
    levels, rows, given, padded, polar, inner, outer, geo, kap, both
):
    def store(f, l, r0, value, extra):
        at = pl.ds(r0, TILE)
        both[f, l, at, :] = given[f, l, at, :] + (0.5 * time_step) * extra

    add_halo(levels, rows, range(levels), padded, polar, inner, outer, geo, kap, store)


def side_copy(at, t, levels, odd, out, staged, sems):
    real, here = jnp.where(odd == 1, levels - at - REACH, at), pl.ds(t * TILE, TILE)
    there = (slice(None), pl.ds(real, REACH), here)
    return pltpu.make_async_copy(staged.at[there], out.at[there], sems.at[at // REACH, t])


def write_tile(at, t, share, levels, padded, both, kap, staged):
    odd, mirror = mirrored()
    here, inside = pl.ds(t * TILE, TILE), pl.ds((t + 1) * TILE, TILE)
    extra = None
    if share is not None:
        wind = [padded[3, at + a, inside, :] for a in range(REACH)]
        temper = [padded[4, at + a, inside, :] for a in range(REACH)]
        extra = share(t * TILE, wind, temper, [kap[at + a] for a in range(REACH)])
    for f in range(FIELDS):
        for a in range(REACH):
            new = both[f, at + a, here, :]
            if extra is not None:
                new = new + (0.5 * time_step) * extra[f][a]
            real = jnp.where(odd == 1, levels - 1 - at - a, at + a)
            staged[f, real, here, :] = mirror * new if f == 3 else new


def end_kernel(levels, rows, padded, both, kap, out, staged, sems):
    odd, _ = mirrored()
    for at in (0, levels - REACH):

        @pl.when(jnp.logical_not(bordered(at)))
        def _():
            copies = [side_copy(at, t, levels, odd, out, staged, sems) for t in range(rows // TILE)]
            for t, copy in enumerate(copies):
                write_tile(at, t, None, levels, padded, both, kap, staged)
                copy.start()
            for copy in copies:
                copy.wait()


def last_kernel(
    levels, rows, padded, both, below, above, more_low, more_high, kap, given, out, staged, sems
):
    odd, _ = mirrored()

    def share_by(sent, more, up):
        def share(r0, wind, temper, kappa):
            halo, there = own_tile(sent, rows, r0), own_tile(more, rows, r0)
            halo = [[halo[f][b] + there[f][b] for b in range(REACH)] for f in range(FIELDS)]
            return across_level(wind, temper, halo, kappa, up)

        return share

    sides = (
        (0, share_by(below, more_low, False)),
        (levels - REACH, share_by(above, more_high, True)),
    )
    for at, share in sides:

        @pl.when(bordered(at))
        def _():
            for t in range(rows // TILE):
                write_tile(at, t, share, levels, padded, both, kap, staged)
                side_copy(at, t, levels, odd, out, staged, sems).start()

    for at, _ in sides:

        @pl.when(bordered(at))
        def _():
            for t in range(rows // TILE):
                side_copy(at, t, levels, odd, out, staged, sems).wait()


def on_device(state, outer_rows, kappa):
    levels, rows, width = state.shape[1:]
    ring, depth = lax.axis_size("lon"), lax.axis_size("rad")
    assert ring % 4 == 0 and width == LANES and levels == 2 * REACH and GROUPS % levels == 0
    assert rows % (TILE * (GROUPS // levels)) == 0
    matrix = stencil_matrix(width)
    geo = geometry(rows, width * ring, width)
    halo_rows = FIELDS * REACH * rows
    packs = -(-(FIELDS * levels * rows // TILE // GROUPS) // 2) * TILE
    pad_shape = (FIELDS, levels, rows + 2 * TILE, width)
    full_shape = (FIELDS, levels, rows, width)

    def call(kernel, out_shape, in_specs, args, scratch=(), aliases=None, cost=1.0, name=None):
        spaces = {id(VMEM): pltpu.VMEM, id(HBM): pltpu.HBM}
        args = [pltpu.with_memory_space_constraint(x, spaces[id(s)]) for s, x in zip(in_specs, args)]
        return pl.pallas_call(
            functools.partial(kernel, levels, rows),
            out_shape=out_shape,
            in_specs=list(in_specs),
            out_specs=jax.tree.map(lambda o: HBM if o.memory_space is pltpu.HBM else VMEM, out_shape),
            scratch_shapes=list(scratch),
            input_output_aliases=aliases or {},
            cost_estimate=pl.CostEstimate(flops=0, bytes_accessed=int(cost * 3.69e6), transcendentals=0),
            compiler_params=pltpu.CompilerParams(vmem_limit_bytes=16 * 2**20),
            name=name,
        )(*args)

    pairs = [(i, i + 1) for i in range(0, ring, 2)]
    swap_inner = pairs + [(b, a) for a, b in pairs]
    pairs = [(i, (i + 1) % ring) for i in range(1, ring, 2)]
    swap_outer = pairs + [(b, a) for a, b in pairs]
    half = [(i, (i + ring // 2) % ring) for i in range(ring)]
    onward = []
    for lon in range(0, ring, 2):
        even, odd = lon * depth, (lon + 1) * depth
        onward += [(even + i, even + i + 1) for i in range(depth - 1)] + [(even + depth - 1, odd + depth - 1)]
        onward += [(odd + i + 1, odd + i) for i in range(depth - 1)] + [(odd, even)]
    back = [(b, a) for a, b in onward]
    axes = ("lon", "rad")

    def around(inner, outer, polar):
        inner = lax.ppermute(inner, "lon", swap_inner)
        outer = lax.ppermute(outer, "lon", swap_outer)
        return inner, outer, lax.ppermute(polar, "lon", half)

    edge_shapes = [in_vmem(packs, width), in_vmem(packs, width), in_vmem(FIELDS * levels * REACH, width)]
    payload = in_vmem(halo_rows + TILE, width)
    flat = state.reshape(-1, width)
    high, kap, raw_kap = call(
        high_kernel,
        [payload, in_vmem(levels, TILE, width), in_vmem(TILE, width)],
        (HBM,) * 2,
        (flat, kappa),
        scratch=(pltpu.SMEM(kappa.shape, jnp.float32), pltpu.SemaphoreType.DMA((2 * FIELDS + 1,))),
        name="high",
    )
    below = lax.ppermute(high, axes, onward)
    low = call(low_kernel, payload, (VMEM,) * 2, (flat, raw_kap), cost=0.2, name="low")
    above = lax.ppermute(low, axes, back)
    edges = call(edges_kernel, edge_shapes, (VMEM,) * 2, (high, low), cost=0.4, name="edges")
    inner, outer, beyond = around(*edges)
    lon_scratch = (in_vmem(*full_shape), in_vmem(*full_shape[1:]))
    side = in_vmem(halo_rows, width)
    padded, rate = call(
        first_kernel,
        [in_vmem(*pad_shape), in_vmem(*full_shape)],
        (VMEM,) * 6,
        (high, low, outer_rows, matrix, geo, kap),
        scratch=lon_scratch,
        cost=2.0,
        name="first",
    )

    def first_halo(rate, at):
        return call(
            functools.partial(first_halo_kernel, at),
            [in_vmem(*full_shape), side],
            (VMEM,) * 7,
            (rate, padded, beyond, inner, outer, geo, kap),
            aliases={0: 0},
            cost=0.6,
            name="first_halo",
        )

    rate, high = first_halo(rate, levels - REACH)
    below2 = lax.ppermute(high, axes, onward)
    rate, low = first_halo(rate, 0)
    above2 = lax.ppermute(low, axes, back)
    section_shapes = [in_vmem(*full_shape), in_vmem(*pad_shape)]
    full, ahead = call(
        section_low_kernel,
        section_shapes,
        (VMEM,) * 4,
        (padded, rate, below, kap),
        cost=0.4,
        name="section_low",
    )
    full, ahead, *edges = call(
        section_high_kernel,
        [*section_shapes, *edge_shapes],
        (VMEM,) * 6,
        (padded, rate, above, kap, full, ahead),
        aliases={4: 0, 5: 1},
        cost=0.5,
        name="section_high",
    )
    inner, outer, beyond = around(*edges)
    both, low, high = call(
        second_kernel,
        [in_vmem(*full_shape), side, side],
        (VMEM,) * 8,
        (ahead, matrix, geo, kap, full, padded, below, above),
        scratch=lon_scratch,
        cost=2.5,
        name="second",
    )
    both = call(
        second_halo_kernel,
        in_vmem(*full_shape),
        (VMEM,) * 7,
        (both, ahead, beyond, inner, outer, geo, kap),
        aliases={0: 0},
        name="second_halo",
    )
    last_scratch = (in_vmem(*full_shape), pltpu.SemaphoreType.DMA((2, rows // TILE)))
    out = call(
        end_kernel,
        pltpu.HBM(full_shape, jnp.float32),
        (VMEM,) * 3,
        (ahead, both, kap),
        scratch=last_scratch,
        cost=0.5,
        name="end",
    )
    return call(
        last_kernel,
        pltpu.HBM(full_shape, jnp.float32),
        (VMEM,) * 7 + (HBM,),
        (ahead, both, below2, above2, low, high, kap, out),
        scratch=last_scratch,
        aliases={7: 0},
        name="last",
    )


def solution(mesh):
    placed = (P(None, "rad", None, "lon"), P(None, "rad", None, "lon"), P("rad"))
    return jax.shard_map(
        on_device,
        mesh=mesh,
        in_specs=placed,
        out_specs=P(None, "rad", None, "lon"),
        check_vma=False,
    )
```

```python
import functools
import math

import jax
import jax.numpy as jnp
import numpy as np
from jax import lax
from jax.experimental import pallas as pl
from jax.experimental.pallas import tpu as pltpu
from jax.sharding import PartitionSpec as P

first_coeffs = (0.8, -0.2, 4.0 / 105.0, -1.0 / 280.0)
second_coeffs = (-205.0 / 72.0, 1.6, -0.2, 8.0 / 315.0, -1.0 / 560.0)
time_step = 0.002
gamma_less_one = 0.4
radial_ratio = 3.0
FIELDS = 5
REACH = 4
TILE = 8
LANES = 128
GROUPS = LANES // (2 * REACH)
signs = (1.0, -1.0, -1.0, 1.0, 1.0)
first_whole = (672.0, -168.0, 32.0, -3.0)
second_whole = (8064.0, -1008.0, 128.0, -9.0)

level_first = tuple(radial_ratio * c for c in first_coeffs)
level_second = tuple(radial_ratio * radial_ratio * c for c in second_coeffs)

VMEM = pl.BlockSpec(memory_space=pltpu.VMEM)
HBM = pl.BlockSpec(memory_space=pltpu.HBM)


def in_vmem(*shape):
    return pltpu.VMEM(shape, jnp.float32)


def stencil_matrix(width):
    matrix = np.zeros((width, 2 * width), np.float32)
    for out in range(width):
        for k in range(1, REACH + 1):
            for sign in (1, -1):
                if 0 <= out + sign * k < width:
                    matrix[out + sign * k, out] = sign * first_whole[k - 1]
                    matrix[out + sign * k, width + out] = second_whole[k - 1]
    return jnp.asarray(matrix)


def geometry(rows, nlon, width):
    theta = (np.arange(rows) + 0.5) * (2.0 * math.pi / nlon)
    metric = 1.0 / np.sin(theta)
    table = np.stack([metric / 840.0, metric * metric / 5040.0, np.cos(theta) * metric])
    return jnp.asarray(np.broadcast_to(table[:, :, None], (3, rows, width)), jnp.float32)


def packed(tiles, lane):
    total = None
    for g, tile in enumerate(tiles):
        moved = pltpu.roll(tile, (REACH + 2 * REACH * g) % LANES, 1)
        if total is None:
            total = moved
        else:
            total = jnp.where(lane >= 2 * REACH * g, moved, total)
    return total


def across_level(center_wind, center_temper, halo, kappa, above):
    out = [[None] * REACH for _ in range(FIELDS)]
    for a in range(REACH):
        slopes = []
        for f in range(FIELDS):
            total = None
            for b in range(REACH):
                k = b + REACH - a if above else a + REACH - b
                if 1 <= k <= REACH:
                    c = level_first[k - 1] if above else -level_first[k - 1]
                    term = c * halo[f][b]
                    total = term if total is None else total + term
            slopes.append(total)
        curve = None
        for b in range(REACH):
            k = b + REACH - a if above else a + REACH - b
            if 1 <= k <= REACH:
                term = level_second[k] * halo[4][b]
                curve = term if curve is None else curve + term
        wind, temper = center_wind[a], center_temper[a]
        out[0][a] = -wind * slopes[0] - slopes[3]
        out[1][a] = -wind * slopes[1]
        out[2][a] = -wind * slopes[2]
        out[3][a] = -wind * slopes[3] - temper * slopes[0] - slopes[4]
        out[4][a] = -wind * slopes[4] - (gamma_less_one * temper) * slopes[3] + kappa[a] * curve
    return out


def high_kernel(
    levels, rows, state, kappa, high, kap, raw_kap, kappa_scalars, sems
):
    block = REACH * rows
    odd, _ = mirrored()
    start = jnp.where(odd == 1, 0, REACH)
    half, reads = block // 2, [(kappa, kappa_scalars)]
    for f in range(FIELDS):
        for part in range(2):
            at = pl.multiple_of((f * levels + start) * rows + part * half, TILE)
            reads.append((state.at[pl.ds(at, half)], high.at[pl.ds(f * block + part * half, half)]))
    copies = [pltpu.make_async_copy(*read, sems.at[i]) for i, read in enumerate(reads)]
    for copy in copies:
        copy.start()
    copies[0].wait()
    for i in range(REACH):
        row = pl.ds(FIELDS * block + i, 1)
        high[row, :] = jnp.full((1, LANES), kappa_scalars[start + i], jnp.float32)
        raw_kap[pl.ds(i, 1), :] = jnp.full((1, LANES), kappa_scalars[REACH - start + i], jnp.float32)
    for l in range(levels):
        value = kappa_scalars[jnp.where(odd == 1, levels - 1 - l, l)]
        kap[l] = jnp.full((TILE, LANES), value, jnp.float32)
    for copy in copies[1:]:
        copy.wait()


def low_kernel(levels, rows, state, raw_kap, low):
    block = REACH * rows
    odd, _ = mirrored()
    start = jnp.where(odd == 1, REACH, 0)
    for f in range(FIELDS):
        at = pl.multiple_of((f * levels + start) * rows, TILE)
        low[pl.ds(f * block, block), :] = state[pl.ds(at, block), :]
    low[pl.ds(FIELDS * block, REACH), :] = raw_kap[pl.ds(0, REACH), :]


def own_level(high, low, rows, f, l, odd):
    i = l % REACH
    at = (f * REACH + jnp.where(odd == 1, REACH - 1 - i, i)) * rows
    return (low if l < REACH else high), pl.multiple_of(at, TILE)


def edges_kernel(levels, rows, high, low, inner, outer, polar):
    odd, mirror = mirrored()
    packs = []
    for f in range(FIELDS):
        tiles = []
        for l in range(levels):
            side, at = own_level(high, low, rows, f, l, odd)
            tiles.append([side[pl.ds(at + t * TILE, TILE), :] for t in range(rows // TILE)])
            cap = side[pl.ds(at, REACH), :]
            polar[pl.ds((f * levels + l) * REACH, REACH), :] = mirror * cap if f == 3 else cap
        packs += [mirror * pack if f == 3 else pack for pack in packed(levels, rows, tiles)]
    store_packs(packs, inner, outer)


def mirrored():
    odd = lax.axis_index("lon") % 2
    return odd, jnp.where(odd == 1, -1.0, 1.0).astype(jnp.float32)


def bordered(at):
    last = lax.axis_size("rad") - 1
    here = lax.axis_index("rad")
    odd, _ = mirrored()
    from_first = jnp.where(odd == 1, last - here, here)
    return from_first > 0 if at == 0 else from_first < last


def share_of(at, factor):
    return jnp.where(bordered(at), factor, 0.0).astype(jnp.float32)


def lanes():
    return lax.broadcasted_iota(jnp.int32, (TILE, LANES), 1)


def packed(levels, rows, tiles):
    per = GROUPS // levels
    out = []
    for j in range(rows // TILE // per):
        total = None
        for g in range(GROUPS):
            moved = pltpu.roll(tiles[g % levels][j * per + g // levels], (REACH + 2 * REACH * g) % LANES, 1)
            total = moved if total is None else jnp.where(lanes() >= 2 * REACH * g, moved, total)
        out.append(total)
    return out


def store_packs(packs, inner, outer):
    first_half = lanes() % (2 * REACH) < REACH
    odd = lax.axis_index("lon") % 2 == 1
    for i in range(0, len(packs), 2):
        a, b = packs[i], packs[min(i + 1, len(packs) - 1)]
        at = pl.ds(i // 2 * TILE, TILE)
        east = jnp.where(first_half, a, pltpu.roll(b, REACH, 1))
        west = jnp.where(first_half, pltpu.roll(a, LANES - REACH, 1), b)
        inner[at, :] = jnp.where(odd, west, east)
        outer[at, :] = jnp.where(odd, east, west)


def load_packs(count, inner, outer):
    first_half = lanes() % (2 * REACH) < REACH
    odd = lax.axis_index("lon") % 2 == 1
    out = []
    for i in range(0, count, 2):
        at = pl.ds(i // 2 * TILE, TILE)
        before = jnp.where(odd, inner[at, :], outer[at, :])
        after = jnp.where(odd, outer[at, :], inner[at, :])
        out.append(jnp.where(first_half, before, pltpu.roll(after, REACH, 1)))
        out.append(jnp.where(first_half, pltpu.roll(before, LANES - REACH, 1), after))
    return out[:count]


def pieces_of(x):
    out = []
    for piece in range(3):
        out.append(x.astype(jnp.bfloat16))
        if piece < 2:
            x = x - out[-1].astype(jnp.float32)
    return out


def times_whole(pieces, m):
    total = None
    for piece in pieces:
        term = jnp.dot(piece, m, preferred_element_type=jnp.float32)
        total = term if total is None else total + term
    return total


def longitude_slopes(levels, rows, padded, matrix, dlon, elon):
    for f in range(FIELDS):
        x = padded[f, :, pl.ds(TILE, rows), :].reshape(levels * rows, LANES)
        whole = matrix[:, pl.ds(0, 2 * LANES if f == 4 else LANES)].astype(jnp.bfloat16)
        total = times_whole(pieces_of(x), whole)
        dlon[f] = total[:, :LANES].reshape(levels, rows, LANES)
        if f == 4:
            elon[...] = total[:, LANES:].reshape(levels, rows, LANES)


def groups_slope(pack, coeffs, sign):
    place = lanes() % (2 * REACH)
    total = None
    for k in range(1, REACH + 1):
        ahead = pltpu.roll(pack, LANES - k, 1)
        behind = pltpu.roll(pack, k, 1)
        from_after = (place < REACH) & (place >= REACH - k)
        from_before = (place >= REACH) & (place < REACH + k)
        term = jnp.where(from_after, coeffs[k - 1] * ahead, 0.0)
        term = jnp.where(from_before, (sign * coeffs[k - 1]) * behind, term)
        total = term if total is None else total + term
    return total


def add_halo(levels, rows, padded, polar, inner, outer, geo, kap, store):
    per = GROUPS // levels
    count = rows // TILE // per
    packs = load_packs(FIELDS * count, inner, outer)
    slopes = [groups_slope(pack, first_whole, -1.0) for pack in packs]
    bends = [groups_slope(pack, second_whole, 1.0) for pack in packs[4 * count :]]
    lane = lanes()
    at_side = (lane < REACH) | (lane >= LANES - REACH)
    row = lax.broadcasted_iota(jnp.int32, (TILE, LANES), 0)

    def by_row(coeffs, m):
        total = jnp.zeros((TILE, LANES), jnp.float32)
        for k in range(m + 1, REACH + 1):
            total = jnp.where(row == k - m - 1, coeffs[k - 1], total)
        return total

    first_rows = [by_row([-c for c in first_coeffs], m) for m in range(REACH)]
    second_rows = [by_row(second_coeffs[1:], m) for m in range(REACH)]
    for t in range(rows // TILE):
        j, u = divmod(t, per)
        here = pl.ds(t * TILE, TILE)
        metric = jnp.where(at_side, geo[0, here, :], 0.0)
        metric2 = jnp.where(at_side, geo[1, here, :], 0.0)
        for l in range(levels):
            shift = (LANES - REACH - 2 * REACH * (u * levels + levels - 1 - l)) % LANES
            center = [padded[f, l, pl.ds((t + 1) * TILE, TILE), :] for f in range(FIELDS)]
            wlon, wrow, temper = center[1], center[2], center[4]
            slon = [metric * pltpu.roll(slopes[f * count + j], shift, 1) for f in range(FIELDS)]
            slon[3] = -slon[3]
            laplace = metric2 * pltpu.roll(bends[j], shift, 1)
            extra = [-wlon * slope for slope in slon]
            extra[1] = extra[1] - temper * slon[0] - slon[4]
            spread = slon[1]
            if t == 0:
                srow = []
                for f in range(FIELDS):
                    total = None
                    for m in range(REACH):
                        across = signs[f] * polar[pl.ds((f * levels + l) * REACH + m, 1), :]
                        term = first_rows[m] * across
                        total = term if total is None else total + term
                        if f == 4:
                            laplace = laplace + second_rows[m] * across
                    srow.append(total)
                extra = [e - wrow * slope for e, slope in zip(extra, srow)]
                extra[2] = extra[2] - temper * srow[0] - srow[4]
                spread = spread + srow[2]
            extra[0] = extra[0] - spread
            extra[4] = extra[4] - (gamma_less_one * temper) * spread + kap[l] * laplace
            for f in range(FIELDS):
                store(f, l, t * TILE, center[f], extra[f])


def interior(levels, rows, padded, dlon, elon, geo, kappa, store):
    def body(t, carry):
        r0 = pl.multiple_of(t * TILE, TILE)
        here = pl.ds(r0, TILE)
        metric = geo[0, here, :]
        metric2 = geo[1, here, :]
        curvature = geo[2, here, :]
        center = [[padded[f, l, pl.ds(r0 + TILE, TILE), :] for l in range(levels)] for f in range(FIELDS)]
        out = [[None] * levels for _ in range(FIELDS)]
        for l in range(levels):
            wlon, wrow, wlev, temper = (center[f][l] for f in (1, 2, 3, 4))
            slon, srow, slev = [], [], []
            for f in range(FIELDS):
                slon.append(metric * dlon[f, l, here, :])
                total = None
                for k in range(1, REACH + 1):
                    ahead = padded[f, l, pl.ds(r0 + TILE + k, TILE), :]
                    behind = padded[f, l, pl.ds(r0 + TILE - k, TILE), :]
                    term = first_coeffs[k - 1] * (ahead - behind)
                    total = term if total is None else total + term
                    if f == 4:
                        curve = second_coeffs[k] * (ahead + behind)
                        bend = curve if k == 1 else bend + curve
                srow.append(total)
                total = None
                for k in range(1, REACH + 1):
                    up = center[f][l + k] if l + k < levels else None
                    down = center[f][l - k] if l - k >= 0 else None
                    if up is not None and down is not None:
                        term = level_first[k - 1] * (up - down)
                    elif up is not None:
                        term = level_first[k - 1] * up
                    elif down is not None:
                        term = -level_first[k - 1] * down
                    else:
                        continue
                    total = term if total is None else total + term
                slev.append(total)
            lift = None
            for k in range(1, REACH + 1):
                near = [center[4][l + s * k] for s in (1, -1) if 0 <= l + s * k < levels]
                if near:
                    term = level_second[k] * (near[0] + near[1] if len(near) == 2 else near[0])
                    lift = term if lift is None else lift + term
            middle = second_coeffs[0]
            laplace = metric2 * (elon[l, here, :] + (5040.0 * middle) * temper) + bend
            laplace = laplace + (middle + level_second[0]) * temper + lift
            carried = [wlon * slon[f] + wrow * srow[f] + wlev * slev[f] for f in range(FIELDS)]
            spread = slon[1] + srow[2] + slev[3] + curvature * wrow
            out[0][l] = -carried[0] - spread
            out[1][l] = -carried[1] - temper * slon[0] - slon[4]
            out[2][l] = -carried[2] - temper * srow[0] - srow[4]
            out[3][l] = -carried[3] - temper * slev[0] - slev[4]
            out[4][l] = -carried[4] - (gamma_less_one * temper) * spread + kappa[l] * laplace
            for f in range(FIELDS):
                store(f, l, r0, out[f][l])
        return carry

    lax.fori_loop(0, rows // TILE, body, 0)


def first_kernel(levels, rows, high, low, beyond, matrix, geo, kap, padded, rate, dlon, elon):
    odd, mirror = mirrored()
    for f in range(FIELDS):
        for l in range(levels):
            side, at = own_level(high, low, rows, f, l, odd)
            whole = side[pl.ds(at, rows), :]
            after = beyond[f, jnp.where(odd == 1, levels - 1 - l, l)]
            if f == 3:
                whole, after = mirror * whole, mirror * after
            padded[f, l, pl.ds(0, TILE), :] = jnp.zeros((TILE, LANES), jnp.float32)
            padded[f, l, pl.ds(TILE, rows), :] = whole
            padded[f, l, pl.ds(TILE + rows, REACH), :] = after
    longitude_slopes(levels, rows, padded, matrix, dlon, elon)

    def store(f, l, r0, tendency):
        rate[f, l, pl.ds(r0, TILE), :] = tendency

    interior(levels, rows, padded, dlon, elon, geo, kap, store)


def first_halo_kernel(levels, rows, given, padded, polar, inner, outer, geo, kap, rate, low, high):
    def store(f, l, r0, value, extra):
        tendency = given[f, l, pl.ds(r0, TILE), :] + extra
        rate[f, l, pl.ds(r0, TILE), :] = tendency
        side = low if l < REACH else high
        side[pl.ds((f * REACH + l % REACH) * rows + r0, TILE), :] = value + time_step * tendency

    add_halo(levels, rows, padded, polar, inner, outer, geo, kap, store)


def raw_tile(ref, rows, r0, odd, mirror):
    out = []
    for f in range(FIELDS):
        ats = [(f * REACH + jnp.where(odd == 1, REACH - 1 - b, b)) * rows + r0 for b in range(REACH)]
        out.append([ref[pl.ds(pl.multiple_of(at, TILE), TILE), :] for at in ats])
    out[3] = [mirror * v for v in out[3]]
    return out


def own_tile(ref, rows, r0):
    return [
        [ref[pl.ds((f * REACH + b) * rows + r0, TILE), :] for b in range(REACH)] for f in range(FIELDS)
    ]


def section_side(at, up, rows, padded, rate, sent, kappa, store):
    odd, mirror = mirrored()
    there = share_of(at, 1.0)

    def body(t, carry):
        r0 = pl.multiple_of(t * TILE, TILE)
        here, inside = pl.ds(r0, TILE), pl.ds(r0 + TILE, TILE)
        halo = raw_tile(sent, rows, r0, odd, mirror)
        center = [[padded[f, at + a, inside, :] for a in range(REACH)] for f in range(FIELDS)]
        extra = across_level(center[3], center[4], halo, [kappa[at + a] for a in range(REACH)], up)
        for f in range(FIELDS):
            for a in range(REACH):
                total = rate[f, at + a, here, :] + there * extra[f][a]
                store(f, a, r0, total, center[f][a] + time_step * total)
        return carry

    lax.fori_loop(0, rows // TILE, body, 0)


def section_low_kernel(levels, rows, padded, rate, below, kappa, full_low, ahead_low):
    def store(f, a, r0, total, ahead):
        full_low[f, a, pl.ds(r0, TILE), :] = total
        ahead_low[f, a, pl.ds(r0, TILE), :] = ahead

    section_side(0, False, rows, padded, rate, below, kappa, store)


def section_high_kernel(
    levels, rows, padded, rate, above, kappa, full_low, ahead_low, full, ahead, inner, outer, polar
):
    at = levels - REACH

    def store(f, a, r0, total, value):
        full[f, at + a, pl.ds(r0, TILE), :] = total
        ahead[f, at + a, pl.ds(r0 + TILE, TILE), :] = value

    section_side(at, True, rows, padded, rate, above, kappa, store)
    packs = []
    for f in range(FIELDS):
        for l in range(levels):
            if l < REACH:
                full[f, l] = full_low[f, l]
                ahead[f, l, pl.ds(TILE, rows), :] = ahead_low[f, l]
            ahead[f, l, pl.ds(0, TILE), :] = jnp.zeros((TILE, LANES), jnp.float32)
            ahead[f, l, pl.ds(rows + TILE, REACH), :] = padded[f, l, pl.ds(rows + TILE, REACH), :]
            polar[pl.ds((f * levels + l) * REACH, REACH), :] = ahead[f, l, pl.ds(TILE, REACH), :]
        tiles = [[ahead[f, l, pl.ds((t + 1) * TILE, TILE), :] for t in range(rows // TILE)] for l in range(levels)]
        packs += packed(levels, rows, tiles)
    store_packs(packs, inner, outer)


def second_kernel(
    levels, rows, padded, matrix, geo, kap, full, start, below, above, both, low, high, dlon, elon
):
    longitude_slopes(levels, rows, padded, matrix, dlon, elon)

    def store(f, l, r0, tendency):
        at = pl.ds(r0, TILE)
        both[f, l, at, :] = (0.5 * time_step) * (full[f, l, at, :] + tendency)

    interior(levels, rows, padded, dlon, elon, geo, kap, store)
    tail = FIELDS * REACH * rows
    odd, mirror = mirrored()

    def body(t, carry):
        r0 = pl.multiple_of(t * TILE, TILE)
        for halo_ref, out, at, up in ((below, low, 0, True), (above, high, levels - REACH, False)):
            beyond = raw_tile(halo_ref, rows, r0, odd, mirror)
            mine = [
                [start[f, at + a, pl.ds(r0 + TILE, TILE), :] for a in range(REACH)] for f in range(FIELDS)
            ]
            kappas = [
                halo_ref[pl.ds(tail + jnp.where(odd == 1, REACH - 1 - a, a), 1), :] for a in range(REACH)
            ]
            there = share_of(at, time_step)
            extra = across_level(beyond[3], beyond[4], mine, kappas, up)
            for f in range(FIELDS):
                for a in range(REACH):
                    out[pl.ds((f * REACH + a) * rows + r0, TILE), :] = there * extra[f][a]
        return carry

    lax.fori_loop(0, rows // TILE, body, 0)


def second_halo_kernel(
    levels, rows, given, padded, polar, inner, outer, geo, kap, both
):
    def store(f, l, r0, value, extra):
        at = pl.ds(r0, TILE)
        both[f, l, at, :] = given[f, l, at, :] + (0.5 * time_step) * extra

    add_halo(levels, rows, padded, polar, inner, outer, geo, kap, store)


def side_copy(at, t, levels, odd, out, staged, sems):
    real, here = jnp.where(odd == 1, levels - at - REACH, at), pl.ds(t * TILE, TILE)
    there = (slice(None), pl.ds(real, REACH), here)
    return pltpu.make_async_copy(staged.at[there], out.at[there], sems.at[at // REACH, t])


def write_tile(at, t, share, levels, padded, both, kap, staged):
    odd, mirror = mirrored()
    here, inside = pl.ds(t * TILE, TILE), pl.ds((t + 1) * TILE, TILE)
    extra = None
    if share is not None:
        wind = [padded[3, at + a, inside, :] for a in range(REACH)]
        temper = [padded[4, at + a, inside, :] for a in range(REACH)]
        extra = share(t * TILE, wind, temper, [kap[at + a] for a in range(REACH)])
    for f in range(FIELDS):
        for a in range(REACH):
            new = both[f, at + a, here, :]
            if extra is not None:
                new = new + (0.5 * time_step) * extra[f][a]
            real = jnp.where(odd == 1, levels - 1 - at - a, at + a)
            staged[f, real, here, :] = mirror * new if f == 3 else new


def end_kernel(levels, rows, padded, both, kap, out, staged, sems):
    odd, _ = mirrored()
    for at in (0, levels - REACH):

        @pl.when(jnp.logical_not(bordered(at)))
        def _():
            copies = [side_copy(at, t, levels, odd, out, staged, sems) for t in range(rows // TILE)]
            for t, copy in enumerate(copies):
                write_tile(at, t, None, levels, padded, both, kap, staged)
                copy.start()
            for copy in copies:
                copy.wait()


def last_kernel(
    levels, rows, padded, both, above, below, more_low, more_high, kap, given, out, staged, sems
):
    odd, _ = mirrored()

    def share_by(sent, more, up):
        def share(r0, wind, temper, kappa):
            halo, there = own_tile(sent, rows, r0), own_tile(more, rows, r0)
            halo = [[halo[f][b] + there[f][b] for b in range(REACH)] for f in range(FIELDS)]
            return across_level(wind, temper, halo, kappa, up)

        return share

    sides = (
        (0, share_by(below, more_low, False)),
        (levels - REACH, share_by(above, more_high, True)),
    )
    for at, share in sides:

        @pl.when(bordered(at))
        def _():
            for t in range(rows // TILE):
                write_tile(at, t, share, levels, padded, both, kap, staged)
                side_copy(at, t, levels, odd, out, staged, sems).start()

    for at, _ in sides:

        @pl.when(bordered(at))
        def _():
            for t in range(rows // TILE):
                side_copy(at, t, levels, odd, out, staged, sems).wait()


def on_device(state, outer_rows, kappa):
    levels, rows, width = state.shape[1:]
    ring, depth = lax.axis_size("lon"), lax.axis_size("rad")
    assert ring % 4 == 0 and width == LANES and levels == 2 * REACH and GROUPS % levels == 0
    assert rows % (TILE * (GROUPS // levels)) == 0
    matrix = stencil_matrix(width)
    geo = geometry(rows, width * ring, width)
    halo_rows = FIELDS * REACH * rows
    packs = -(-(FIELDS * levels * rows // TILE // GROUPS) // 2) * TILE
    pad_shape = (FIELDS, levels, rows + 2 * TILE, width)
    full_shape = (FIELDS, levels, rows, width)

    def call(kernel, out_shape, in_specs, args, scratch=(), aliases=None, cost=1.0, name=None):
        spaces = {id(VMEM): pltpu.VMEM, id(HBM): pltpu.HBM}
        args = [pltpu.with_memory_space_constraint(x, spaces[id(s)]) for s, x in zip(in_specs, args)]
        return pl.pallas_call(
            functools.partial(kernel, levels, rows),
            out_shape=out_shape,
            in_specs=list(in_specs),
            out_specs=jax.tree.map(lambda o: HBM if o.memory_space is pltpu.HBM else VMEM, out_shape),
            scratch_shapes=list(scratch),
            input_output_aliases=aliases or {},
            cost_estimate=pl.CostEstimate(flops=0, bytes_accessed=int(cost * 3.69e6), transcendentals=0),
            compiler_params=pltpu.CompilerParams(vmem_limit_bytes=16 * 2**20),
            name=name,
        )(*args)

    pairs = [(i, i + 1) for i in range(0, ring, 2)]
    swap_inner = pairs + [(b, a) for a, b in pairs]
    pairs = [(i, (i + 1) % ring) for i in range(1, ring, 2)]
    swap_outer = pairs + [(b, a) for a, b in pairs]
    half = [(i, (i + ring // 2) % ring) for i in range(ring)]
    onward = []
    for lon in range(0, ring, 2):
        even, odd = lon * depth, (lon + 1) * depth
        onward += [(even + i, even + i + 1) for i in range(depth - 1)] + [(even + depth - 1, odd + depth - 1)]
        onward += [(odd + i + 1, odd + i) for i in range(depth - 1)] + [(odd, even)]
    back = [(b, a) for a, b in onward]
    axes = ("lon", "rad")

    def around(inner, outer, polar):
        inner = lax.ppermute(inner, "lon", swap_inner)
        outer = lax.ppermute(outer, "lon", swap_outer)
        return inner, outer, lax.ppermute(polar, "lon", half)

    edge_shapes = [in_vmem(packs, width), in_vmem(packs, width), in_vmem(FIELDS * levels * REACH, width)]
    payload = in_vmem(halo_rows + TILE, width)
    flat = state.reshape(-1, width)
    high, kap, raw_kap = call(
        high_kernel,
        [payload, in_vmem(levels, TILE, width), in_vmem(TILE, width)],
        (HBM,) * 2,
        (flat, kappa),
        scratch=(pltpu.SMEM(kappa.shape, jnp.float32), pltpu.SemaphoreType.DMA((2 * FIELDS + 1,))),
        name="high",
    )
    below = lax.ppermute(high, axes, onward)
    low = call(low_kernel, payload, (VMEM,) * 2, (flat, raw_kap), cost=0.2, name="low")
    above = lax.ppermute(low, axes, back)
    edges = call(edges_kernel, edge_shapes, (VMEM,) * 2, (high, low), cost=0.4, name="edges")
    inner, outer, beyond = around(*edges)
    lon_scratch = (in_vmem(*full_shape), in_vmem(*full_shape[1:]))
    side = in_vmem(halo_rows, width)
    padded, rate = call(
        first_kernel,
        [in_vmem(*pad_shape), in_vmem(*full_shape)],
        (VMEM,) * 6,
        (high, low, outer_rows, matrix, geo, kap),
        scratch=lon_scratch,
        cost=2.0,
        name="first",
    )

    rate, low, high = call(
        first_halo_kernel,
        [in_vmem(*full_shape), side, side],
        (VMEM,) * 7,
        (rate, padded, beyond, inner, outer, geo, kap),
        aliases={0: 0},
        cost=1.2,
        name="first_halo",
    )
    below2 = lax.ppermute(high, axes, onward)
    above2 = lax.ppermute(low, axes, back)
    four = in_vmem(FIELDS, REACH, rows, width)
    full_low, ahead_low = call(
        section_low_kernel,
        [four, four],
        (VMEM,) * 4,
        (padded, rate, below, kap),
        cost=0.4,
        name="section_low",
    )
    full, ahead, *edges = call(
        section_high_kernel,
        [in_vmem(*full_shape), in_vmem(*pad_shape), *edge_shapes],
        (VMEM,) * 6,
        (padded, rate, above, kap, full_low, ahead_low),
        cost=0.5,
        name="section_high",
    )
    inner, outer, beyond = around(*edges)
    both, low, high = call(
        second_kernel,
        [in_vmem(*full_shape), side, side],
        (VMEM,) * 8,
        (ahead, matrix, geo, kap, full, padded, below, above),
        scratch=lon_scratch,
        cost=2.5,
        name="second",
    )
    both = call(
        second_halo_kernel,
        in_vmem(*full_shape),
        (VMEM,) * 7,
        (both, ahead, beyond, inner, outer, geo, kap),
        name="second_halo",
    )
    last_scratch = (in_vmem(*full_shape), pltpu.SemaphoreType.DMA((2, rows // TILE)))
    out = call(
        end_kernel,
        pltpu.HBM(full_shape, jnp.float32),
        (VMEM,) * 3,
        (ahead, both, kap),
        scratch=last_scratch,
        cost=0.5,
        name="end",
    )
    return call(
        last_kernel,
        pltpu.HBM(full_shape, jnp.float32),
        (VMEM,) * 7 + (HBM,),
        (ahead, both, above2, below2, low, high, kap, out),
        scratch=last_scratch,
        aliases={7: 0},
        name="last",
    )


def solution(mesh):
    placed = (P(None, "rad", None, "lon"), P(None, "rad", None, "lon"), P("rad"))
    return jax.shard_map(
        on_device,
        mesh=mesh,
        in_specs=placed,
        out_specs=P(None, "rad", None, "lon"),
        check_vma=False,
    )
```
